32 devices in a mesh: tok: 8 (over z, y), head: 4 (over x, core).
Axes of the slice: x: 2, y: 2, z: 4, core: 2. Of those that a mesh axis runs over, the one named last changes fastest.
Arguments:
- hidden_in: bfloat16 [16384, 768], P('tok'), may hold values from -6 to 6
- norm_gain: float32 [768], replicated, may hold values from 0.1 to 1.9
- w_zx: bfloat16 [768, 2, 1536], P(None, None, 'head'), may hold values from -0.21875 to 0.21875
- w_bc: bfloat16 [768, 256], replicated, may hold values from -0.21875 to 0.21875
- w_dt: bfloat16 [768, 24], replicated, may hold values from -0.21875 to 0.21875
- dt_bias: float32 [24], replicated, may hold values from -6 to -4
- a_log: float32 [24], replicated, may hold values from -5.5 to 1.6
- conv_x: float32 [5, 1536], P(None, 'head'), may hold values from -3 to 3
- conv_bc: float32 [5, 256], replicated, may hold values from -3 to 3
- d_skip: float32 [24], replicated, may hold values from 0.5 to 1.5
- gate_gain: float32 [1536], P('head'), may hold values from 0.1 to 1.9
- w_out: bfloat16 [1536, 768], P('head'), may hold values from -0.15625 to 0.15625
- out_grad: bfloat16 [16384, 768], P('tok'), may hold values from -6 to 6
- group_first: int32 [64], P('tok'), may hold values from 0 to 1, as said below
- group_valid: int32 [64], P('tok'), may hold values from 128 to 256, as said below
Outputs:
- block_out: bfloat16 [16384, 768], P('tok')
- grad_in: float32 [16384, 768], P('tok')
- grad_norm_gain: float32 [768], replicated
- grad_w_zx: float32 [768, 2, 1536], P(None, None, 'head')
- grad_w_bc: float32 [768, 256], replicated
- grad_w_dt: float32 [768, 24], replicated
- grad_dt_bias: float32 [24], replicated
- grad_a_log: float32 [24], replicated
- grad_conv_x: float32 [5, 1536], P(None, 'head')
- grad_conv_bc: float32 [5, 256], replicated
- grad_d_skip: float32 [24], replicated
- grad_gate_gain: float32 [1536], P('head')
- grad_w_out: float32 [1536, 768], P('head')
The draws below stay inside these ranges and needn't reach their ends.
Inputs may be any that keep to these rules, and one draw needn't show every extreme that they name: `group_first`: the first group begins a sequence; sequences occupy whole groups. `group_valid`: below 256 only in the last group of a sequence.
All inputs are finite; a program needn't handle non-finite values.
Results may differ from the reference program's by a relative error of at most 0.0029.
The reference program's roundings to bfloat16 on the way count: a program that leaves them out, or rounds other values in their place, can miss the bound.
Values may be sent and summed in bfloat16 or wider, within the bound.
No kernel may reach another device: no remote copies, remote signals or barrier semaphores. Data moves between devices by JAX's collectives and lax.ppermute only.
A program may use at most 192 MiB of HBM per device.

```python
import jax
import jax.numpy as jnp
from jax import lax

D = 768
H = 24
P_SIZE = 64
N = 128
KCONV = 4
GROUP = 256
TOK_DEV = 2048
DI = 1536
TOKENS = 16384


def group_layout(key):
    per_device = TOK_DEV // GROUP
    group_total = TOKENS // GROUP
    key_start, key_stop, key_coin, key_fill = jax.random.split(key, 4)
    long_start = jax.random.randint(key_start, (), 0, per_device)
    long_stop = jax.random.randint(key_stop, (), group_total - per_device, group_total)
    group_pos = jnp.arange(group_total)
    coin_flip = jax.random.randint(key_coin, (group_total,), 0, 2)
    inside = (group_pos > long_start) & (group_pos <= long_stop)
    forced = (group_pos == 0) | (group_pos == long_start) | (group_pos == long_stop + 1)
    starts = jnp.where(inside, 0, jnp.where(forced, 1, coin_flip)).astype(jnp.int32)
    next_start = jnp.concatenate([starts[1:], jnp.ones((1,), jnp.int32)])
    fill_count = jax.random.randint(key_fill, (group_total,), GROUP // 2, GROUP + 1)
    valid_count = jnp.where(next_start == 1, fill_count, GROUP)
    valid_count = jnp.where(group_pos == group_total - 1, GROUP // 2, valid_count)
    return (starts, valid_count.astype(jnp.int32))


def draw_group_first(key, part):
    layout = group_layout(key)
    return layout[0]


def draw_group_valid(key, part):
    layout = group_layout(key)
    return layout[1]


def draw_a_log(key, part):
    key = jax.random.fold_in(key, 7)
    return jax.random.uniform(key, (H,), jnp.float32, -5.5, 1.6)


def block_levels(own_key, dims, cuts, least, largest):
    loudness = 1.0
    for dim, shards_of in cuts:
        steps = jax.random.uniform(jax.random.fold_in(jax.random.fold_in(own_key, 6), dim), (shards_of,), jnp.float32, least / len(cuts), largest / len(cuts))
        loudness = loudness * jnp.repeat(jnp.exp(steps), dims[dim] // shards_of).reshape((-1,) + (1,) * (len(dims) - 1 - dim))
    return loudness


def noise(stream_key, extent, deviation, reach, pieces=(), held_as=jnp.bfloat16):
    factor_of = block_levels(stream_key, extent, pieces, -0.22, 0.18) if pieces else 1.0
    entries = jax.random.normal(stream_key, extent, jnp.float32) * deviation * factor_of
    return jnp.minimum(jnp.maximum(entries, -reach), reach).astype(held_as)


def setup_inputs(seed: int = 0) -> dict:
    splits = jax.random.split(jax.random.key(seed), 16)
    return {
        "hidden_in": noise(splits[0], (TOKENS, D), 1.0, 6.0, ((0, 8),)),
        "norm_gain": jnp.clip(1.0 + 0.18 * jax.random.normal(splits[1], (D,), jnp.float32), 0.1, 1.9),
        "w_zx": noise(splits[2], (D, 2, DI), D ** -0.5, 0.21875, ((2, 4),)),
        "w_bc": noise(splits[3], (D, 2 * N), D ** -0.5, 0.21875),
        "w_dt": noise(splits[4], (D, H), D ** -0.5, 0.21875),
        "dt_bias": jnp.clip(jax.random.uniform(splits[5], (H,), jnp.float32, -6.0, -4.0), -6.0, -4.0),
        "a_log": draw_a_log(jax.random.fold_in(splits[15], 71), 0),
        "conv_x": noise(splits[7], (KCONV + 1, DI), KCONV ** -0.5, 3.0, ((1, 4),), jnp.float32),
        "conv_bc": noise(splits[8], (KCONV + 1, 2 * N), KCONV ** -0.5, 3.0, (), jnp.float32),
        "d_skip": jnp.clip(jax.random.uniform(splits[9], (H,), jnp.float32, 0.5, 1.5), 0.5, 1.5),
        "gate_gain": jnp.clip(1.0 + 0.18 * jax.random.normal(splits[10], (DI,), jnp.float32), 0.1, 1.9),
        "w_out": noise(splits[11], (DI, D), DI ** -0.5, 0.15625, ((0, 4),)),
        "out_grad": noise(splits[12], (TOKENS, D), 1.0, 6.0, ((0, 8),)),
        "group_first": draw_group_first(jax.random.fold_in(splits[15], 71), 0),
        "group_valid": draw_group_valid(jax.random.fold_in(splits[15], 71), 0),
    }


NORM_EPS = 1e-05
PRECISE = lax.Precision.HIGHEST

@jax.custom_vjp
def low(v):
    return lax.optimization_barrier(v.astype(jnp.bfloat16)).astype(jnp.float32)

@jax.custom_vjp
def low_back(v):
    return v

def low_keep(v):
    return (low(v), None)

def low_pass(kept, grad):
    return (grad,)

def back_keep(v):
    return (v, None)

def back_low(kept, grad):
    return (low(grad),)
low.defvjp(low_keep, low_pass)
low_back.defvjp(back_keep, back_low)

def lag_keep(group_first, length):
    position = jnp.arange(length) % GROUP
    start_rows = jnp.repeat(group_first.astype(jnp.float32), GROUP, total_repeat_length=length)
    return [1.0 - (position < KCONV - 1 - tap_index).astype(jnp.float32) * start_rows for tap_index in range(KCONV)]

def conv_silu(extended, conv_taps, keep_list):
    row_count = extended.shape[0] - (KCONV - 1)
    running = conv_taps[KCONV] + jnp.zeros((row_count, conv_taps.shape[1]), jnp.float32)
    for tap_index in range(KCONV):
        running = running + conv_taps[tap_index] * extended[tap_index:tap_index + row_count] * keep_list[tap_index][:, None]
    return jax.nn.silu(running)

def group_inner(x_blocks, write_blocks, read_blocks, step_blocks, decay_blocks):
    length = decay_blocks.shape[1]
    cum_decay = jnp.cumsum(decay_blocks, axis=1)
    cum_heads = jnp.swapaxes(cum_decay, 1, 2)
    scores = jnp.einsum('kln,ksn->kls', read_blocks, write_blocks, precision=PRECISE)
    causal = jnp.tril(jnp.ones((length, length), bool))
    decay_gap = cum_heads[:, :, :, None] - cum_heads[:, :, None, :]
    weights = jnp.where(causal, jnp.exp(jnp.where(causal, decay_gap, 0.0)), 0.0) * scores[:, None]
    x_scaled = x_blocks * step_blocks[..., None]
    within = jnp.einsum('khls,kshp->klhp', weights, x_scaled, precision=PRECISE)
    to_end = jnp.exp(cum_decay[:, -1:, :] - cum_decay)
    group_states = jnp.einsum('kshp,ksn->khpn', x_scaled * to_end[..., None], write_blocks, precision=PRECISE)
    return (within, group_states, cum_decay)

def group_outer(read_blocks, cum_decay, entry_states):
    return jnp.einsum('kln,khpn->klhp', read_blocks, entry_states, precision=PRECISE) * jnp.exp(cum_decay)[..., None]

def scan_states(x_heads, write_map, read_map, step_size, log_decay, start_float):
    group_total = start_float.shape[0]

    def split_up(value):
        return value.reshape((group_total, 1, GROUP) + value.shape[1:])
    items = (split_up(x_heads), split_up(write_map), split_up(read_map), split_up(step_size), split_up(log_decay), start_float)

    def advance(state, item):
        x_block, write_block, read_block, step_block, decay_block, is_start = item
        within, group_states, cum_decay = group_inner(x_block, write_block, read_block, step_block, decay_block)
        entry = (1.0 - is_start) * state
        across = group_outer(read_block, cum_decay, entry[None])
        leaving = jnp.exp(cum_decay[0, -1])[:, None, None] * entry + group_states[0]
        return (leaving, (within + across)[0])
    initial = jnp.zeros((H, P_SIZE, N), jnp.float32)
    _, outputs = lax.scan(jax.checkpoint(advance), initial, items)
    return outputs.reshape(group_total * GROUP, H * P_SIZE)

def forward(hidden, norm_gain, w_zx, w_bc, w_dt, dt_bias, a_log, conv_x, conv_bc, d_skip, gate_gain, w_out, start_float, live_mask, keep_list):
    row_count = hidden.shape[0]
    inner_width = H * P_SIZE
    inv_rms = lax.rsqrt(lax.optimization_barrier(jnp.mean(hidden * hidden, axis=1, keepdims=True)) + NORM_EPS)
    normed_low = low(hidden * inv_rms * norm_gain)
    proj_zx = low_back(jnp.dot(normed_low, w_zx.reshape(D, 2 * inner_width), preferred_element_type=jnp.float32, precision=PRECISE)).reshape(row_count, 2, inner_width)
    state_raw = jnp.dot(normed_low, w_bc, preferred_element_type=jnp.float32, precision=PRECISE)
    step_raw = low_back(jnp.dot(normed_low, w_dt, preferred_element_type=jnp.float32, precision=PRECISE))
    mixed = jnp.concatenate([proj_zx[:, 1], state_raw], axis=1)
    padded = jnp.concatenate([jnp.zeros((KCONV - 1, mixed.shape[1]), jnp.float32), mixed], axis=0)
    activated = conv_silu(padded, jnp.concatenate([conv_x, conv_bc], axis=1), keep_list)
    x_low = low(activated[:, :inner_width])
    write_map = low(activated[:, inner_width:inner_width + N])
    read_map = low(activated[:, inner_width + N:])
    step_size = jax.nn.softplus(step_raw + dt_bias) * live_mask[:, None]
    log_decay = step_size * -jnp.exp(a_log)
    mixer_out = scan_states(x_low.reshape(row_count, H, P_SIZE), write_map, read_map, step_size, log_decay, start_float)
    mixer_total = low_back(mixer_out + x_low * jnp.repeat(d_skip, P_SIZE))
    gated_out = mixer_total * jax.nn.silu(proj_zx[:, 0])
    gate_inv = lax.rsqrt(lax.optimization_barrier(jnp.mean(gated_out * gated_out, axis=1, keepdims=True)) + NORM_EPS)
    normed_out = low(gated_out * gate_inv * gate_gain)
    return hidden + jnp.dot(normed_out, w_out, preferred_element_type=jnp.float32, precision=PRECISE)

def reference(hidden_in, norm_gain, w_zx, w_bc, w_dt, dt_bias, a_log, conv_x, conv_bc, d_skip, gate_gain, w_out, out_grad, group_first, group_valid):
    live_mask = (jnp.arange(GROUP)[None, :] < group_valid[:, None]).astype(jnp.float32).reshape(TOKENS)
    keep_list = lag_keep(group_first, TOKENS)
    start_float = group_first.astype(jnp.float32)
    float_args = (hidden_in.astype(jnp.float32), norm_gain, w_zx.astype(jnp.float32), w_bc.astype(jnp.float32), w_dt.astype(jnp.float32), dt_bias, a_log, conv_x, conv_bc, d_skip, gate_gain, w_out.astype(jnp.float32))

    def wrapped(*params):
        return forward(*params, start_float, live_mask, keep_list)
    block_value, pullback = jax.vjp(wrapped, *float_args)
    gradients = pullback(out_grad.astype(jnp.float32))
    return (block_value.astype(jnp.bfloat16), gradients[0], gradients[1], gradients[2], gradients[3], gradients[4], gradients[5], gradients[6], gradients[7], gradients[8], gradients[9], gradients[10], gradients[11])
```

```python
import functools

import jax
import jax.numpy as jnp
from jax import lax
from jax.experimental import pallas as pl
from jax.experimental.pallas import tpu as pltpu
from jax.sharding import PartitionSpec as P

P_SIZE = 64
N = 128
KCONV = 4
GROUP = 256
CHUNK = 128
LANES = 128
PARTS = GROUP // CHUNK
EPS = 1e-05
VMEM_LIMIT = 16 * 1024 * 1024
F32 = jnp.float32
BF16 = jnp.bfloat16


def mm(a, b, ca=1, cb=0):
    return lax.dot_general(a, b, (((ca,), (cb,)), ((), ())), preferred_element_type=F32)


def iota(shape, dim):
    return lax.broadcasted_iota(jnp.int32, shape, dim)


def spread(cols, width):
    rows = cols.shape[0]
    low = iota((rows, LANES), 1) < P_SIZE
    tiles = [
        jnp.where(low, cols[:, 2 * p : 2 * p + 1], cols[:, 2 * p + 1 : 2 * p + 2])
        for p in range(width // LANES)
    ]
    return jnp.concatenate(tiles, axis=1)


def gather_heads(width):
    return (iota((width, LANES), 0) // P_SIZE == iota((width, LANES), 1)).astype(BF16)


def fold_rows(value):
    rows, width = value.shape
    return value.reshape(rows // 8, 8, width).sum(axis=0)


def tri(kind):
    row, col = iota((CHUNK, CHUNK), 0), iota((CHUNK, CHUNK), 1)
    return {"le": col <= row, "ge": col >= row, "lt": col < row}[kind]


def pair_rows(tile):
    low = iota(tile.shape, 1) < P_SIZE
    zero = jnp.zeros_like(tile)
    return jnp.concatenate([jnp.where(low, tile, zero), jnp.where(low, zero, tile)], axis=0)


def split2(value):
    high = value.astype(BF16)
    return high, (value - high.astype(F32)).astype(BF16)


def split3(value):
    high, rest = split2(value)
    return high, rest, (value - high.astype(F32) - rest.astype(F32)).astype(BF16)


def mm_left(a, b, ca=1, cb=0):
    high, low = split2(a)
    return mm(high, b, ca, cb) + mm(low, b, ca, cb)


def mm_right(a, b, ca=1, cb=0):
    high, low = split2(b)
    return mm(a, high, ca, cb) + mm(a, low, ca, cb)


def mm_both(a, b, ca=1, cb=0):
    ah, al = split2(a)
    bh, bl = split2(b)
    return mm(ah, bh, ca, cb) + mm(al, bh, ca, cb) + mm(ah, bl, ca, cb)


def stacked(value):
    return jnp.concatenate(
        [value[:, c : c + LANES] for c in range(0, value.shape[1], LANES)], axis=0
    )


def tree(terms):
    while len(terms) > 1:
        terms = [terms[k] + terms[k + 1] for k in range(0, len(terms), 2)]
    return terms[0]


def rms_inv(u):
    return lax.rsqrt(jnp.mean(u * u, axis=1, keepdims=True) + EPS)


def k_project(hid, gain, w_x, w_bc, w_dt, hp, h_o, v_o, pre_o):
    width = w_x.shape[1]
    u = hid[...].astype(F32)
    h = (u * rms_inv(u) * gain[...]).astype(BF16)
    h_o[...] = h
    v_o[:, :width] = mm(h, w_x[...])
    v_o[:, width:] = mm(h, w_bc[...])
    pre_o[...] = mm(h, w_dt[...]) + hp[0:1, :]


def k_conv(
    first, valid, v, pre, rim, gain, w_x, w_bc, hp, cx, cb,
    cv_o, xs_o, bc_o, dt_o, cum_o, ent_o, pd_o, fin_o,
    vbuf, state, decay,
):
    g = pl.program_id(0)
    width = w_x.shape[1]

    @pl.when(g == 0)
    def _():
        u = rim[...].astype(F32)
        hr = (u * rms_inv(u) * gain[...]).astype(BF16)
        vbuf[0:8, :width] = mm(hr, w_x[...])[8:16]
        vbuf[0:8, width:] = mm(hr, w_bc[...])[8:16]
        state[...] = jnp.zeros_like(state)
        decay[...] = jnp.ones_like(decay)

    keep = 1.0 - first[g].astype(F32)
    vbuf[0:8, :] = vbuf[0:8, :] * keep
    state[...] = state[...] * keep
    decay[...] = decay[...] * keep
    vbuf[8:, :] = v[...]
    taps = jnp.concatenate([cx[...], cb[...]], axis=1)
    conv = taps[KCONV : KCONV + 1, :] + taps[0:1, :] * vbuf[5 : 5 + GROUP, :]
    for k in range(1, KCONV):
        conv = conv + taps[k : k + 1, :] * vbuf[5 + k : 5 + k + GROUP, :]
    cv_o[...] = conv
    act = (conv * jax.nn.sigmoid(conv)).astype(BF16)
    xs_o[...] = act[:, :width]
    bc_o[...] = act[:, width:]
    vbuf[0:8, :] = vbuf[GROUP : GROUP + 8, :]
    raw = pre[...]
    live = iota((GROUP, LANES), 0) < valid[g]
    soft = jnp.maximum(raw, 0.0) + jnp.log1p(jnp.exp(-jnp.abs(raw)))
    dt = jnp.where(live, soft, 0.0)
    dt_o[...] = dt
    ld = dt * -jnp.exp(hp[1:2, :])
    lower = tri("le").astype(BF16)
    lower = jnp.concatenate([lower] * 3, axis=1)
    for c in range(PARTS):
        rows = slice(c * CHUNK, (c + 1) * CHUNK)
        cum = mm(lower, jnp.concatenate(split3(ld[rows]), axis=0))
        cum_o[rows, :] = cum
        end = cum[CHUNK - 1 : CHUNK, :]
        factor = dt[rows] * jnp.exp(end - cum)
        ent_o[c] = state[...]
        pd_o[c] = decay[0:1]
        xd = act[rows, :width].astype(F32) * spread(factor, width)
        new = mm_right(act[rows, width : width + N], xd, 0, 0)
        ec = spread(jnp.exp(end), width)
        state[...] = state[...] * ec + new
        decay[...] = decay[...] * ec

    @pl.when(g == pl.num_programs(0) - 1)
    def _():
        fin_o[0:N, :] = state[...]
        fin_o[N:, :] = decay[...]


def k_proj(h, og, w_z, w_out, z_o, gyn_o):
    z_o[...] = mm(h[...], w_z[...])
    gyn_o[...] = mm(og[...], w_out[...], 1, 1)


def k_within(xs, bc, dt, cum, y_o):
    width = xs.shape[1]
    mask = tri("le")
    for c in range(PARTS):
        rows = slice(c * CHUNK, (c + 1) * CHUNK)
        scores = mm(bc[rows, N:], bc[rows, :N], 1, 1)
        a = cum[rows, :]
        b = jnp.transpose(a - jnp.log(dt[rows, :]))
        for p in range(width // LANES):
            lanes = slice(p * LANES, (p + 1) * LANES)
            weights = []
            for h in (2 * p, 2 * p + 1):
                gap = a[:, h : h + 1] - b[h : h + 1, :]
                weights.append(jnp.where(mask, jnp.exp(gap), 0.0) * scores)
            y_o[rows, lanes] = mm_left(jnp.concatenate(weights, axis=1), pair_rows(xs[rows, lanes]))


def k_gate(ent, pd, prev, bc, cum, yw, xs, z, gyn, gain, hp, mix_o, ent_o, sums_o):
    width = xs.shape[1]
    skip = spread(hp[2:3, :], width)
    for c in range(PARTS):
        rows = slice(c * CHUNK, (c + 1) * CHUNK)
        entry = ent[c] + pd[c] * prev[0:N, :]
        ent_o[c] = entry
        across = mm_right(bc[rows, N:], entry) * spread(jnp.exp(cum[rows, :]), width)
        mix_o[rows, :] = yw[rows, :] + across + skip * xs[rows, :].astype(F32)
    zz = z[...]
    gated = mix_o[...] * (zz * jax.nn.sigmoid(zz))
    square = jnp.sum(gated * gated, axis=1, keepdims=True)
    inner = jnp.sum(gyn[...] * gain[...] * gated, axis=1, keepdims=True)
    lane = iota((GROUP, LANES), 1)
    both = jnp.where(lane == 0, square, inner)
    sums_o[...] = jnp.transpose(both)[0:2, :]


def k_gate_back(
    total, count, first, mix, z, gyn, gain, xs, bc, cum, *rest,
):
    sums = rest[:count]
    yn_o, g_o, gz_o, ds_o, qd_o, again_o, askip_o, fin_o, state, decay = rest[count:]
    i = pl.program_id(0)
    g = pl.num_programs(0) - 1 - i
    width = xs.shape[1]

    @pl.when(i == 0)
    def _():
        state[...] = jnp.zeros_like(state)
        decay[...] = jnp.ones_like(decay)
        again_o[...] = jnp.zeros_like(again_o)
        askip_o[...] = jnp.zeros_like(askip_o)

    rows2 = tree([part[...] for part in sums])
    both = jnp.transpose(jnp.concatenate([rows2, jnp.zeros((LANES - 2, GROUP), F32)], axis=0))
    inv = lax.rsqrt(both[:, 0:1] / total + EPS)
    inner = both[:, 1:2] / total
    zz = z[...]
    sig = jax.nn.sigmoid(zz)
    silu = zz * sig
    mixer = mix[...]
    gated = mixer * silu
    scaled = gated * inv
    gy = gyn[...]
    gn = gain[...]
    yn_o[...] = (scaled * gn).astype(BF16)
    again_o[...] += fold_rows(gy * scaled)
    gg = inv * gn * gy - gated * (inv * inv * inv * inner)
    gm = (gg * silu).astype(BF16)
    g_o[...] = gm
    gz_o[...] = (gg * mixer * sig * (1.0 + zz * (1.0 - sig))).astype(BF16)
    gmf = gm.astype(F32)
    askip_o[...] += fold_rows(gmf * xs[...].astype(F32))
    for c in reversed(range(PARTS)):
        rows = slice(c * CHUNK, (c + 1) * CHUNK)
        ecum = spread(jnp.exp(cum[rows, :]), width)
        ds_o[c] = state[...]
        qd_o[c] = decay[0:1]
        new = mm_right(bc[rows, N:], gmf[rows] * ecum, 0, 0)
        ec = ecum[CHUNK - 1 : CHUNK, :]
        state[...] = state[...] * ec + new
        decay[...] = decay[...] * ec
    keep = 1.0 - first[g].astype(F32)
    state[...] = state[...] * keep
    decay[...] = decay[...] * keep

    @pl.when(i == pl.num_programs(0) - 1)
    def _():
        fin_o[0:N, :] = state[...]
        fin_o[N:, :] = decay[...]


def k_weights(place, yn, og, h, gz, keep_o, send_o, acc_z, acc_out):
    i = pl.program_id(0)

    @pl.when(i == 0)
    def _():
        acc_z[...] = jnp.zeros_like(acc_z)
        acc_out[...] = jnp.zeros_like(acc_out)

    acc_z[...] += mm(h[...], gz[...], 0, 0)
    acc_out[...] += mm(yn[...], og[...], 0, 0)

    @pl.when(i == pl.num_programs(0) - 1)
    def _():
        count = keep_o.shape[0]
        rz, ro = acc_z.shape[0] // (2 * count), acc_out.shape[0] // (2 * count)
        side = place[3] % 2
        for k in range(count):
            for out, at in ((keep_o, 2 * k + side), (send_o, 2 * k + 1 - side)):
                out[k] = jnp.concatenate(
                    [
                        stacked(acc_z[pl.ds(pl.multiple_of(at * rz, 8), rz), :]),
                        stacked(acc_out[pl.ds(pl.multiple_of(at * ro, 8), ro), :]),
                    ],
                    axis=0,
                )


def k_pair(place, keep, arrived, *outs):
    for k, out in enumerate(outs):
        at = (place[3] // 2) ^ k
        out[...] = (keep[at] + arrived[at]).astype(BF16)


def k_join(mask, place, mine, other, out):
    count = mine.shape[0]
    upper = (place[3] // mask) % 2
    out[pl.ds(upper * count, count)] = mine[...]
    out[pl.ds((1 - upper) * count, count)] = other[...]


def k_within_back(
    xs, bc, g, dt, cum, mix, ent, hp,
    dxw_o, dbc_o, rq_o, qw_o,
):
    width = xs.shape[1]
    mask = tri("ge")
    heads = gather_heads(width)
    skip = spread(hp[2:3, :], width)
    for c in range(PARTS):
        rows = slice(c * CHUNK, (c + 1) * CHUNK)
        bw, cr = bc[rows, :N], bc[rows, N:]
        scores = mm(bw, cr, 1, 1)
        a = cum[rows, :]
        b = a - jnp.log(dt[rows, :])
        at = jnp.transpose(a)
        dscore = jnp.zeros((CHUNK, CHUNK), F32)
        for p in range(width // LANES):
            lanes = slice(p * LANES, (p + 1) * LANES)
            decays = [
                jnp.where(mask, jnp.exp(at[h : h + 1, :] - b[:, h : h + 1]), 0.0)
                for h in (2 * p, 2 * p + 1)
            ]
            gt = g[rows, lanes]
            pairs = mm(pair_rows(xs[rows, lanes]), gt, 1, 1)
            dscore = dscore + pairs[:CHUNK] * decays[0] + pairs[CHUNK:] * decays[1]
            weights = jnp.concatenate([d * scores for d in decays], axis=1)
            dxw_o[rows, lanes] = mm_left(weights, pair_rows(gt))
        high, low = split2(dscore)
        gf = g[rows, :].astype(F32)
        xf = xs[rows, :].astype(F32)
        ge = gf * spread(jnp.exp(a), width)
        dbc_o[rows, :N] = mm(high, cr) + mm(low, cr)
        dbc_o[rows, N:] = mm(high, bw, 0, 0) + mm(low, bw, 0, 0) + mm_both(ge, ent[c], 1, 1)
        row_part = mm_left(gf * (mix[rows, :] - skip * xf), heads)
        col_part = mm_left(xf * dxw_o[rows, :], heads)
        rq_o[rows, :] = row_part - col_part
        qw_o[rows, :] = col_part


def silu_slope(value):
    sig = jax.nn.sigmoid(value)
    return sig * (1.0 + value * (1.0 - sig))


def k_rim(first, xs, bc, g, dt, cum, cend, dxw, dbc, cv, ds, qd, endg, hp, out, lead_o):
    i = pl.program_id(0)
    width = xs.shape[1]
    d_state = ds[0] + qd[0] * endg[0:N, :]
    factor = spread(dt[...] * jnp.exp(cend[7:8, :] - cum[...]), width)
    skip = spread(hp[2:3, :], width)
    xd = xs[...].astype(F32) * factor
    gx = dxw[...] + factor * mm_right(bc[:, :N], d_state) + g[...].astype(F32) * skip
    gb = dbc[:, :N] + mm_both(xd, d_state, 1, 1)
    slope = silu_slope(cv[...]) * (1.0 - first[i].astype(F32))
    out[0, :, :width] = gx * slope[:, :width]
    out[0, :, width : width + N] = gb * slope[:, width : width + N]
    out[0, :, width + N :] = dbc[:, N:] * slope[:, width + N :]

    @pl.when(i == 0)
    def _():
        lead_o[...] = out[0, 0:8, :]


def k_back(
    place, valid, h, xs, bc, g, pre, dt, cum, v, cv, dxw, dbc, rq, qw, ent, ds, qd, endg,
    rims, rim_in, cx, cb, hp, acc_gain, acc_skip,
    gx_o, gbc_o, gpre_o, grads_o, keep_o, send_o,
    gbuf, small_o, acc_x, acc_bc, acc_dt, acc_taps, acc_heads,
):
    i = pl.program_id(0)
    last = pl.num_programs(0) - 1
    width = xs.shape[1]
    heads = gather_heads(width)
    skip = spread(hp[2:3, :], width)
    rate = -jnp.exp(hp[1:2, :])

    @pl.when(i == 0)
    def _():
        for ref in (acc_x, acc_bc, acc_dt, acc_taps, acc_heads):
            ref[...] = jnp.zeros_like(ref)

    upper, below = tri("ge").astype(BF16), tri("lt").astype(BF16)
    both = jnp.concatenate([upper, upper, below, below], axis=1)
    for c in range(PARTS):
        rows = slice(c * CHUNK, (c + 1) * CHUNK)
        d_state = ds[c] + qd[c] * endg[0:N, :]
        d_high, d_low = split2(d_state)
        a = cum[rows, :]
        end = a[CHUNK - 1 : CHUNK, :]
        factor = spread(dt[rows, :] * jnp.exp(end - a), width)
        xf = xs[rows, :].astype(F32)
        bw = bc[rows, :N]
        dxs = factor * (mm(bw, d_high) + mm(bw, d_low))
        x_high, x_low = split2(xf * factor)
        gb = dbc[rows, :N] + (mm(x_high, d_high, 1, 1) + mm(x_low, d_high, 1, 1) + mm(x_high, d_low, 1, 1))
        gx = dxw[rows, :] + dxs + g[rows, :].astype(F32) * skip
        slope = silu_slope(cv[rows, :])
        gbuf[rows, :width] = gx * slope[:, :width]
        gbuf[rows, width : width + N] = gb * slope[:, width : width + N]
        gbuf[rows, width + N :] = dbc[rows, N:] * slope[:, width + N :]
        qs = mm_left(xf * dxs, heads)
        carried = mm_left(fold_rows(d_state * ent[c]), heads)
        ends = jnp.sum(carried, axis=0, keepdims=True) * jnp.exp(end)
        g_ld = mm(both, jnp.concatenate(split2(rq[rows, :]) + split2(qs), axis=0)) + ends
        step = dt[rows, :]
        direct = jnp.where(step > 0.0, (qw[rows, :] + qs) / jnp.where(step > 0.0, step, 1.0), 0.0)
        live = iota((CHUNK, LANES), 0) + c * CHUNK < valid[i]
        own = iota((CHUNK, LANES), 1) < width // P_SIZE
        g_pre = jnp.where(
            live & own, (direct + g_ld * rate) * jax.nn.sigmoid(pre[rows, :]), 0.0
        )
        acc_heads[0:8, :] += fold_rows(g_pre)
        acc_heads[8:16, :] += fold_rows(g_ld * step * rate)
        low = g_pre.astype(BF16)
        gpre_o[rows, :] = low
        acc_dt[...] += mm(pltpu.roll(low.astype(F32), place[1], 1).astype(BF16), h[rows, :], 0, 0)[0 : acc_dt.shape[0]]

    @pl.when(i < last)
    def _():
        gbuf[GROUP:, :] = rims[0, 0:8, :]

    @pl.when(i == last)
    def _():
        gbuf[GROUP:, :] = rim_in[0:8, :]

    taps = jnp.concatenate([cx[...], cb[...]], axis=1)
    vv = v[...]
    gv = jnp.zeros_like(vv)
    for k in range(KCONV):
        shifted = gbuf[KCONV - 1 - k : KCONV - 1 - k + GROUP, :]
        gv = gv + taps[k : k + 1, :] * shifted
        acc_taps[8 * k : 8 * k + 8, :] += fold_rows(vv * shifted)
    acc_taps[8 * KCONV :, :] += fold_rows(gbuf[0:GROUP, :])
    gx_low = gv[:, :width].astype(BF16)
    bc_high, bc_low = split2(gv[:, width:])
    gx_o[...] = gx_low
    gbc_o[:, : 2 * N] = bc_high
    gbc_o[:, 2 * N :] = bc_low
    hh = h[...]
    acc_x[...] += mm(hh, gx_low, 0, 0)
    acc_bc[...] += mm(hh, bc_high, 0, 0) + mm(hh, bc_low, 0, 0)

    @pl.when(i == last)
    def _():
        count = grads_o.shape[0]
        rx = acc_x.shape[0] // count
        for k in range(count):
            grads_o[k] = stacked(acc_x[k * rx : (k + 1) * rx, :]).astype(BF16)
        dim = acc_bc.shape[0]
        at = 0

        def put(value):
            nonlocal at
            small_o[at : at + value.shape[0], :] = value
            at += value.shape[0]

        put(acc_bc[:, :LANES])
        put(acc_bc[:, LANES:])
        put(stacked(acc_dt[...]))

        def line(value):
            return jnp.sum(value, axis=0, keepdims=True)

        def lane_home(value):
            return pltpu.roll(jnp.broadcast_to(value, (8, LANES)), place[1], 1)[0:1]

        own = iota((1, LANES), 1) < width // P_SIZE
        taps_sum = [line(acc_taps[8 * k : 8 * k + 8, :]) for k in range(KCONV + 1)]
        skips = mm_left(acc_skip[...], heads)
        head_rows = [
            lane_home(jnp.where(own, line(x), 0.0))
            for x in (acc_heads[0:8, :], acc_heads[8:16, :], skips)
        ]
        put(jnp.concatenate([t[:, width : width + N] for t in taps_sum] + head_rows, axis=0))
        spare = jnp.zeros((8 - KCONV - 1, LANES), F32)
        put(jnp.concatenate([t[:, width + N :] for t in taps_sum] + [spare], axis=0))
        small_o[at:, :] = jnp.zeros_like(small_o[at:, :])
        gains = line(acc_gain[...])
        tiles = width // LANES
        own_rows = jnp.concatenate(
            [
                jnp.concatenate(
                    [t[:, k * LANES : (k + 1) * LANES] for t in taps_sum]
                    + [gains[:, k * LANES : (k + 1) * LANES], spare[0:2]],
                    axis=0,
                )
                for k in range(tiles)
            ],
            axis=0,
        )
        small_o[pl.ds(pl.multiple_of(at + place[2] * (8 * tiles), 8), 8 * tiles), :] = own_rows
        rows = keep_o.shape[0]
        keep_o[...] = small_o[pl.ds(pl.multiple_of(place[0] * rows, 8), rows), :]
        send_o[...] = small_o[pl.ds(pl.multiple_of((1 - place[0]) * rows, 8), rows), :]


def input_grad(hid, gz, gx, gbc, gpre, w_z, w_x, w_bc, w_dt):
    gh = (
        mm(gpre[...], w_dt[...], 1, 1)
        + mm(gz[...], w_z[...], 1, 1)
        + mm(gx[...], w_x[...], 1, 1)
        + mm(gbc[:, : 2 * N], w_bc[...], 1, 1)
        + mm(gbc[:, 2 * N :], w_bc[...], 1, 1)
    )
    u = hid[...].astype(F32)
    return gh, fold_rows(gh * (u * rms_inv(u)))


def k_input_sent(place, *refs):
    out, norm_o = refs[9:]

    @pl.when(pl.program_id(0) == 0)
    def _():
        norm_o[...] = jnp.zeros_like(norm_o)

    gh, norm = input_grad(*refs[:9])
    out[...] = gh
    norm_o[...] += norm


def k_input_own(place, *refs):
    arrived, before, out, norm_o, acc = refs[9:]
    i = pl.program_id(0)

    @pl.when(i == 0)
    def _():
        acc[...] = before[...]

    gh, norm = input_grad(*refs[:9])
    out[...] = (gh + arrived[...]).astype(BF16)
    acc[...] += norm

    @pl.when(i == pl.num_programs(0) - 1)
    def _():
        rows = acc.shape[1] // LANES
        norm_o[0:rows, :] = stacked(jnp.sum(acc[...], axis=0, keepdims=True))
        norm_o[rows:, :] = jnp.zeros((8 - rows, LANES), F32)


def k_reduce(*refs):
    out = refs[-1]
    out[...] = tree([part[...].astype(F32) for part in refs[:-1]]).astype(BF16)


def k_halve(mask, place, kept, arrived, keep_o, send_o):
    rows = keep_o.shape[0]
    upper = (place[2] // mask) % 2
    for out, at in ((keep_o, upper * rows), (send_o, (1 - upper) * rows)):
        at = pl.multiple_of(at, 8)
        out[...] = kept[pl.ds(at, rows), :] + arrived[pl.ds(at, rows), :]


def k_pieces(kept, arrived, norm, out):
    count = out.shape[0]
    rows = kept.shape[0] // count
    spare = jnp.zeros((7, LANES), F32)
    for k in range(count):
        own = slice(k * rows, (k + 1) * rows)
        out[k, 0:rows, :] = kept[own, :] + arrived[own, :]
        line = norm[k : k + 1, :] if k < 8 else spare[0:1]
        out[k, rows:, :] = jnp.concatenate([line, spare], axis=0)


def k_reduce_both(large, small, out):
    count = out.shape[0]
    total = tree([large[k].astype(F32) for k in range(count)]).astype(BF16)
    rest = tree([small[k] for k in range(count)])
    joined = jnp.concatenate([total, *split2(rest)], axis=0)
    for k in range(count):
        out[k] = joined


def k_quarter(cut, parts, out):
    count = parts.shape[0]
    rows = out.shape[0] // count - 1
    for k in range(count):
        value = parts[k, cut:, :].astype(F32)
        value = value[: rows + 8] + value[rows + 8 :]
        out[k * rows : (k + 1) * rows, :] = value[:rows]
        out[count * rows + k : count * rows + k + 1, :] = value[rows : rows + 1]


def unstack(value, rows):
    return jnp.concatenate(
        [value[k : k + rows, :] for k in range(0, value.shape[0], rows)], axis=1
    )


def k_unpack(place, mine, other, b, w_zx_o, w_out_o):
    count = b.shape[0]
    dim, _, real = w_zx_o.shape
    rz = dim // count
    width = -(-real // LANES) * LANES
    cut = rz * width // LANES
    ro = width // count
    side = place[3] % 2
    for k in range(count // 2):
        for part, at in ((mine, 2 * k + side), (other, 2 * k + 1 - side)):
            piece = part[k].astype(F32)
            w_zx_o[pl.ds(at * rz, rz), 0, :] = unstack(piece[0:cut], rz)[:, :real]
            w_out_o[pl.ds(pl.multiple_of(at * ro, 8), ro), :] = unstack(piece[cut:], ro)
    for k in range(count):
        own = unstack(b[k, 0:cut, :].astype(F32), rz)[:, :real]
        w_zx_o[k * rz : (k + 1) * rz, 1, :] = own


def k_small(place, *refs):
    count = len(refs) - 9
    w_bc_o, w_dt_o, bc_taps_o, bias_o, alog_o, skip_o, norm_o, own_o, buf = refs[count:]
    quarter = buf.shape[0] // count
    norms = []
    for k in range(count):
        from_head, at = place[2] ^ k, 0
        for mask in powers(count):
            at = 2 * at + (from_head // mask) % 2
        buf[pl.ds(pl.multiple_of(at * quarter, 8), quarter), :] = refs[k][0:quarter, :]
        norms.append(refs[k][quarter : quarter + 8, :])
    norm = tree(norms)
    dim = w_bc_o.shape[0]
    for k in range(dim // LANES):
        norm_o[:, k * LANES : (k + 1) * LANES] = norm[k : k + 1, :]
    w_bc_o[:, :LANES] = buf[0:dim, :]
    w_bc_o[:, LANES:] = buf[dim : 2 * dim, :]
    at = 2 * dim
    heads = w_dt_o.shape[0]
    w_dt_o[...] = unstack(buf[at : at + heads * dim // LANES, :], heads)
    at += heads * dim // LANES
    bc_taps_o[...] = unstack(buf[at : at + 16, :], 8)[0 : KCONV + 1]
    for k, out in enumerate((bias_o, alog_o, skip_o)):
        out[...] = buf[at + KCONV + 1 + k : at + KCONV + 2 + k, 0 : out.shape[1]]
    tiles = -(-own_o.shape[1] // LANES)
    own = buf[pl.ds(pl.multiple_of(at + 16 + place[2] * (8 * tiles), 8), 8 * tiles), :]
    own_o[...] = unstack(own, 8)[:, 0 : own_o.shape[1]]


def k_out(hid, *refs):
    count = (len(refs) - 1) // 2
    out = refs[-1]
    total = tree([mm(refs[k][...], refs[count + k][...]) for k in range(count)])
    out[...] = (hid[...].astype(F32) + total).astype(BF16)


def k_in_back(place, hid, og, gain, *refs):
    i = pl.program_id(0)
    half = pl.num_programs(0) // 2
    count = (len(refs) - 1) // 2
    out = refs[-1]

    def finish(parts):
        gh = tree([part[...].astype(F32) for part in parts])
        u = hid[...].astype(F32)
        inv = rms_inv(u)
        scaled = gh * gain[...]
        dot = jnp.sum(scaled * u, axis=1, keepdims=True) / u.shape[1]
        out[...] = inv * scaled - u * (inv * inv * inv * dot) + og[...].astype(F32)

    @pl.when(i < half)
    def _():
        finish(refs[:count])

    @pl.when(i >= half)
    def _():
        finish(refs[count : 2 * count])


def row_block(shape, rows, at=None):
    at = at or (lambda i, *s: i)
    rest = tuple(shape[1:])
    return pl.BlockSpec((rows,) + rest, lambda i, *s: (at(i, *s),) + (0,) * len(rest))


def whole(shape):
    return pl.BlockSpec(tuple(shape), lambda i, *s: (0,) * len(shape))


SMEM = pl.BlockSpec(memory_space=pltpu.SMEM)


class Kept:
    def __init__(self, rows, at=None):
        self.rows = rows
        self.at = at or (lambda i, *s: i)

    def view(self, ref, i, scalars):
        start = pl.multiple_of(self.at(i, *scalars) * self.rows, self.rows)
        return ref.at[pl.ds(start, self.rows)]


def call(kernel, steps, ins, outs, scratch, flops, name, place=None):
    moved = sum(a.size * a.dtype.itemsize for a, _ in ins)
    for shape, dtype, _ in outs:
        moved += functools.reduce(lambda x, y: x * y, shape) * jnp.dtype(dtype).itemsize
    scalars = [] if place is None else [place]
    specs = [spec for _, spec in ins] + [spec for _, _, spec in outs]
    first = len(scalars)

    def body(*refs):
        i = pl.program_id(0)
        seen = list(refs)
        for k, spec in enumerate(specs):
            if isinstance(spec, Kept):
                seen[first + k] = spec.view(refs[first + k], i, refs[:first])
        kernel(*seen)

    places = [
        pl.BlockSpec(memory_space=pltpu.VMEM) if isinstance(spec, Kept) else spec for spec in specs
    ]
    return pl.pallas_call(
        body,
        grid_spec=pltpu.PrefetchScalarGridSpec(
            num_scalar_prefetch=len(scalars),
            grid=(steps,),
            in_specs=places[: len(ins)],
            out_specs=places[len(ins) :],
            scratch_shapes=scratch,
        ),
        out_shape=[jax.ShapeDtypeStruct(s, d) for s, d, _ in outs],
        compiler_params=pltpu.CompilerParams(
            dimension_semantics=("arbitrary",), vmem_limit_bytes=VMEM_LIMIT
        ),
        cost_estimate=pl.CostEstimate(flops=flops, bytes_accessed=moved, transcendentals=0),
        name=name,
    )(*scalars, *[a for a, _ in ins])


def swap(value, axis, mask):
    return lax.ppermute(value, axis, [(i, i ^ mask) for i in range(lax.axis_size(axis))])


def after(value, *others):
    return lax.optimization_barrier((value,) + others)[0]


def powers(count):
    return [1 << k for k in range(count.bit_length() - 1)]


def k_merge(mask, backward, first, place, *refs):
    total, other = refs[:2]
    before = None if first else refs[2]
    outs = refs[2 if first else 3 :]
    upper = (place[3] // mask) % 2 == 1
    later = jnp.logical_not(upper) if backward else upper

    def merge(early, late, out):
        scale = late[N : N + 1, :]
        out[0:N, :] = scale * early[0:N, :] + late[0:N, :]
        out[N:, :] = scale * early[N:, :]

    @pl.when(later)
    def _():
        if first:
            outs[0][...] = other[...]
        else:
            merge(other, before, outs[0])
        if len(outs) > 1:
            merge(other, total, outs[1])

    @pl.when(jnp.logical_not(later))
    def _():
        if first:
            outs[0][0:N, :] = jnp.zeros((N, total.shape[1]), F32)
            outs[0][N:, :] = jnp.ones((8, total.shape[1]), F32)
        else:
            outs[0][...] = before[...]
        if len(outs) > 1:
            merge(total, other, outs[1])


def carried_in(total, backward, place):
    before, firsts = [], []
    shape = total.shape
    masks = powers(lax.axis_size("tok"))
    for mask in masks:
        ins = [total, swap(total, "tok", mask)] + before
        last = mask == masks[-1]
        found = call(
            functools.partial(k_merge, mask, backward, not before),
            1,
            [(a, whole(shape)) for a in ins],
            [(shape, F32, whole(shape))] * (1 if last else 2),
            [],
            10**6,
            "merge",
            place,
        )
        before, total = [found[0]], found[-1]
        firsts.append(found[0])
    return before[0], firsts[0]


def exchange(pieces, axis):
    return lax.all_to_all(pieces, axis, 0, 0, tiled=True)


def distances(value, axis, step):
    return [value] + [swap(value, axis, step * k) for k in range(1, lax.axis_size(axis) // step)]


def head_gathered(value):
    found = [value]
    masks = powers(lax.axis_size("head"))
    for mask in masks[1:] + masks[:1]:
        found = found + [swap(a, "head", mask) for a in found]
    return found


def on_device(
    hidden_in, norm_gain, w_zx, w_bc, w_dt, dt_bias, a_log, conv_x, conv_bc, d_skip, gate_gain,
    w_out, out_grad, group_first, group_valid,
):
    tokens, dim = hidden_in.shape
    real = w_zx.shape[2]
    own_heads = real // P_SIZE
    heads = w_dt.shape[1]
    groups = tokens // GROUP
    chunks = groups * PARTS
    width = -(-real // LANES) * LANES
    extra = width - real
    conv_width = width + 2 * N
    tok_count = lax.axis_size("tok")
    head_count = lax.axis_size("head")
    head_start = lax.axis_index("head") * own_heads

    def wide(a, dim_at, by=extra):
        return jnp.pad(a, [(0, by if k == dim_at else 0) for k in range(a.ndim)]) if by else a

    route = [(i - 1, i) for i in range(1, tok_count)]
    rim = lax.ppermute(hidden_in[tokens - 16 :], "tok", route)
    w_z = wide(w_zx[:, 0], 1)
    w_x = wide(w_zx[:, 1], 1)
    w_o = wide(w_out, 0)
    w_dt_here = wide(lax.dynamic_slice_in_dim(w_dt, head_start, own_heads, 1), 1, LANES - own_heads)
    per_head = jnp.stack([dt_bias, a_log, d_skip])
    per_head = lax.dynamic_slice_in_dim(per_head, head_start, own_heads, 1)
    per_head = jnp.pad(per_head, ((0, 5), (0, LANES - own_heads)))
    cx = wide(conv_x, 1)
    gain_in = norm_gain[None, :]
    gain_gate = wide(gate_gain, 0)[None, :]
    at_head = lax.axis_index("head")
    place = jnp.stack([at_head & 1, head_start, at_head, lax.axis_index("tok")]).astype(jnp.int32)
    hidden_in, place, w_z, w_x, w_o, w_dt_here, per_head, cx, gain_in, gain_gate = lax.optimization_barrier(
        (hidden_in, place, w_z, w_x, w_o, w_dt_here, per_head, cx, gain_in, gain_gate)
    )
    w_outs = head_gathered(w_o)

    def rows(a, at=None):
        return (a, row_block(a.shape, GROUP, at))

    def full(a):
        return (a, whole(a.shape))

    def kept(a, at=None):
        return (a, Kept(GROUP, at))

    def per_chunk(a, at=None):
        return (a, Kept(PARTS, at))

    def out_rows(cols, dtype, at=None):
        return ((tokens, cols), dtype, row_block((tokens, cols), GROUP, at))

    def out_kept(cols, dtype, at=None):
        return ((tokens, cols), dtype, Kept(GROUP, at))

    def out_full(shape, dtype):
        return (shape, dtype, whole(shape))

    def out_chunk(shape, dtype, at=None):
        return ((chunks,) + shape, dtype, Kept(PARTS, at))

    carry = (N + 8, width)
    h, v, pre = call(
        k_project,
        groups,
        [rows(hidden_in), full(gain_in), full(w_x), full(w_bc), full(w_dt_here), full(per_head)],
        [out_kept(dim, BF16), out_kept(conv_width, F32), out_kept(LANES, F32)],
        [],
        4 * 10**9,
        "project",
    )
    cv, xs, bc, dt, cum, ent, pd, fin = call(
        k_conv,
        groups,
        [
            (group_first, SMEM), (group_valid, SMEM), kept(v), kept(pre), full(rim), full(gain_in),
            full(w_x), full(w_bc), full(per_head), full(cx), full(conv_bc),
        ],
        [
            out_kept(conv_width, F32), out_kept(width, BF16), out_kept(2 * N, BF16),
            out_kept(LANES, F32), out_kept(LANES, F32), out_chunk((N, width), F32),
            out_chunk((1, width), F32), out_full(carry, F32),
        ],
        [
            pltpu.VMEM((GROUP + 8, conv_width), F32), pltpu.VMEM((N, width), F32),
            pltpu.VMEM((8, width), F32),
        ],
        4 * 10**9,
        "conv",
    )
    prev, _ = carried_in(fin, False, place)
    z, gyn = call(
        k_proj,
        groups,
        [kept(h), rows(after(out_grad, fin)), full(w_z), full(w_o)],
        [out_kept(width, F32), out_kept(width, F32)],
        [],
        5 * 10**9,
        "proj",
    )
    (yw,) = call(
        k_within,
        groups,
        [kept(xs), kept(bc), kept(dt), kept(cum)],
        [out_kept(width, F32)],
        [],
        5 * 10**9,
        "within",
    )
    mix, entry, sums = call(
        k_gate,
        groups,
        [
            per_chunk(ent), per_chunk(pd), full(after(prev, *w_outs)), kept(bc), kept(cum), kept(yw), kept(xs),
            kept(z), kept(gyn), full(gain_gate), full(per_head),
        ],
        [
            out_kept(width, F32), out_chunk((N, width), F32),
            ((2, tokens), F32, pl.BlockSpec((2, GROUP), lambda i: (0, i))),
        ],
        [],
        3 * 10**9,
        "gate",
    )
    sums = [sums] + [swap(sums, "head", mask) for mask in range(1, head_count)]

    def back(i):
        return groups - 1 - i

    yn, gm, gz, ds, qd, acc_gain, acc_skip, fin_back = call(
        functools.partial(k_gate_back, float(heads * P_SIZE), head_count),
        groups,
        [
            (group_first, SMEM), kept(mix, back), kept(z, back), kept(gyn, back), full(gain_gate), kept(xs, back),
            kept(bc, back), kept(cum, back),
        ]
        + [(a, pl.BlockSpec((2, GROUP), lambda i: (0, groups - 1 - i))) for a in sums],
        [
            out_kept(width, BF16, back), out_kept(width, BF16, back), out_kept(width, BF16, back),
            out_chunk((N, width), F32, back), out_chunk((1, width), F32, back),
            out_full((8, width), F32), out_full((8, width), F32), out_full(carry, F32),
        ],
        [pltpu.VMEM((N, width), F32), pltpu.VMEM((8, width), F32)],
        3 * 10**9,
        "gate_back",
    )
    end_grad, first_grad = carried_in(fin_back, True, place)
    yns = head_gathered(yn)
    rows_z, rows_o = dim // tok_count, width // tok_count
    piece_a = (rows_z * width + rows_o * dim) // LANES
    sides = tok_count // 2
    keep_a, send_a = call(
        k_weights,
        groups,
        [kept(yn), rows(out_grad), kept(h), kept(gz)],
        [out_full((sides, piece_a, LANES), F32)] * 2,
        [pltpu.VMEM((dim, width), F32), pltpu.VMEM((width, dim), F32)],
        3 * 10**9,
        "weights",
        place,
    )
    arrived_a = swap(after(send_a, first_grad), "tok", 1)
    per_token = [
        out_kept(width, F32), out_kept(2 * N, F32), out_kept(LANES, F32), out_kept(LANES, F32)
    ]
    inner = [kept(xs), kept(bc), kept(after(gm, keep_a)), kept(dt), kept(cum), kept(mix), per_chunk(entry), full(per_head)]
    dxw, dbc, rq, qw = call(
        k_within_back, groups, inner, per_token, [], 10 * 10**9, "within_back"
    )

    def leading(a):
        per = GROUP // 16
        return (a, Kept(16, lambda i: i * per))

    rims, lead = call(
        k_rim,
        groups,
        [
            (group_first, SMEM), leading(xs), leading(bc), leading(gm), leading(dt), leading(cum),
            (cum, Kept(8, lambda i: i * (GROUP // 8) + CHUNK // 8 - 1)),
            leading(dxw), leading(dbc), leading(cv),
            (ds, Kept(1, lambda i: i * PARTS)),
            (qd, Kept(1, lambda i: i * PARTS)),
            full(end_grad), full(per_head),
        ],
        [((groups, 16, conv_width), F32, Kept(1)), out_full((8, conv_width), F32)],
        [],
        10**9,
        "rim",
    )
    rim_in = lax.ppermute(lead, "tok", [(i, i - 1) for i in range(1, tok_count)])
    at_head = lax.axis_index("head")
    place = jnp.stack([at_head & 1, head_start, at_head, lax.axis_index("tok")]).astype(jnp.int32)
    pairs_a = call(
        k_pair,
        1,
        [full(after(keep_a, end_grad)), full(arrived_a)],
        [out_full((piece_a, LANES), BF16)] * sides,
        [],
        10**6,
        "pair",
        place,
    )
    arrived_a = [pairs_a[0]] + [swap(pairs_a[k], "tok", 2 * k) for k in range(1, sides)]
    half = groups // 2
    piece_b = rows_z * width // LANES
    tiles = width // LANES
    small_rows = 2 * dim + heads * dim // LANES + 16 + head_count * 8 * tiles
    unit = head_count * tok_count * 8
    small_rows = -(-small_rows // unit) * unit
    gx, gbc, gpre, grads_b, small_keep, small_send = call(
        k_back,
        groups,
        [
            (group_valid, SMEM),
            kept(h), kept(xs), kept(bc), kept(gm), kept(pre), kept(dt), kept(cum), kept(v), kept(cv),
            kept(dxw), kept(dbc), kept(rq), kept(qw), per_chunk(entry), per_chunk(ds), per_chunk(qd),
            full(end_grad),
            (rims, row_block(rims.shape, 1, lambda i, s: jnp.minimum(i + 1, groups - 1))),
            full(after(rim_in, pairs_a[0], yns[1])), full(cx), full(conv_bc), full(per_head), full(acc_gain), full(acc_skip),
        ],
        [
            out_kept(width, BF16), out_kept(4 * N, BF16), out_kept(LANES, BF16),
            out_full((tok_count, piece_b, LANES), BF16), out_full((small_rows // 2, LANES), F32),
            out_full((small_rows // 2, LANES), F32),
        ],
        [
            pltpu.VMEM((GROUP + 8, conv_width), F32), pltpu.VMEM((small_rows, LANES), F32),
            pltpu.VMEM((dim, width), F32), pltpu.VMEM((dim, 2 * N), F32), pltpu.VMEM((heads, dim), F32),
            pltpu.VMEM((8 * KCONV + 8, conv_width), F32), pltpu.VMEM((16, LANES), F32),
        ],
        10 * 10**9,
        "back",
        place,
    )

    (total_a,) = call(
        k_reduce, 1, [full(a) for a in arrived_a], [out_full((piece_a, LANES), BF16)], [], 10**6, "reduce"
    )

    small_arrived = swap(small_send, "head", 1)
    for mask in powers(head_count)[1:]:
        shape = (small_keep.shape[0] // 2, LANES)
        small_keep, small_send = call(
            functools.partial(k_halve, mask), 1, [full(small_keep), full(small_arrived)],
            [out_full(shape, F32)] * 2, [], 10**6, "halve", place,
        )
        small_arrived = swap(small_send, "head", mask)
    shape = (tokens // 2, dim)

    def input_ins(own):
        def turned(i, s):
            return i + half * (s[0] if own else 1 - s[0])

        return [rows(hidden_in, turned)] + [
            kept(a, turned) for a in (gz, gx, gbc, after(gpre, total_a))
        ] + [
            full(a) for a in (w_z, w_x, w_bc, w_dt_here)
        ]

    sent, norm = call(
        k_input_sent, half, input_ins(False),
        [(shape, F32, row_block(shape, GROUP)), out_full((8, dim), F32)], [], 3 * 10**9,
        "input_sent", place,
    )
    arrived = after(swap(sent, "head", 1), small_keep)
    part, norm = call(
        k_input_own, half, input_ins(True) + [rows(arrived), full(norm)],
        [(shape, BF16, row_block(shape, GROUP)), out_full((8, LANES), F32)],
        [pltpu.VMEM((8, dim), F32)], 3 * 10**9, "input_own", place,
    )
    parts = [after(part, small_arrived)]
    for mask in powers(head_count)[1:]:
        parts = parts + [swap(a, "head", mask) for a in parts]
    others = [swap(a, "head", 1) for a in parts]

    (block_out,) = call(
        k_out,
        groups,
        [rows(hidden_in)] + [rows(a) for a in yns] + [full(a) for a in w_outs],
        [out_rows(dim, BF16)],
        [],
        5 * 10**9,
        "out",
    )
    arrived_b = exchange(grads_b, "tok")
    joined = total_a[None]
    shape = joined.shape
    joins = []
    for mask in powers(sides):
        shape = (2 * shape[0],) + shape[1:]
        (joined,) = call(
            functools.partial(k_join, 2 * mask), 1, [full(joined), full(swap(joined, "tok", 2 * mask))],
            [out_full(shape, BF16)], [], 10**6, "join", place,
        )
        joins.append(joined)
    mine_a = joined
    other_a = swap(mine_a, "tok", 1)
    shape = (tok_count, small_keep.shape[0] // tok_count + 8, LANES)
    (pieces,) = call(
        k_pieces, 1, [full(small_keep), full(small_arrived), full(norm)], [out_full(shape, F32)], [],
        10**6, "pieces",
    )
    pieces = exchange(pieces, "tok")
    shape = (tok_count, piece_b + 2 * pieces.shape[1], LANES)
    (copies,) = call(
        k_reduce_both, 1, [full(after(arrived_b, mine_a)), full(pieces)], [out_full(shape, BF16)], [], 10**6,
        "reduce_both",
    )
    sum_b = exchange(copies, "tok")
    shape = (small_rows // head_count + tok_count, LANES)
    (quarter,) = call(
        functools.partial(k_quarter, piece_b), 1, [full(after(sum_b, block_out))], [out_full(shape, F32)],
        [], 10**6, "quarter",
    )
    quarters = [(quarter, 0)]
    for mask in powers(head_count):
        quarters = quarters + [(swap(a, "head", mask), k | mask) for a, k in quarters]
    quarters = [a for a, _ in sorted(quarters, key=lambda item: item[1])]

    grad_w_zx, grad_w_out = call(
        k_unpack,
        1,
        [full(mine_a), full(other_a), full(sum_b)],
        [out_full((dim, 2, real), F32), out_full((width, dim), F32)],
        [],
        10**6,
        "unpack",
        place,
    )
    grad_w_bc, grad_w_dt, grad_taps, grad_bias, grad_alog, grad_skip, grad_norm, own = call(
        k_small,
        1,
        [full(a) for a in quarters],
        [
            out_full((dim, 2 * N), F32), out_full((heads, dim), F32), out_full((KCONV + 1, 2 * N), F32),
            out_full((1, heads), F32), out_full((1, heads), F32), out_full((1, heads), F32),
            out_full((1, dim), F32), out_full((8, real), F32),
        ],
        [pltpu.VMEM((small_rows, LANES), F32)],
        10**6,
        "small",
        place,
    )

    def turned_back(i, s):
        return lax.rem(i + half * s[0], groups)

    def first_half(a):
        return (a, row_block(a.shape, GROUP, lambda i, s: jnp.minimum(i, half - 1)))

    def second_half(a):
        return (a, row_block(a.shape, GROUP, lambda i, s: jnp.maximum(i - half, 0)))

    (grad_in,) = call(
        k_in_back,
        groups,
        [rows(hidden_in, turned_back), rows(out_grad, turned_back), full(gain_in)]
        + [first_half(a) for a in parts]
        + [second_half(a) for a in others],
        [out_rows(dim, F32, turned_back)],
        [],
        10**9,
        "in_back",
        place,
    )
    return (
        block_out,
        grad_in,
        grad_norm[0],
        grad_w_zx,
        grad_w_bc,
        grad_w_dt.T,
        grad_bias[0],
        grad_alog[0],
        own[: KCONV + 1],
        grad_taps,
        grad_skip[0],
        own[KCONV + 1],
        grad_w_out[:real],
    )


def solution(mesh):
    return jax.shard_map(
        on_device,
        mesh=mesh,
        in_specs=(
            P("tok", None), P(), P(None, None, "head"), P(), P(), P(), P(), P(None, "head"), P(), P(),
            P("head"), P("head", None), P("tok", None), P("tok"), P("tok"),
        ),
        out_specs=(
            P("tok", None), P("tok", None), P(), P(None, None, "head"), P(), P(), P(), P(),
            P(None, "head"), P(), P(), P("head"), P("head", None),
        ),
        check_vma=False,
    )
```

```python
import functools
import math

import jax
import jax.numpy as jnp
from jax import lax
from jax.experimental import pallas as pl
from jax.experimental.pallas import tpu as pltpu
from jax.sharding import PartitionSpec as P

P_SIZE = 64
N = 128
KCONV = 4
GROUP = 256
CHUNK = 128
LANES = 128
PARTS = GROUP // CHUNK
EPS = 1e-05
VMEM_LIMIT = 10 * 1024 * 1024
F32 = jnp.float32
BF16 = jnp.bfloat16


def mm(a, b, ca=1, cb=0):
    return lax.dot_general(a, b, (((ca,), (cb,)), ((), ())), preferred_element_type=F32)


def iota(shape, dim):
    return lax.broadcasted_iota(jnp.int32, shape, dim)


def spread(cols, width):
    rows = cols.shape[0]
    low = iota((rows, LANES), 1) < P_SIZE
    tiles = [
        jnp.where(low, cols[:, 2 * p : 2 * p + 1], cols[:, 2 * p + 1 : 2 * p + 2])
        for p in range(width // LANES)
    ]
    return jnp.concatenate(tiles, axis=1)


def gather_heads(width):
    return (iota((width, LANES), 0) // P_SIZE == iota((width, LANES), 1)).astype(BF16)


def fold_rows(value):
    rows, width = value.shape
    return value.reshape(rows // 8, 8, width).sum(axis=0)


def tri(kind):
    row, col = iota((CHUNK, CHUNK), 0), iota((CHUNK, CHUNK), 1)
    return {"le": col <= row, "ge": col >= row, "lt": col < row}[kind]


def pair_rows(tile):
    low = iota(tile.shape, 1) < P_SIZE
    zero = jnp.zeros_like(tile)
    return jnp.concatenate([jnp.where(low, tile, zero), jnp.where(low, zero, tile)], axis=0)


def split2(value):
    high = value.astype(BF16)
    return high, (value - high.astype(F32)).astype(BF16)


def split3(value):
    high, rest = split2(value)
    return high, rest, (value - high.astype(F32) - rest.astype(F32)).astype(BF16)


def mm_left(a, b, ca=1, cb=0):
    high, low = split2(a)
    return mm(high, b, ca, cb) + mm(low, b, ca, cb)


def mm_right(a, b, ca=1, cb=0):
    high, low = split2(b)
    return mm(a, high, ca, cb) + mm(a, low, ca, cb)


def mm_both(a, b, ca=1, cb=0):
    ah, al = split2(a)
    bh, bl = split2(b)
    return mm(ah, bh, ca, cb) + mm(al, bh, ca, cb) + mm(ah, bl, ca, cb)


def stacked(value):
    return jnp.concatenate(
        [value[:, c : c + LANES] for c in range(0, value.shape[1], LANES)], axis=0
    )


def tree(terms):
    while len(terms) > 1:
        terms = [terms[k] + terms[k + 1] for k in range(0, len(terms), 2)]
    return terms[0]


def rms_inv(u):
    return lax.rsqrt(jnp.mean(u * u, axis=1, keepdims=True) + EPS)


def k_project(hid, gain, w_x, w_bc, w_dt, hp, h_o, v_o, pre_o):
    width = w_x.shape[1]
    u = hid[...].astype(F32)
    h = (u * rms_inv(u) * gain[...]).astype(BF16)
    h_o[...] = h
    v_o[:, :width] = mm(h, w_x[...])
    v_o[:, width:] = mm(h, w_bc[...])
    pre_o[...] = mm(h, w_dt[...]) + hp[0:1, :]


def k_conv(
    first, valid, v, pre, rim, gain, w_x, w_bc, hp, cx, cb,
    cv_o, xs_o, bc_o, dt_o, cum_o, ent_o, pd_o, fin_o,
    vbuf, state, decay,
):
    g = pl.program_id(0)
    width = w_x.shape[1]

    @pl.when(g == 0)
    def _():
        u = rim[...].astype(F32)
        hr = (u * rms_inv(u) * gain[...]).astype(BF16)
        vbuf[0:8, :width] = mm(hr, w_x[...])[8:16]
        vbuf[0:8, width:] = mm(hr, w_bc[...])[8:16]
        state[...] = jnp.zeros_like(state)
        decay[...] = jnp.ones_like(decay)

    keep = 1.0 - first[g].astype(F32)
    vbuf[0:8, :] = vbuf[0:8, :] * keep
    state[...] = state[...] * keep
    decay[...] = decay[...] * keep
    vbuf[8:, :] = v[...]
    taps = jnp.concatenate([cx[...], cb[...]], axis=1)
    conv = taps[KCONV : KCONV + 1, :] + taps[0:1, :] * vbuf[5 : 5 + GROUP, :]
    for k in range(1, KCONV):
        conv = conv + taps[k : k + 1, :] * vbuf[5 + k : 5 + k + GROUP, :]
    cv_o[...] = conv
    act = (conv * jax.nn.sigmoid(conv)).astype(BF16)
    xs_o[...] = act[:, :width]
    bc_o[...] = act[:, width:]
    vbuf[0:8, :] = vbuf[GROUP : GROUP + 8, :]
    raw = pre[...]
    live = iota((GROUP, LANES), 0) < valid[g]
    soft = jnp.maximum(raw, 0.0) + jnp.log1p(jnp.exp(-jnp.abs(raw)))
    dt = jnp.where(live, soft, 0.0)
    dt_o[...] = dt
    ld = dt * -jnp.exp(hp[1:2, :])
    lower = tri("le").astype(BF16)
    lower = jnp.concatenate([lower] * 3, axis=1)
    for c in range(PARTS):
        rows = slice(c * CHUNK, (c + 1) * CHUNK)
        cum = mm(lower, jnp.concatenate(split3(ld[rows]), axis=0))
        cum_o[rows, :] = cum
        end = cum[CHUNK - 1 : CHUNK, :]
        factor = dt[rows] * jnp.exp(end - cum)
        ent_o[c] = state[...]
        pd_o[c] = decay[0:1]
        xd = act[rows, :width].astype(F32) * spread(factor, width)
        new = mm_right(act[rows, width : width + N], xd, 0, 0)
        ec = spread(jnp.exp(end), width)
        state[...] = state[...] * ec + new
        decay[...] = decay[...] * ec

    @pl.when(g == pl.num_programs(0) - 1)
    def _():
        fin_o[0:N, :] = state[...]
        fin_o[N:, :] = decay[...]


def k_proj(h, og, w_z, w_out, z_o, gyn_o):
    z_o[...] = mm(h[...], w_z[...])
    gyn_o[...] = mm(og[...], w_out[...], 1, 1)


def k_within(xs, bc, dt, cum, y_o):
    width = xs.shape[1]
    mask = tri("le")
    for c in range(PARTS):
        rows = slice(c * CHUNK, (c + 1) * CHUNK)
        scores = mm(bc[rows, N:], bc[rows, :N], 1, 1)
        a = cum[rows, :]
        b = jnp.transpose(a - jnp.log(dt[rows, :]))
        for p in range(width // LANES):
            lanes = slice(p * LANES, (p + 1) * LANES)
            weights = []
            for h in (2 * p, 2 * p + 1):
                gap = a[:, h : h + 1] - b[h : h + 1, :]
                weights.append(jnp.where(mask, jnp.exp(gap), 0.0) * scores)
            y_o[rows, lanes] = mm_left(jnp.concatenate(weights, axis=1), pair_rows(xs[rows, lanes]))


def k_gate(ent, pd, prev, bc, cum, yw, xs, z, gyn, gain, hp, mix_o, ent_o, sums_o):
    width = xs.shape[1]
    skip = spread(hp[2:3, :], width)
    for c in range(PARTS):
        rows = slice(c * CHUNK, (c + 1) * CHUNK)
        entry = ent[c] + pd[c] * prev[0:N, :]
        ent_o[c] = entry
        across = mm_right(bc[rows, N:], entry) * spread(jnp.exp(cum[rows, :]), width)
        mix_o[rows, :] = yw[rows, :] + across + skip * xs[rows, :].astype(F32)
    zz = z[...]
    gated = mix_o[...] * (zz * jax.nn.sigmoid(zz))
    square = jnp.sum(gated * gated, axis=1, keepdims=True)
    inner = jnp.sum(gyn[...] * gain[...] * gated, axis=1, keepdims=True)
    lane = iota((GROUP, LANES), 1)
    both = jnp.where(lane == 0, square, inner)
    sums_o[...] = jnp.transpose(both)[0:2, :]


def k_gate_back(
    total, count, first, mix, z, gyn, gain, xs, bc, cum, *rest,
):
    sums = rest[:count]
    yn_o, g_o, gz_o, ds_o, qd_o, again_o, askip_o, fin_o, state, decay = rest[count:]
    i = pl.program_id(0)
    g = pl.num_programs(0) - 1 - i
    width = xs.shape[1]

    @pl.when(i == 0)
    def _():
        state[...] = jnp.zeros_like(state)
        decay[...] = jnp.ones_like(decay)
        again_o[...] = jnp.zeros_like(again_o)
        askip_o[...] = jnp.zeros_like(askip_o)

    rows2 = tree([part[...] for part in sums])
    both = jnp.transpose(jnp.concatenate([rows2, jnp.zeros((LANES - 2, GROUP), F32)], axis=0))
    inv = lax.rsqrt(both[:, 0:1] / total + EPS)
    inner = both[:, 1:2] / total
    zz = z[...]
    sig = jax.nn.sigmoid(zz)
    silu = zz * sig
    mixer = mix[...]
    gated = mixer * silu
    scaled = gated * inv
    gy = gyn[...]
    gn = gain[...]
    yn_o[...] = (scaled * gn).astype(BF16)
    again_o[...] += fold_rows(gy * scaled)
    gg = inv * gn * gy - gated * (inv * inv * inv * inner)
    gm = (gg * silu).astype(BF16)
    g_o[...] = gm
    gz_o[...] = (gg * mixer * sig * (1.0 + zz * (1.0 - sig))).astype(BF16)
    gmf = gm.astype(F32)
    askip_o[...] += fold_rows(gmf * xs[...].astype(F32))
    for c in reversed(range(PARTS)):
        rows = slice(c * CHUNK, (c + 1) * CHUNK)
        ecum = spread(jnp.exp(cum[rows, :]), width)
        ds_o[c] = state[...]
        qd_o[c] = decay[0:1]
        new = mm_right(bc[rows, N:], gmf[rows] * ecum, 0, 0)
        ec = ecum[CHUNK - 1 : CHUNK, :]
        state[...] = state[...] * ec + new
        decay[...] = decay[...] * ec
    keep = 1.0 - first[g].astype(F32)
    state[...] = state[...] * keep
    decay[...] = decay[...] * keep

    @pl.when(i == pl.num_programs(0) - 1)
    def _():
        fin_o[0:N, :] = state[...]
        fin_o[N:, :] = decay[...]


def k_weights(place, yn, og, h, gz, keep_o, send_o, acc_z, acc_out):
    i = pl.program_id(0)

    @pl.when(i == 0)
    def _():
        acc_z[...] = jnp.zeros_like(acc_z)
        acc_out[...] = jnp.zeros_like(acc_out)

    acc_z[...] += mm(h[...], gz[...], 0, 0)
    acc_out[...] += mm(yn[...], og[...], 0, 0)

    @pl.when(i == pl.num_programs(0) - 1)
    def _():
        count = keep_o.shape[0]
        rz, ro = acc_z.shape[0] // (2 * count), acc_out.shape[0] // (2 * count)
        side = place[3] % 2
        for k in range(count):
            for out, at in ((keep_o, 2 * k + side), (send_o, 2 * k + 1 - side)):
                out[k] = jnp.concatenate(
                    [
                        stacked(acc_z[pl.ds(pl.multiple_of(at * rz, 8), rz), :]),
                        stacked(acc_out[pl.ds(pl.multiple_of(at * ro, 8), ro), :]),
                    ],
                    axis=0,
                )


def k_pair(place, keep, arrived, *outs):
    for k, out in enumerate(outs):
        at = (place[3] // 2) ^ k
        out[...] = (keep[at] + arrived[at]).astype(BF16)


def k_join(place, *refs):
    out = refs[-1]
    for k, part in enumerate(refs[:-1]):
        out[(place[3] // 2) ^ k] = part[...]


def k_within_back(
    xs, bc, g, dt, cum, mix, ent, hp,
    dxw_o, dbc_o, rq_o, qw_o,
):
    width = xs.shape[1]
    mask = tri("ge")
    heads = gather_heads(width)
    skip = spread(hp[2:3, :], width)
    for c in range(PARTS):
        rows = slice(c * CHUNK, (c + 1) * CHUNK)
        bw, cr = bc[rows, :N], bc[rows, N:]
        scores = mm(bw, cr, 1, 1)
        a = cum[rows, :]
        b = a - jnp.log(dt[rows, :])
        at = jnp.transpose(a)
        dscore = jnp.zeros((CHUNK, CHUNK), F32)
        for p in range(width // LANES):
            lanes = slice(p * LANES, (p + 1) * LANES)
            decays = [
                jnp.where(mask, jnp.exp(at[h : h + 1, :] - b[:, h : h + 1]), 0.0)
                for h in (2 * p, 2 * p + 1)
            ]
            gt = g[rows, lanes]
            pairs = mm(pair_rows(xs[rows, lanes]), gt, 1, 1)
            dscore = dscore + pairs[:CHUNK] * decays[0] + pairs[CHUNK:] * decays[1]
            weights = jnp.concatenate([d * scores for d in decays], axis=1)
            dxw_o[rows, lanes] = mm_left(weights, pair_rows(gt))
        high, low = split2(dscore)
        gf = g[rows, :].astype(F32)
        xf = xs[rows, :].astype(F32)
        ge = gf * spread(jnp.exp(a), width)
        dbc_o[rows, :N] = mm(high, cr) + mm(low, cr)
        dbc_o[rows, N:] = mm(high, bw, 0, 0) + mm(low, bw, 0, 0) + mm_both(ge, ent[c], 1, 1)
        row_part = mm_left(gf * (mix[rows, :] - skip * xf), heads)
        col_part = mm_left(xf * dxw_o[rows, :], heads)
        rq_o[rows, :] = row_part - col_part
        qw_o[rows, :] = col_part


def silu_slope(value):
    sig = jax.nn.sigmoid(value)
    return sig * (1.0 + value * (1.0 - sig))


def k_rim(first, xs, bc, g, dt, cum, cend, dxw, dbc, cv, ds, qd, endg, hp, out, lead_o):
    i = pl.program_id(0)
    width = xs.shape[1]
    d_state = ds[0] + qd[0] * endg[0:N, :]
    factor = spread(dt[...] * jnp.exp(cend[7:8, :] - cum[...]), width)
    skip = spread(hp[2:3, :], width)
    xd = xs[...].astype(F32) * factor
    gx = dxw[...] + factor * mm_right(bc[:, :N], d_state) + g[...].astype(F32) * skip
    gb = dbc[:, :N] + mm_both(xd, d_state, 1, 1)
    slope = silu_slope(cv[...]) * (1.0 - first[i].astype(F32))
    out[0, :, :width] = gx * slope[:, :width]
    out[0, :, width : width + N] = gb * slope[:, width : width + N]
    out[0, :, width + N :] = dbc[:, N:] * slope[:, width + N :]

    @pl.when(i == 0)
    def _():
        lead_o[...] = out[0, 0:8, :]


def k_back(final, place, *refs):
    (
        valid, h, xs, bc, g, pre, dt, cum, v, cv, dxw, dbc, rq, qw, ent, ds, qd, endg, rims, cx, cb, hp,
    ) = refs[:22]
    if final:
        rim_in, acc_gain, acc_skip = refs[22:25]
        gx_o, gbc_o, gpre_o = refs[33:36]
        acc_x, acc_bc, acc_dt, acc_taps, acc_heads = refs[36:41]
        grads_o, keep_o, send_o, gbuf, small_o = refs[41:]
    else:
        gx_o, gbc_o, gpre_o, acc_x, acc_bc, acc_dt, acc_taps, acc_heads, gbuf = refs[22:]
    i = pl.program_id(0)
    last = pl.num_programs(0) - 1
    group = i + pl.num_programs(0) if final else i
    width = xs.shape[1]
    heads = gather_heads(width)
    skip = spread(hp[2:3, :], width)
    rate = -jnp.exp(hp[1:2, :])

    if not final:

        @pl.when(i == 0)
        def _():
            for ref in (acc_x, acc_bc, acc_dt, acc_taps, acc_heads):
                ref[...] = jnp.zeros_like(ref)

    upper, below = tri("ge").astype(BF16), tri("lt").astype(BF16)
    both = jnp.concatenate([upper, upper, below, below], axis=1)
    for c in range(PARTS):
        rows = slice(c * CHUNK, (c + 1) * CHUNK)
        d_state = ds[c] + qd[c] * endg[0:N, :]
        d_high, d_low = split2(d_state)
        a = cum[rows, :]
        end = a[CHUNK - 1 : CHUNK, :]
        factor = spread(dt[rows, :] * jnp.exp(end - a), width)
        xf = xs[rows, :].astype(F32)
        bw = bc[rows, :N]
        dxs = factor * (mm(bw, d_high) + mm(bw, d_low))
        x_high, x_low = split2(xf * factor)
        gb = dbc[rows, :N] + (mm(x_high, d_high, 1, 1) + mm(x_low, d_high, 1, 1) + mm(x_high, d_low, 1, 1))
        gx = dxw[rows, :] + dxs + g[rows, :].astype(F32) * skip
        slope = silu_slope(cv[rows, :])
        gbuf[rows, :width] = gx * slope[:, :width]
        gbuf[rows, width : width + N] = gb * slope[:, width : width + N]
        gbuf[rows, width + N :] = dbc[rows, N:] * slope[:, width + N :]
        qs = mm_left(xf * dxs, heads)
        carried = mm_left(fold_rows(d_state * ent[c]), heads)
        ends = jnp.sum(carried, axis=0, keepdims=True) * jnp.exp(end)
        g_ld = mm(both, jnp.concatenate(split2(rq[rows, :]) + split2(qs), axis=0)) + ends
        step = dt[rows, :]
        direct = jnp.where(step > 0.0, (qw[rows, :] + qs) / jnp.where(step > 0.0, step, 1.0), 0.0)
        live = iota((CHUNK, LANES), 0) + c * CHUNK < valid[group]
        own = iota((CHUNK, LANES), 1) < width // P_SIZE
        g_pre = jnp.where(
            live & own, (direct + g_ld * rate) * jax.nn.sigmoid(pre[rows, :]), 0.0
        )
        acc_heads[0:8, :] += fold_rows(g_pre)
        acc_heads[8:16, :] += fold_rows(g_ld * step * rate)
        low = g_pre.astype(BF16)
        gpre_o[rows, :] = low
        acc_dt[...] += mm(pltpu.roll(low.astype(F32), place[1], 1).astype(BF16), h[rows, :], 0, 0)[0 : acc_dt.shape[0]]

    gbuf[GROUP:, :] = rims[0, 0:8, :]
    if final:

        @pl.when(i == last)
        def _():
            gbuf[GROUP:, :] = rim_in[0:8, :]

    taps = jnp.concatenate([cx[...], cb[...]], axis=1)
    vv = v[...]
    gv = jnp.zeros_like(vv)
    for k in range(KCONV):
        shifted = gbuf[KCONV - 1 - k : KCONV - 1 - k + GROUP, :]
        gv = gv + taps[k : k + 1, :] * shifted
        acc_taps[8 * k : 8 * k + 8, :] += fold_rows(vv * shifted)
    acc_taps[8 * KCONV :, :] += fold_rows(gbuf[0:GROUP, :])
    gx_low = gv[:, :width].astype(BF16)
    bc_high, bc_low = split2(gv[:, width:])
    gx_o[...] = gx_low
    gbc_o[:, : 2 * N] = bc_high
    gbc_o[:, 2 * N :] = bc_low
    hh = h[...]
    acc_x[...] += mm(hh, gx_low, 0, 0)
    acc_bc[...] += mm(hh, bc_high, 0, 0) + mm(hh, bc_low, 0, 0)
    if not final:
        return

    @pl.when(i == last)
    def _():
        count = grads_o.shape[0]
        rx = acc_x.shape[0] // count
        for k in range(count):
            grads_o[k] = stacked(acc_x[k * rx : (k + 1) * rx, :]).astype(BF16)
        dim = acc_bc.shape[0]
        at = 0

        def put(value):
            nonlocal at
            small_o[at : at + value.shape[0], :] = value
            at += value.shape[0]

        put(acc_bc[:, :LANES])
        put(acc_bc[:, LANES:])
        put(stacked(acc_dt[...]))

        def line(value):
            return jnp.sum(value, axis=0, keepdims=True)

        def lane_home(value):
            return pltpu.roll(jnp.broadcast_to(value, (8, LANES)), place[1], 1)[0:1]

        own = iota((1, LANES), 1) < width // P_SIZE
        taps_sum = [line(acc_taps[8 * k : 8 * k + 8, :]) for k in range(KCONV + 1)]
        skips = mm_left(acc_skip[...], heads)
        head_rows = [
            lane_home(jnp.where(own, line(x), 0.0))
            for x in (acc_heads[0:8, :], acc_heads[8:16, :], skips)
        ]
        put(jnp.concatenate([t[:, width : width + N] for t in taps_sum] + head_rows, axis=0))
        spare = jnp.zeros((8 - KCONV - 1, LANES), F32)
        put(jnp.concatenate([t[:, width + N :] for t in taps_sum] + [spare], axis=0))
        small_o[at:, :] = jnp.zeros_like(small_o[at:, :])
        gains = line(acc_gain[...])
        tiles = width // LANES
        own_rows = jnp.concatenate(
            [
                jnp.concatenate(
                    [t[:, k * LANES : (k + 1) * LANES] for t in taps_sum]
                    + [gains[:, k * LANES : (k + 1) * LANES], spare[0:2]],
                    axis=0,
                )
                for k in range(tiles)
            ],
            axis=0,
        )
        small_o[pl.ds(pl.multiple_of(at + place[2] * (8 * tiles), 8), 8 * tiles), :] = own_rows
        rows = keep_o.shape[0]
        keep_o[...] = small_o[pl.ds(pl.multiple_of(place[0] * rows, 8), rows), :]
        send_o[...] = small_o[pl.ds(pl.multiple_of((1 - place[0]) * rows, 8), rows), :]


def input_grad(hid, gz, gx, gbc, gpre, w_z, w_x, w_bc, w_dt):
    gh = (
        mm(gpre[...], w_dt[...], 1, 1)
        + mm(gz[...], w_z[...], 1, 1)
        + mm(gx[...], w_x[...], 1, 1)
        + mm(gbc[:, : 2 * N], w_bc[...], 1, 1)
        + mm(gbc[:, 2 * N :], w_bc[...], 1, 1)
    )
    u = hid[...].astype(F32)
    return gh, fold_rows(gh * (u * rms_inv(u)))


def k_input(begins, own, ends, place, *refs):
    refs, (out, norm_o, acc) = refs[:-3], refs[-3:]
    i = pl.program_id(0)

    @pl.when(i == 0)
    def _():
        acc[...] = jnp.zeros_like(acc) if begins else refs[-1][...]

    gh, norm = input_grad(*refs[:9])
    out[...] = (gh + refs[9][...]).astype(BF16) if own else gh
    acc[...] += norm

    @pl.when(i == pl.num_programs(0) - 1)
    def _():
        if ends:
            rows = acc.shape[1] // LANES
            norm_o[0:rows, :] = stacked(jnp.sum(acc[...], axis=0, keepdims=True))
            norm_o[rows:, :] = jnp.zeros((8 - rows, LANES), F32)
        else:
            norm_o[...] = acc[...]


def k_reduce(*refs):
    out = refs[-1]
    out[...] = tree([part[...].astype(F32) for part in refs[:-1]]).astype(BF16)


def k_halve(mask, place, kept, arrived, keep_o, send_o):
    rows = keep_o.shape[0]
    upper = (place[2] // mask) % 2
    for out, at in ((keep_o, upper * rows), (send_o, (1 - upper) * rows)):
        at = pl.multiple_of(at, 8)
        out[...] = kept[pl.ds(at, rows), :] + arrived[pl.ds(at, rows), :]


def k_pieces(kept, arrived, norm, large, out):
    count = out.shape[0]
    rows = kept.shape[0] // count
    cut = large.shape[1]
    spare = jnp.zeros((7, LANES), F32)
    for k in range(count):
        own = slice(k * rows, (k + 1) * rows)
        line = norm[k : k + 1, :] if k < 8 else spare[0:1]
        small = jnp.concatenate([kept[own, :] + arrived[own, :], line, spare], axis=0)
        out[k, 0:cut, :] = large[k]
        out[k, cut:, :] = jnp.concatenate(split2(small), axis=0)


def k_reduce_both(cut, parts, out):
    count = out.shape[0]
    rows = (out.shape[1] - cut) // 2
    terms = [parts[k].astype(F32) for k in range(count)]
    small = tree([term[cut : cut + rows] + term[cut + rows :] for term in terms])
    large = tree([term[:cut] for term in terms]).astype(BF16)
    joined = jnp.concatenate([large, *split2(small)], axis=0)
    for k in range(count):
        out[k] = joined


def k_quarter(cut, parts, out):
    count = parts.shape[0]
    rows = out.shape[0] // count - 1
    for k in range(count):
        value = parts[k, cut:, :].astype(F32)
        value = value[: rows + 8] + value[rows + 8 :]
        out[k * rows : (k + 1) * rows, :] = value[:rows]
        out[count * rows + k : count * rows + k + 1, :] = value[rows : rows + 1]


def unstack(value, rows):
    return jnp.concatenate(
        [value[k : k + rows, :] for k in range(0, value.shape[0], rows)], axis=1
    )


def k_unpack_out(place, mine, other, w_out_o):
    count = 2 * mine.shape[0]
    ro = w_out_o.shape[0] // count
    rows = ro * w_out_o.shape[1] // LANES
    side = place[3] % 2
    for k in range(count // 2):
        for part, at in ((mine, 2 * k + side), (other, 2 * k + 1 - side)):
            piece = part[k].astype(F32)
            w_out_o[pl.ds(pl.multiple_of(at * ro, 8), ro), :] = unstack(piece[piece.shape[0] - rows :], ro)


def k_unpack(place, mine, other, b, w_zx_o):
    count = b.shape[0]
    dim, _, real = w_zx_o.shape
    rz = dim // count
    cut = rz * -(-real // LANES)
    side = place[3] % 2
    for k in range(count // 2):
        for part, at in ((mine, 2 * k + side), (other, 2 * k + 1 - side)):
            piece = part[k].astype(F32)
            w_zx_o[pl.ds(at * rz, rz), 0, :] = unstack(piece[0:cut], rz)[:, :real]
    for k in range(count):
        own = unstack(b[k, 0:cut, :].astype(F32), rz)[:, :real]
        w_zx_o[k * rz : (k + 1) * rz, 1, :] = own


def k_small(place, *refs):
    count = len(refs) - 10
    w_bc_o, w_dt_o, bc_taps_o, bias_o, alog_o, skip_o, norm_o, taps_o, gain_o, buf = refs[count:]
    quarter = buf.shape[0] // count
    norms = []
    for k in range(count):
        from_head, at = place[2] ^ k, 0
        for mask in powers(count):
            at = 2 * at + (from_head // mask) % 2
        buf[pl.ds(pl.multiple_of(at * quarter, 8), quarter), :] = refs[k][0:quarter, :]
        norms.append(refs[k][quarter : quarter + 8, :])
    norm = tree(norms)
    dim = w_bc_o.shape[0]
    for k in range(dim // LANES):
        norm_o[:, k * LANES : (k + 1) * LANES] = norm[k : k + 1, :]
    w_bc_o[:, :LANES] = buf[0:dim, :]
    w_bc_o[:, LANES:] = buf[dim : 2 * dim, :]
    at = 2 * dim
    heads = w_dt_o.shape[0]
    w_dt_o[...] = unstack(buf[at : at + heads * dim // LANES, :], heads)
    at += heads * dim // LANES
    bc_taps_o[...] = unstack(buf[at : at + 16, :], 8)[0 : KCONV + 1]
    for k, out in enumerate((bias_o, alog_o, skip_o)):
        out[...] = buf[at + KCONV + 1 + k : at + KCONV + 2 + k, 0 : out.shape[1]]
    real = taps_o.shape[1]
    tiles = -(-real // LANES)
    own = buf[pl.ds(pl.multiple_of(at + 16 + place[2] * (8 * tiles), 8), 8 * tiles), :]
    own = unstack(own, 8)[:, 0:real]
    taps_o[...] = own[0 : KCONV + 1]
    gain_o[...] = own[KCONV + 1 : KCONV + 2]


def k_out(hid, *refs):
    count = (len(refs) - 1) // 2
    out = refs[-1]
    total = tree([mm(refs[k][...], refs[count + k][...]) for k in range(count)])
    out[...] = (hid[...].astype(F32) + total).astype(BF16)


def k_in_back(steps, place, hid, og, gain, *refs):
    i = pl.program_id(0)
    cuts = pl.num_programs(0) // steps
    out = refs[-1]
    count = (len(refs) - 1) // cuts

    def finish(parts):
        gh = tree([part[...].astype(F32) for part in parts])
        u = hid[...].astype(F32)
        inv = rms_inv(u)
        scaled = gh * gain[...]
        dot = jnp.sum(scaled * u, axis=1, keepdims=True) / u.shape[1]
        out[...] = inv * scaled - u * (inv * inv * inv * dot) + og[...].astype(F32)

    for k in range(cuts):
        pl.when(i // steps == k)(functools.partial(finish, refs[k * count : (k + 1) * count]))


def row_block(shape, rows, at=None):
    at = at or (lambda i, *s: i)
    rest = tuple(shape[1:])
    return pl.BlockSpec((rows,) + rest, lambda i, *s: (at(i, *s),) + (0,) * len(rest))


def whole(shape):
    return pl.BlockSpec(tuple(shape), lambda i, *s: (0,) * len(shape))


SMEM = pl.BlockSpec(memory_space=pltpu.SMEM)
VMEM = pl.BlockSpec(memory_space=pltpu.VMEM)


class Kept:
    def __init__(self, rows, at=None):
        self.rows = rows
        self.at = at or (lambda i, *s: i)

    def view(self, ref, i, scalars):
        start = pl.multiple_of(self.at(i, *scalars) * self.rows, self.rows)
        return ref.at[pl.ds(start, self.rows)]


def call(kernel, steps, ins, outs, scratch, flops, name, place=None, weight=1, alias=()):
    moved = sum(a.size * a.dtype.itemsize for a, _ in ins)
    for shape, dtype, _ in outs:
        moved += functools.reduce(lambda x, y: x * y, shape) * jnp.dtype(dtype).itemsize
    scalars = [] if place is None else [place]
    specs = [spec for _, spec in ins] + [spec for _, _, spec in outs]
    first = len(scalars)

    def body(*refs):
        i = pl.program_id(0)
        seen = list(refs)
        for k, spec in enumerate(specs):
            if isinstance(spec, Kept):
                seen[first + k] = spec.view(refs[first + k], i, refs[:first])
        kernel(*seen)

    places = [
        pl.BlockSpec(memory_space=pltpu.VMEM) if isinstance(spec, Kept) else spec for spec in specs
    ]
    held = 4 * 1024 * 1024
    for (shape, dtype), spec in zip(
        [(a.shape, a.dtype) for a, _ in ins] + [(shape, dtype) for shape, dtype, _ in outs], places
    ):
        if spec.block_shape is not None:
            padded = list(spec.block_shape)
            padded[-1] = -(-padded[-1] // LANES) * LANES
            held += 2 * math.prod(padded) * jnp.dtype(dtype).itemsize
    for buffer in scratch:
        held += math.prod(buffer.shape) * jnp.dtype(buffer.dtype).itemsize
    return pl.pallas_call(
        body,
        grid_spec=pltpu.PrefetchScalarGridSpec(
            num_scalar_prefetch=len(scalars),
            grid=(steps,),
            in_specs=places[: len(ins)],
            out_specs=places[len(ins) :],
            scratch_shapes=scratch,
        ),
        out_shape=[jax.ShapeDtypeStruct(s, d) for s, d, _ in outs],
        compiler_params=pltpu.CompilerParams(
            dimension_semantics=("arbitrary",), vmem_limit_bytes=max(VMEM_LIMIT, held)
        ),
        cost_estimate=pl.CostEstimate(
            flops=flops * weight, bytes_accessed=moved * weight, transcendentals=0
        ),
        input_output_aliases={first + k: j for k, j in alias},
        name=name,
    )(*scalars, *[a for a, _ in ins])


def swap(value, axis, mask):
    return lax.ppermute(value, axis, [(i, i ^ mask) for i in range(lax.axis_size(axis))])


def after(value, *others):
    return lax.optimization_barrier((value,) + others)[0]


def powers(count):
    return [1 << k for k in range(count.bit_length() - 1)]


def k_merge(mask, backward, first, place, *refs):
    total, other = refs[:2]
    before = None if first else refs[2]
    outs = refs[2 if first else 3 :]
    upper = (place[3] // mask) % 2 == 1
    later = jnp.logical_not(upper) if backward else upper

    def merge(early, late, out):
        scale = late[N : N + 1, :]
        out[0:N, :] = scale * early[0:N, :] + late[0:N, :]
        out[N:, :] = scale * early[N:, :]

    @pl.when(later)
    def _():
        if first:
            outs[0][...] = other[...]
        else:
            merge(other, before, outs[0])
        if len(outs) > 1:
            merge(other, total, outs[1])

    @pl.when(jnp.logical_not(later))
    def _():
        if first:
            outs[0][0:N, :] = jnp.zeros((N, total.shape[1]), F32)
            outs[0][N:, :] = jnp.ones((8, total.shape[1]), F32)
        else:
            outs[0][...] = before[...]
        if len(outs) > 1:
            merge(total, other, outs[1])


def carried_in(total, backward, place, beside=()):
    before, firsts = [], []
    shape = total.shape
    masks = powers(lax.axis_size("tok"))
    for mask in masks:
        other = swap(total, "tok", mask)
        ins = [total, other if before else after(other, *beside), *before]
        last = mask == masks[-1]
        found = call(
            functools.partial(k_merge, mask, backward, not before),
            1,
            [(a, whole(shape)) for a in ins],
            [(shape, F32, whole(shape))] * (1 if last else 2),
            [],
            10**6,
            "merge",
            place,
        )
        before, total = [found[0]], found[-1]
        firsts.append(found[0])
    return before[0], firsts[0]


def exchange(pieces, axis):
    return lax.all_to_all(pieces, axis, 0, 0, tiled=True)


def distances(value, axis, step):
    return [value] + [swap(value, axis, step * k) for k in range(1, lax.axis_size(axis) // step)]


def head_gathered(value):
    found = [value]
    masks = powers(lax.axis_size("head"))
    for mask in masks[1:] + masks[:1]:
        found = found + [swap(a, "head", mask) for a in found]
    return found


def on_device(
    hidden_in, norm_gain, w_zx, w_bc, w_dt, dt_bias, a_log, conv_x, conv_bc, d_skip, gate_gain,
    w_out, out_grad, group_first, group_valid,
):
    tokens, dim = hidden_in.shape
    real = w_zx.shape[2]
    own_heads = real // P_SIZE
    heads = w_dt.shape[1]
    groups = tokens // GROUP
    chunks = groups * PARTS
    width = -(-real // LANES) * LANES
    extra = width - real
    conv_width = width + 2 * N
    tok_count = lax.axis_size("tok")
    head_count = lax.axis_size("head")
    head_start = lax.axis_index("head") * own_heads

    def wide(a, dim_at, by=extra):
        return jnp.pad(a, [(0, by if k == dim_at else 0) for k in range(a.ndim)]) if by else a

    route = [(i - 1, i) for i in range(1, tok_count)]
    rim = lax.ppermute(hidden_in[tokens - 16 :], "tok", route)
    w_z = wide(w_zx[:, 0], 1)
    w_x = wide(w_zx[:, 1], 1)
    w_o = wide(w_out, 0)
    w_dt_here = wide(lax.dynamic_slice_in_dim(w_dt, head_start, own_heads, 1), 1, LANES - own_heads)
    per_head = jnp.stack([dt_bias, a_log, d_skip])
    per_head = lax.dynamic_slice_in_dim(per_head, head_start, own_heads, 1)
    per_head = jnp.pad(per_head, ((0, 5), (0, LANES - own_heads)))
    cx = wide(conv_x, 1)
    gain_in = norm_gain[None, :]
    gain_gate = wide(gate_gain, 0)[None, :]
    at_head = lax.axis_index("head")
    place = jnp.stack([at_head & 1, head_start, at_head, lax.axis_index("tok")]).astype(jnp.int32)
    hidden_in, place, w_z, w_x, w_o, w_dt_here, per_head, cx, gain_in, gain_gate = lax.optimization_barrier(
        (hidden_in, place, w_z, w_x, w_o, w_dt_here, per_head, cx, gain_in, gain_gate)
    )
    w_outs = head_gathered(w_o)

    def rows(a, at=None):
        return (a, row_block(a.shape, GROUP, at))

    def full(a):
        return (a, whole(a.shape))

    def kept(a, at=None):
        return (a, Kept(GROUP, at))

    def per_chunk(a, at=None):
        return (a, Kept(PARTS, at))

    def out_rows(cols, dtype, at=None):
        return ((tokens, cols), dtype, row_block((tokens, cols), GROUP, at))

    def out_kept(cols, dtype, at=None):
        return ((tokens, cols), dtype, Kept(GROUP, at))

    def out_full(shape, dtype):
        return (shape, dtype, whole(shape))

    def out_chunk(shape, dtype, at=None):
        return ((chunks,) + shape, dtype, Kept(PARTS, at))

    carry = (N + 8, width)
    h, v, pre = call(
        k_project,
        groups,
        [rows(hidden_in), full(gain_in), full(w_x), full(w_bc), full(w_dt_here), full(per_head)],
        [out_kept(dim, BF16), out_kept(conv_width, F32), out_kept(LANES, F32)],
        [],
        4 * 10**9,
        "project",
    )
    cv, xs, bc, dt, cum, ent, pd, fin = call(
        k_conv,
        groups,
        [
            (group_first, SMEM), (group_valid, SMEM), kept(v), kept(pre), full(rim), full(gain_in),
            full(w_x), full(w_bc), full(per_head), full(cx), full(conv_bc),
        ],
        [
            out_kept(conv_width, F32), out_kept(width, BF16), out_kept(2 * N, BF16),
            out_kept(LANES, F32), out_kept(LANES, F32), out_chunk((N, width), F32),
            out_chunk((1, width), F32), out_full(carry, F32),
        ],
        [
            pltpu.VMEM((GROUP + 8, conv_width), F32), pltpu.VMEM((N, width), F32),
            pltpu.VMEM((8, width), F32),
        ],
        4 * 10**9,
        "conv",
    )
    prev, _ = carried_in(fin, False, place)
    z, gyn = call(
        k_proj,
        groups,
        [kept(h), rows(after(out_grad, fin)), full(w_z), full(w_o)],
        [out_kept(width, F32), out_kept(width, F32)],
        [],
        5 * 10**9,
        "proj",
    )
    (yw,) = call(
        k_within,
        groups,
        [kept(xs), kept(bc), kept(dt), kept(cum)],
        [out_kept(width, F32)],
        [],
        5 * 10**9,
        "within",
    )
    mix, entry, sums = call(
        k_gate,
        groups,
        [
            per_chunk(ent), per_chunk(pd), full(after(prev, *w_outs)), kept(bc), kept(cum), kept(yw), kept(xs),
            kept(z), kept(gyn), full(gain_gate), full(per_head),
        ],
        [
            out_kept(width, F32), out_chunk((N, width), F32),
            ((2, tokens), F32, pl.BlockSpec((2, GROUP), lambda i: (0, i))),
        ],
        [],
        3 * 10**9,
        "gate",
    )
    sums = [sums] + [swap(sums, "head", mask) for mask in range(1, head_count)]

    def back(i):
        return groups - 1 - i

    yn, gm, gz, ds, qd, acc_gain, acc_skip, fin_back = call(
        functools.partial(k_gate_back, float(heads * P_SIZE), head_count),
        groups,
        [
            (group_first, SMEM), kept(mix, back), kept(z, back), kept(gyn, back), full(gain_gate), kept(xs, back),
            kept(bc, back), kept(cum, back),
        ]
        + [(a, pl.BlockSpec((2, GROUP), lambda i: (0, groups - 1 - i))) for a in sums],
        [
            out_kept(width, BF16, back), out_kept(width, BF16, back), out_kept(width, BF16, back),
            out_chunk((N, width), F32, back), out_chunk((1, width), F32, back),
            out_full((8, width), F32), out_full((8, width), F32), out_full(carry, F32),
        ],
        [pltpu.VMEM((N, width), F32), pltpu.VMEM((8, width), F32)],
        3 * 10**9,
        "gate_back",
    )
    yns = [yn]
    for mask in powers(head_count)[1:]:
        yns = yns + [swap(a, "head", mask) for a in yns]
    rows_z, rows_o = dim // tok_count, width // tok_count
    piece_a = (rows_z * width + rows_o * dim) // LANES
    sides = tok_count // 2
    keep_a, send_a = call(
        k_weights,
        groups,
        [kept(yn), rows(out_grad), kept(h), kept(gz)],
        [out_full((sides, piece_a, LANES), F32)] * 2,
        [pltpu.VMEM((dim, width), F32), pltpu.VMEM((width, dim), F32)],
        3 * 10**9,
        "weights",
        place,
        4,
    )
    end_grad, first_grad = carried_in(fin_back, True, place, (keep_a,))
    arrived_a = swap(after(send_a, first_grad), "tok", 1)
    per_token = [
        out_kept(width, F32), out_kept(2 * N, F32), out_kept(LANES, F32), out_kept(LANES, F32)
    ]
    inner = [kept(xs), kept(bc), kept(after(gm, keep_a)), kept(dt), kept(cum), kept(mix), per_chunk(entry), full(per_head)]
    dxw, dbc, rq, qw = call(
        k_within_back, groups, inner, per_token, [], 10 * 10**9, "within_back", None, 4
    )

    def leading(a):
        per = GROUP // 16
        return (a, Kept(16, lambda i: i * per))

    rims, lead = call(
        k_rim,
        groups,
        [
            (group_first, SMEM), leading(xs), leading(bc), leading(gm), leading(dt), leading(cum),
            (cum, Kept(8, lambda i: i * (GROUP // 8) + CHUNK // 8 - 1)),
            leading(dxw), leading(dbc), leading(cv),
            (ds, Kept(1, lambda i: i * PARTS)),
            (qd, Kept(1, lambda i: i * PARTS)),
            full(end_grad), full(per_head),
        ],
        [((groups, 16, conv_width), F32, Kept(1)), out_full((8, conv_width), F32)],
        [],
        10**9,
        "rim",
    )
    rim_in = lax.ppermute(lead, "tok", [(i, i - 1) for i in range(1, tok_count)])
    at_head = lax.axis_index("head")
    place = jnp.stack([at_head & 1, head_start, at_head, lax.axis_index("tok")]).astype(jnp.int32)
    pairs_a = call(
        k_pair,
        1,
        [full(after(keep_a, lead)), full(arrived_a)],
        [out_full((piece_a, LANES), BF16)] * sides,
        [],
        10**6,
        "pair",
        place,
    )
    arrived_a = [pairs_a[0]] + [swap(pairs_a[k], "tok", 2 * k) for k in range(1, sides)]
    half = groups // 2
    piece_b = rows_z * width // LANES
    tiles = width // LANES
    small_rows = 2 * dim + heads * dim // LANES + 16 + head_count * 8 * tiles
    unit = head_count * tok_count * 8
    small_rows = -(-small_rows // unit) * unit
    acc_shapes = [(dim, width), (dim, 2 * N), (heads, dim), (8 * KCONV + 8, conv_width), (16, LANES)]

    def back_call(final, more_in, more_out, more_scratch, alias, ready):
        def at(i, *s):
            return i + half if final else i

        return call(
            functools.partial(k_back, final),
            half,
            [(group_valid, SMEM)]
            + [
                kept(a, at)
                for a in (after(h, *ready), xs, bc, gm, pre, dt, cum, v, cv, dxw, dbc, rq, qw)
            ]
            + [per_chunk(entry, at), per_chunk(ds, at), per_chunk(qd, at), full(end_grad)]
            + [(rims, Kept(1, lambda i, s: jnp.minimum(at(i) + 1, groups - 1)))]
            + [full(cx), full(conv_bc), full(per_head)]
            + more_in,
            [out_kept(width, BF16, at), out_kept(4 * N, BF16, at), out_kept(LANES, BF16, at)]
            + [(a, F32, VMEM) for a in acc_shapes]
            + more_out,
            [pltpu.VMEM((GROUP + 8, conv_width), F32)] + more_scratch,
            5 * 10**9,
            "back_end" if final else "back_start",
            place,
            4,
            alias,
        )

    partial = back_call(False, [], [], [], (), (pairs_a[0],))
    (total_a,) = call(
        k_reduce, 1, [full(after(a, partial[0])) for a in arrived_a], [out_full((piece_a, LANES), BF16)],
        [], 10**6, "reduce",
    )
    found = back_call(
        True,
        [full(rim_in), full(acc_gain), full(acc_skip)] + [(a, VMEM) for a in partial],
        [
            out_full((tok_count, piece_b, LANES), BF16), out_full((small_rows // 2, LANES), F32),
            out_full((small_rows // 2, LANES), F32),
        ],
        [pltpu.VMEM((small_rows, LANES), F32)],
        [(25 + k, k) for k in range(8)],
        (total_a, yns[1]),
    )
    gx, gbc, gpre = found[:3]
    grads_b, small_keep, small_send = found[8:]
    parts_a = distances(total_a, "tok", 2)
    (mine_a,) = call(
        k_join, 1, [full(after(a, gx)) for a in parts_a], [out_full((sides, piece_a, LANES), BF16)], [],
        10**6, "join", place,
    )

    cuts = 2
    steps = half // cuts
    shape = (tokens // 2 // cuts, dim)

    def input_call(own, k, norm, more, ready):
        def turned(i, s):
            return i + k * steps + half * (s[0] if own else 1 - s[0])

        ends = own and k == cuts - 1
        return call(
            functools.partial(k_input, norm is None, own, ends),
            steps,
            [rows(hidden_in, turned)]
            + [kept(a, turned) for a in (gz, gx, gbc, after(gpre, *ready))]
            + [full(a) for a in (w_z, w_x, w_bc, w_dt_here)]
            + [rows(a) for a in more]
            + ([] if norm is None else [full(norm)]),
            [
                (shape, BF16 if own else F32, row_block(shape, GROUP)),
                out_full((8, LANES if ends else dim), F32),
            ],
            [pltpu.VMEM((8, dim), F32)],
            10**9,
            "input_own" if own else "input_sent",
            place,
        )

    sent, norm = input_call(False, 0, None, [], (mine_a,))
    arrived = [swap(sent, "head", 1)]
    small_arrived = after(swap(after(small_send, mine_a), "head", 1), sent)
    for mask in powers(head_count)[1:]:
        small_shape = (small_keep.shape[0] // 2, LANES)
        small_keep, small_send = call(
            functools.partial(k_halve, mask), 1, [full(small_keep), full(small_arrived)],
            [out_full(small_shape, F32)] * 2, [], 10**6, "halve", place,
        )
        small_arrived = swap(small_send, "head", mask)
    for k in range(1, cuts):
        sent, norm = input_call(False, k, norm, [], (mine_a, small_keep))
        arrived.append(swap(sent, "head", 1))
    parts = []
    for k in range(cuts):
        part, norm = input_call(True, k, norm, [arrived[k]], (mine_a,))
        found = [part]
        for mask in powers(head_count)[1:]:
            found = found + [swap(a, "head", mask) for a in found]
        parts.append(found)

    shape = (tok_count, piece_b + 2 * (small_keep.shape[0] // tok_count + 8), LANES)
    (pieces,) = call(
        k_pieces, 1, [full(small_keep), full(small_arrived), full(norm), full(grads_b)],
        [out_full(shape, BF16)], [], 10**6, "pieces",
    )
    other_a = swap(after(mine_a, pieces), "tok", 1)
    yns = yns + [swap(after(a, pieces), "head", 1) for a in yns]
    (block_out,) = call(
        k_out,
        groups,
        [rows(after(hidden_in, pieces))] + [rows(a) for a in yns] + [full(a) for a in w_outs],
        [out_rows(dim, BF16)],
        [],
        5 * 10**9,
        "out",
    )

    (copies,) = call(
        functools.partial(k_reduce_both, piece_b), 1,
        [full(after(exchange(pieces, "tok"), block_out, other_a))],
        [out_full(shape, BF16)], [], 10**6, "reduce_both",
    )
    sum_b = exchange(copies, "tok")
    (grad_w_out,) = call(
        k_unpack_out, 1, [full(after(mine_a, copies)), full(other_a)], [out_full((width, dim), F32)],
        [], 10**6, "unpack_out", place,
    )
    others = [
        [swap(found[0], "head", 1)] + [swap(after(a, grad_w_out), "head", 1) for a in found[1:]]
        for found in parts
    ]

    def turned_back(i, s):
        return lax.rem(i + half * s[0], groups)

    def in_cut(a, k):
        return (a, row_block(a.shape, GROUP, lambda i, s: jnp.clip(i - k * steps, 0, steps - 1)))

    (grad_in,) = call(
        functools.partial(k_in_back, steps),
        groups,
        [rows(hidden_in, turned_back), rows(out_grad, turned_back), full(gain_in)]
        + [in_cut(a, k) for k, found in enumerate(parts + others) for a in found],
        [out_rows(dim, F32, turned_back)],
        [],
        10**9,
        "in_back",
        place,
    )
    shape = (small_rows // head_count + tok_count, LANES)
    (quarter,) = call(
        functools.partial(k_quarter, piece_b), 1, [full(after(sum_b, grad_in))], [out_full(shape, F32)],
        [], 10**6, "quarter",
    )
    quarters = [(quarter, 0)]
    for mask in powers(head_count):
        quarters = quarters + [(swap(a, "head", mask), k | mask) for a, k in quarters]
    quarters = [a for a, _ in sorted(quarters, key=lambda item: item[1])]

    (grad_w_zx,) = call(
        k_unpack,
        1,
        [full(mine_a), full(other_a), full(sum_b)],
        [out_full((dim, 2, real), F32)],
        [],
        10**6,
        "unpack",
        place,
    )
    grad_w_bc, grad_w_dt, grad_taps, grad_bias, grad_alog, grad_skip, grad_norm, own_taps, own_gain = call(
        k_small,
        1,
        [full(a) for a in quarters],
        [
            out_full((dim, 2 * N), F32), out_full((heads, dim), F32), out_full((KCONV + 1, 2 * N), F32),
            out_full((1, heads), F32), out_full((1, heads), F32), out_full((1, heads), F32),
            out_full((1, dim), F32), out_full((KCONV + 1, real), F32), out_full((1, real), F32),
        ],
        [pltpu.VMEM((small_rows, LANES), F32)],
        10**6,
        "small",
        place,
    )

    return (
        block_out,
        grad_in,
        grad_norm[0],
        grad_w_zx,
        grad_w_bc,
        grad_w_dt.T,
        grad_bias[0],
        grad_alog[0],
        own_taps,
        grad_taps,
        grad_skip[0],
        own_gain[0],
        grad_w_out[:real],
    )


def solution(mesh):
    return jax.shard_map(
        on_device,
        mesh=mesh,
        in_specs=(
            P("tok", None), P(), P(None, None, "head"), P(), P(), P(), P(), P(None, "head"), P(), P(),
            P("head"), P("head", None), P("tok", None), P("tok"), P("tok"),
        ),
        out_specs=(
            P("tok", None), P("tok", None), P(), P(None, None, "head"), P(), P(), P(), P(),
            P(None, "head"), P(), P(), P("head"), P("head", None),
        ),
        check_vma=False,
    )
```

```python
import functools
import math

import jax
import jax.numpy as jnp
from jax import lax
from jax.experimental import pallas as pl
from jax.experimental.pallas import tpu as pltpu
from jax.sharding import PartitionSpec as P

P_SIZE = 64
N = 128
KCONV = 4
GROUP = 256
CHUNK = 128
LANES = 128
PARTS = GROUP // CHUNK
EPS = 1e-05
VMEM_LIMIT = 10 * 1024 * 1024
F32 = jnp.float32
BF16 = jnp.bfloat16


def mm(a, b, ca=1, cb=0):
    return lax.dot_general(a, b, (((ca,), (cb,)), ((), ())), preferred_element_type=F32)


def iota(shape, dim):
    return lax.broadcasted_iota(jnp.int32, shape, dim)


def spread(cols, width):
    rows = cols.shape[0]
    low = iota((rows, LANES), 1) < P_SIZE
    tiles = [
        jnp.where(low, cols[:, 2 * p : 2 * p + 1], cols[:, 2 * p + 1 : 2 * p + 2])
        for p in range(width // LANES)
    ]
    return jnp.concatenate(tiles, axis=1)


def gather_heads(width):
    return (iota((width, LANES), 0) // P_SIZE == iota((width, LANES), 1)).astype(BF16)


def fold_rows(value):
    rows, width = value.shape
    return value.reshape(rows // 8, 8, width).sum(axis=0)


def tri(kind):
    row, col = iota((CHUNK, CHUNK), 0), iota((CHUNK, CHUNK), 1)
    return {"le": col <= row, "ge": col >= row, "lt": col < row}[kind]


def pair_rows(tile):
    low = iota(tile.shape, 1) < P_SIZE
    zero = jnp.zeros_like(tile)
    return jnp.concatenate([jnp.where(low, tile, zero), jnp.where(low, zero, tile)], axis=0)


def split2(value):
    high = value.astype(BF16)
    return high, (value - high.astype(F32)).astype(BF16)


def split3(value):
    high, rest = split2(value)
    return high, rest, (value - high.astype(F32) - rest.astype(F32)).astype(BF16)


def mm_left(a, b, ca=1, cb=0):
    high, low = split2(a)
    return mm(high, b, ca, cb) + mm(low, b, ca, cb)


def mm_right(a, b, ca=1, cb=0):
    high, low = split2(b)
    return mm(a, high, ca, cb) + mm(a, low, ca, cb)


def mm_both(a, b, ca=1, cb=0):
    ah, al = split2(a)
    bh, bl = split2(b)
    return mm(ah, bh, ca, cb) + mm(al, bh, ca, cb) + mm(ah, bl, ca, cb)


def stacked(value):
    return jnp.concatenate(
        [value[:, c : c + LANES] for c in range(0, value.shape[1], LANES)], axis=0
    )


def tree(terms):
    while len(terms) > 1:
        terms = [terms[k] + terms[k + 1] for k in range(0, len(terms), 2)]
    return terms[0]


def rms_inv(u):
    return lax.rsqrt(jnp.mean(u * u, axis=1, keepdims=True) + EPS)


def k_front(
    first, valid, hid, rim, gain, w_x, w_bc, w_dt, hp, cx, cb,
    h_o, v_o, pre_o, prev_o, lead_o, xs_o, bc_o, dt_o, cum_o, ent_o, pd_o, fin_o,
    vbuf, state, decay,
):
    g = pl.program_id(0)
    width = w_x.shape[1]

    def normed(block):
        u = block.astype(F32)
        return (u * rms_inv(u) * gain[...]).astype(BF16)

    @pl.when(g == 0)
    def _():
        hr = normed(rim[...])
        vbuf[0:8, :width] = mm(hr, w_x[...])[8:16]
        vbuf[0:8, width:] = mm(hr, w_bc[...])[8:16]
        state[...] = jnp.zeros_like(state)
        decay[...] = jnp.ones_like(decay)

    keep = 1.0 - first[g].astype(F32)
    vbuf[0:8, :] = vbuf[0:8, :] * keep
    state[...] = state[...] * keep
    decay[...] = decay[...] * keep
    h = normed(hid[...])
    h_o[...] = h
    raw = mm(h, w_dt[...]) + hp[0:1, :]
    pre_o[...] = raw
    vbuf[8:, :width] = mm(h, w_x[...])
    vbuf[8:, width:] = mm(h, w_bc[...])
    v_o[...] = vbuf[8:, :]
    taps = jnp.concatenate([cx[...], cb[...]], axis=1)
    conv = taps[KCONV : KCONV + 1, :] + taps[0:1, :] * vbuf[5 : 5 + GROUP, :]
    for k in range(1, KCONV):
        conv = conv + taps[k : k + 1, :] * vbuf[5 + k : 5 + k + GROUP, :]
    prev_o[0] = vbuf[0:8, :]
    lead_o[0] = conv[0:16, :]
    act = (conv * jax.nn.sigmoid(conv)).astype(BF16)
    xs_o[...] = act[:, :width]
    bc_o[...] = act[:, width:]
    vbuf[0:8, :] = vbuf[GROUP : GROUP + 8, :]
    live = iota((GROUP, LANES), 0) < valid[g]
    soft = jnp.maximum(raw, 0.0) + jnp.log1p(jnp.exp(-jnp.abs(raw)))
    dt = jnp.where(live, soft, 0.0)
    dt_o[...] = dt
    ld = dt * -jnp.exp(hp[1:2, :])
    lower = tri("le").astype(BF16)
    lower = jnp.concatenate([lower] * 3, axis=1)
    for c in range(PARTS):
        rows = slice(c * CHUNK, (c + 1) * CHUNK)
        cum = mm(lower, jnp.concatenate(split3(ld[rows]), axis=0))
        cum_o[rows, :] = cum
        end = cum[CHUNK - 1 : CHUNK, :]
        factor = dt[rows] * jnp.exp(end - cum)
        ent_o[c] = state[...]
        pd_o[c] = decay[0:1]
        xd = act[rows, :width].astype(F32) * spread(factor, width)
        new = mm_right(act[rows, width : width + N], xd, 0, 0)
        ec = spread(jnp.exp(end), width)
        state[...] = state[...] * ec + new
        decay[...] = decay[...] * ec

    @pl.when(g == pl.num_programs(0) - 1)
    def _():
        fin_o[0:N, :] = state[...]
        fin_o[N:, :] = decay[...]


def k_proj(h, og, w_z, w_out, silu_o, slope_o, gyn_o):
    z = mm(h[...], w_z[...])
    sig = jax.nn.sigmoid(z)
    silu_o[...] = z * sig
    slope_o[...] = sig * (1.0 + z * (1.0 - sig))
    gyn_o[...] = mm(og[...], w_out[...], 1, 1)


def k_within(xs, bc, dt, cum, y_o, ecum_o):
    width = xs.shape[1]
    mask = tri("le")
    for c in range(PARTS):
        rows = slice(c * CHUNK, (c + 1) * CHUNK)
        scores = mm(bc[rows, N:], bc[rows, :N], 1, 1)
        a = cum[rows, :]
        ecum_o[rows, :] = spread(jnp.exp(a), width)
        b = jnp.transpose(a - jnp.log(dt[rows, :]))
        for p in range(width // LANES):
            lanes = slice(p * LANES, (p + 1) * LANES)
            weights = []
            for h in (2 * p, 2 * p + 1):
                gap = a[:, h : h + 1] - b[h : h + 1, :]
                weights.append(jnp.where(mask, jnp.exp(gap), 0.0) * scores)
            y_o[rows, lanes] = mm_left(jnp.concatenate(weights, axis=1), pair_rows(xs[rows, lanes]))


def k_gate(ent, pd, prev, bc, ecum, yw, xs, silu, gyn, gain, hp, mix_o, ent_o, sums_o):
    width = xs.shape[1]
    skip = spread(hp[2:3, :], width)
    for c in range(PARTS):
        rows = slice(c * CHUNK, (c + 1) * CHUNK)
        entry = ent[c] + pd[c] * prev[0:N, :]
        ent_o[c] = entry
        across = mm_right(bc[rows, N:], entry) * ecum[rows, :]
        mix_o[rows, :] = yw[rows, :] + across + skip * xs[rows, :].astype(F32)
    gated = mix_o[...] * silu[...]
    square = jnp.sum(gated * gated, axis=1, keepdims=True)
    inner = jnp.sum(gyn[...] * gain[...] * gated, axis=1, keepdims=True)
    lane = iota((GROUP, LANES), 1)
    both = jnp.where(lane == 0, square, inner)
    sums_o[...] = jnp.transpose(both)[0:2, :]


def k_gate_back(
    total, count, first, mix, silu, slope, gyn, gain, xs, bc, ecum, *rest,
):
    sums = rest[:count]
    yn_o, g_o, gz_o, ds_o, qd_o, again_o, askip_o, fin_o, state, decay = rest[count:]
    i = pl.program_id(0)
    g = pl.num_programs(0) - 1 - i
    width = xs.shape[1]

    @pl.when(i == 0)
    def _():
        state[...] = jnp.zeros_like(state)
        decay[...] = jnp.ones_like(decay)
        again_o[...] = jnp.zeros_like(again_o)
        askip_o[...] = jnp.zeros_like(askip_o)

    rows2 = tree([part[...] for part in sums])
    both = jnp.transpose(jnp.concatenate([rows2, jnp.zeros((LANES - 2, GROUP), F32)], axis=0))
    inv = lax.rsqrt(both[:, 0:1] / total + EPS)
    inner = both[:, 1:2] / total
    silu = silu[...]
    mixer = mix[...]
    gated = mixer * silu
    scaled = gated * inv
    gy = gyn[...]
    gn = gain[...]
    yn_o[...] = (scaled * gn).astype(BF16)
    again_o[...] += fold_rows(gy * scaled)
    gg = inv * gn * gy - gated * (inv * inv * inv * inner)
    gm = (gg * silu).astype(BF16)
    g_o[...] = gm
    gz_o[...] = (gg * mixer * slope[...]).astype(BF16)
    gmf = gm.astype(F32)
    askip_o[...] += fold_rows(gmf * xs[...].astype(F32))
    for c in reversed(range(PARTS)):
        rows = slice(c * CHUNK, (c + 1) * CHUNK)
        ds_o[c] = state[...]
        qd_o[c] = decay[0:1]
        new = mm_right(bc[rows, N:], gmf[rows] * ecum[rows, :], 0, 0)
        ec = ecum[(c + 1) * CHUNK - 1 : (c + 1) * CHUNK, :]
        state[...] = state[...] * ec + new
        decay[...] = decay[...] * ec
    keep = 1.0 - first[g].astype(F32)
    state[...] = state[...] * keep
    decay[...] = decay[...] * keep

    @pl.when(i == pl.num_programs(0) - 1)
    def _():
        fin_o[0:N, :] = state[...]
        fin_o[N:, :] = decay[...]


def k_weights(place, yn, og, h, gz, keep_o, send_o, acc_z, acc_out):
    i = pl.program_id(0)

    @pl.when(i == 0)
    def _():
        acc_z[...] = jnp.zeros_like(acc_z)
        acc_out[...] = jnp.zeros_like(acc_out)

    acc_z[...] += mm(h[...], gz[...], 0, 0)
    acc_out[...] += mm(yn[...], og[...], 0, 0)

    @pl.when(i == pl.num_programs(0) - 1)
    def _():
        count = keep_o.shape[0]
        rz, ro = acc_z.shape[0] // (2 * count), acc_out.shape[0] // (2 * count)
        side = place[3] % 2
        for k in range(count):
            for out, at in ((keep_o, 2 * k + side), (send_o, 2 * k + 1 - side)):
                out[k] = jnp.concatenate(
                    [
                        stacked(acc_z[pl.ds(pl.multiple_of(at * rz, 8), rz), :]),
                        stacked(acc_out[pl.ds(pl.multiple_of(at * ro, 8), ro), :]),
                    ],
                    axis=0,
                )


def k_pair(place, keep, arrived, *outs):
    for k, out in enumerate(outs):
        at = (place[3] // 2) ^ k
        out[...] = (keep[at] + arrived[at]).astype(BF16)


def k_join(place, *refs):
    out = refs[-1]
    for k, part in enumerate(refs[:-1]):
        out[(place[3] // 2) ^ k] = part[...]


def k_within_back(
    xs, bc, g, dt, cum, mix, ent, hp,
    dxw_o, dbc_o, rq_o, qw_o,
):
    width = xs.shape[1]
    mask = tri("ge")
    heads = gather_heads(width)
    skip = spread(hp[2:3, :], width)
    for c in range(PARTS):
        rows = slice(c * CHUNK, (c + 1) * CHUNK)
        bw, cr = bc[rows, :N], bc[rows, N:]
        scores = mm(bw, cr, 1, 1)
        a = cum[rows, :]
        b = a - jnp.log(dt[rows, :])
        at = jnp.transpose(a)
        dscore = jnp.zeros((CHUNK, CHUNK), F32)
        for p in range(width // LANES):
            lanes = slice(p * LANES, (p + 1) * LANES)
            decays = [
                jnp.where(mask, jnp.exp(at[h : h + 1, :] - b[:, h : h + 1]), 0.0)
                for h in (2 * p, 2 * p + 1)
            ]
            gt = g[rows, lanes]
            pairs = mm(pair_rows(xs[rows, lanes]), gt, 1, 1)
            dscore = dscore + pairs[:CHUNK] * decays[0] + pairs[CHUNK:] * decays[1]
            weights = jnp.concatenate([d * scores for d in decays], axis=1)
            dxw_o[rows, lanes] = mm_left(weights, pair_rows(gt))
        high, low = split2(dscore)
        gf = g[rows, :].astype(F32)
        xf = xs[rows, :].astype(F32)
        ge = gf * spread(jnp.exp(a), width)
        dbc_o[rows, :N] = mm(high, cr) + mm(low, cr)
        dbc_o[rows, N:] = mm(high, bw, 0, 0) + mm(low, bw, 0, 0) + mm_both(ge, ent[c], 1, 1)
        row_part = mm_left(gf * (mix[rows, :] - skip * xf), heads)
        col_part = mm_left(xf * dxw_o[rows, :], heads)
        rq_o[rows, :] = row_part - col_part
        qw_o[rows, :] = col_part


def silu_slope(value):
    sig = jax.nn.sigmoid(value)
    return sig * (1.0 + value * (1.0 - sig))


def k_rim(first, xs, bc, g, dt, cum, cend, dxw, dbc, cv, ds, qd, endg, hp, out, lead_o):
    i = pl.program_id(0)
    width = xs.shape[1]
    d_state = ds[0] + qd[0] * endg[0:N, :]
    factor = spread(dt[...] * jnp.exp(cend[7:8, :] - cum[...]), width)
    skip = spread(hp[2:3, :], width)
    xd = xs[...].astype(F32) * factor
    gx = dxw[...] + factor * mm_right(bc[:, :N], d_state) + g[...].astype(F32) * skip
    gb = dbc[:, :N] + mm_both(xd, d_state, 1, 1)
    slope = silu_slope(cv[0]) * (1.0 - first[i].astype(F32))
    out[0, :, :width] = gx * slope[:, :width]
    out[0, :, width : width + N] = gb * slope[:, width : width + N]
    out[0, :, width + N :] = dbc[:, N:] * slope[:, width + N :]

    @pl.when(i == 0)
    def _():
        lead_o[...] = out[0, 0:8, :]


def k_back(final, slots, place, *refs):
    (
        valid, h, xs, bc, g, pre, dt, cum, v, vprev, dxw, dbc, rq, qw, ent, ds, qd, endg, rims, cx, cb, hp,
    ) = refs[:22]
    if final:
        rim_in, acc_gain, acc_skip = refs[22:25]
        gx_o, gbc_o, gpre_o = refs[33:36]
        acc_x, acc_bc, acc_dt, acc_taps, acc_heads = refs[36:41]
        grads_o, keep_o, send_o, gbuf, vbuf, small_o = refs[41:]
    else:
        gx_o, gbc_o, gpre_o, acc_x, acc_bc, acc_dt, acc_taps, acc_heads, gbuf, vbuf = refs[22:]
    i = pl.program_id(0)
    last = pl.num_programs(0) - 1
    group = i + pl.num_programs(0) if final else i
    width = xs.shape[1]
    heads = gather_heads(width)
    skip = spread(hp[2:3, :], width)
    rate = -jnp.exp(hp[1:2, :])

    if not final:

        @pl.when(i == 0)
        def _():
            for ref in (acc_x, acc_bc, acc_dt, acc_taps, acc_heads):
                ref[...] = jnp.zeros_like(ref)

    upper, below = tri("ge").astype(BF16), tri("lt").astype(BF16)
    both = jnp.concatenate([upper, upper, below, below], axis=1)
    taps = jnp.concatenate([cx[...], cb[...]], axis=1)
    vbuf[0:8, :] = vprev[0]
    vbuf[8:, :] = v[...]
    for c in range(PARTS):
        rows = slice(c * CHUNK, (c + 1) * CHUNK)
        d_state = ds[c] + qd[c] * endg[0:N, :]
        d_high, d_low = split2(d_state)
        a = cum[rows, :]
        end = a[CHUNK - 1 : CHUNK, :]
        factor = spread(dt[rows, :] * jnp.exp(end - a), width)
        xf = xs[rows, :].astype(F32)
        bw = bc[rows, :N]
        dxs = factor * (mm(bw, d_high) + mm(bw, d_low))
        x_high, x_low = split2(xf * factor)
        gb = dbc[rows, :N] + (mm(x_high, d_high, 1, 1) + mm(x_low, d_high, 1, 1) + mm(x_high, d_low, 1, 1))
        gx = dxw[rows, :] + dxs + g[rows, :].astype(F32) * skip
        conv = taps[KCONV : KCONV + 1, :]
        for k in range(KCONV):
            start = 5 + k + c * CHUNK
            conv = conv + taps[k : k + 1, :] * vbuf[start : start + CHUNK, :]
        slope = silu_slope(conv)
        gbuf[rows, :width] = gx * slope[:, :width]
        gbuf[rows, width : width + N] = gb * slope[:, width : width + N]
        gbuf[rows, width + N :] = dbc[rows, N:] * slope[:, width + N :]
        qs = mm_left(xf * dxs, heads)
        carried = mm_left(fold_rows(d_state * ent[c]), heads)
        ends = jnp.sum(carried, axis=0, keepdims=True) * jnp.exp(end)
        g_ld = mm(both, jnp.concatenate(split2(rq[rows, :]) + split2(qs), axis=0)) + ends
        step = dt[rows, :]
        direct = jnp.where(step > 0.0, (qw[rows, :] + qs) / jnp.where(step > 0.0, step, 1.0), 0.0)
        live = iota((CHUNK, LANES), 0) + c * CHUNK < valid[group]
        own = iota((CHUNK, LANES), 1) < width // P_SIZE
        g_pre = jnp.where(
            live & own, (direct + g_ld * rate) * jax.nn.sigmoid(pre[rows, :]), 0.0
        )
        acc_heads[0:8, :] += fold_rows(g_pre)
        acc_heads[8:16, :] += fold_rows(g_ld * step * rate)
        low = g_pre.astype(BF16)
        gpre_o[rows, :] = low
        acc_dt[...] += mm(pltpu.roll(low.astype(F32), place[1], 1).astype(BF16), h[rows, :], 0, 0)[0 : acc_dt.shape[0]]

    gbuf[GROUP:, :] = rims[0, 0:8, :]
    if final:

        @pl.when(i == last)
        def _():
            gbuf[GROUP:, :] = rim_in[0:8, :]

    vv = v[...]
    gv = jnp.zeros_like(vv)
    for k in range(KCONV):
        shifted = gbuf[KCONV - 1 - k : KCONV - 1 - k + GROUP, :]
        gv = gv + taps[k : k + 1, :] * shifted
        acc_taps[8 * k : 8 * k + 8, :] += fold_rows(vv * shifted)
    acc_taps[8 * KCONV :, :] += fold_rows(gbuf[0:GROUP, :])
    gx_low = gv[:, :width].astype(BF16)
    bc_high, bc_low = split2(gv[:, width:])
    gx_o[...] = gx_low
    gbc_o[:, : 2 * N] = bc_high
    gbc_o[:, 2 * N :] = bc_low
    hh = h[...]
    acc_x[...] += mm(hh, gx_low, 0, 0)
    acc_bc[...] += mm(hh, bc_high, 0, 0) + mm(hh, bc_low, 0, 0)
    if not final:
        return

    @pl.when(i == last)
    def _():
        count = grads_o.shape[0]
        rx = acc_x.shape[0] // count
        for k in range(count):
            grads_o[k] = stacked(acc_x[k * rx : (k + 1) * rx, :]).astype(BF16)
        dim = acc_bc.shape[0]
        at = 0

        def put(value):
            nonlocal at
            small_o[at : at + value.shape[0], :] = value
            at += value.shape[0]

        put(acc_bc[:, :LANES])
        put(acc_bc[:, LANES:])
        count, each, rest = slots
        if at < count * each:
            put(jnp.zeros((count * each - at, LANES), F32))
        put(stacked(acc_dt[...]))

        def line(value):
            return jnp.sum(value, axis=0, keepdims=True)

        def lane_home(value):
            return pltpu.roll(jnp.broadcast_to(value, (8, LANES)), place[1], 1)[0:1]

        own = iota((1, LANES), 1) < width // P_SIZE
        taps_sum = [line(acc_taps[8 * k : 8 * k + 8, :]) for k in range(KCONV + 1)]
        skips = mm_left(acc_skip[...], heads)
        head_rows = [
            lane_home(jnp.where(own, line(x), 0.0))
            for x in (acc_heads[0:8, :], acc_heads[8:16, :], skips)
        ]
        put(jnp.concatenate([t[:, width : width + N] for t in taps_sum] + head_rows, axis=0))
        spare = jnp.zeros((8 - KCONV - 1, LANES), F32)
        put(jnp.concatenate([t[:, width + N :] for t in taps_sum] + [spare], axis=0))
        small_o[at:, :] = jnp.zeros_like(small_o[at:, :])
        gains = line(acc_gain[...])
        tiles = width // LANES
        own_rows = jnp.concatenate(
            [
                jnp.concatenate(
                    [t[:, k * LANES : (k + 1) * LANES] for t in taps_sum]
                    + [gains[:, k * LANES : (k + 1) * LANES], spare[0:2]],
                    axis=0,
                )
                for k in range(tiles)
            ],
            axis=0,
        )
        small_o[pl.ds(pl.multiple_of(at + place[2] * (8 * tiles), 8), 8 * tiles), :] = own_rows
        for k in range(count // 2):
            for out, side in ((keep_o, place[0]), (send_o, 1 - place[0])):
                slot = side * (count // 2) + k
                to = k * (each + rest)
                out[to : to + each, :] = small_o[pl.ds(pl.multiple_of(slot * each, 8), each), :]
                start = pl.multiple_of(count * each + slot * rest, 8)
                out[to + each : to + each + rest, :] = small_o[pl.ds(start, rest), :]


def input_grad(hid, gz, gx, gbc, gpre, w_z, w_x, w_bc, w_dt):
    gh = (
        mm(gpre[...], w_dt[...], 1, 1)
        + mm(gz[...], w_z[...], 1, 1)
        + mm(gx[...], w_x[...], 1, 1)
        + mm(gbc[:, : 2 * N], w_bc[...], 1, 1)
        + mm(gbc[:, 2 * N :], w_bc[...], 1, 1)
    )
    u = hid[...].astype(F32)
    return gh, fold_rows(gh * (u * rms_inv(u)))


def k_input(begins, own, ends, place, *refs):
    refs, (out, norm_o, acc) = refs[:-3], refs[-3:]
    i = pl.program_id(0)

    @pl.when(i == 0)
    def _():
        acc[...] = jnp.zeros_like(acc) if begins else refs[-1][...]

    gh, norm = input_grad(*refs[:9])
    out[...] = (gh + refs[9][...]).astype(BF16) if own else gh
    acc[...] += norm

    @pl.when(i == pl.num_programs(0) - 1)
    def _():
        if ends:
            rows = acc.shape[1] // LANES
            norm_o[0:rows, :] = stacked(jnp.sum(acc[...], axis=0, keepdims=True))
            norm_o[rows:, :] = jnp.zeros((8 - rows, LANES), F32)
        else:
            norm_o[...] = acc[...]


def k_reduce(*refs):
    out = refs[-1]
    out[...] = tree([part[...].astype(F32) for part in refs[:-1]]).astype(BF16)


def k_halve(mask, place, kept, arrived, keep_o, send_o):
    rows = keep_o.shape[0]
    upper = (place[2] // mask) % 2
    for out, at in ((keep_o, upper * rows), (send_o, (1 - upper) * rows)):
        at = pl.multiple_of(at, 8)
        out[...] = kept[pl.ds(at, rows), :] + arrived[pl.ds(at, rows), :]


def k_pieces(slots, kept, arrived, norm, large, out):
    count = out.shape[0]
    _, each, rest = slots
    rows = each + rest
    cut = large.shape[1]
    spare = jnp.zeros((7, LANES), F32)
    for k in range(count):
        own = slice(k * rows, (k + 1) * rows)
        value = kept[own, :] + arrived[own, :]
        line = norm[k : k + 1, :] if k < 8 else spare[0:1]
        small = jnp.concatenate([value[each:], line, spare], axis=0)
        out[k, 0:cut, :] = large[k]
        out[k, cut : cut + each, :] = value[:each].astype(BF16)
        out[k, cut + each :, :] = jnp.concatenate(split2(small), axis=0)


def k_reduce_both(cut, parts, out):
    count = out.shape[0]
    rows = (out.shape[1] - cut) // 2
    terms = [parts[k].astype(F32) for k in range(count)]
    small = tree([term[cut : cut + rows] + term[cut + rows :] for term in terms])
    large = tree([term[:cut] for term in terms]).astype(BF16)
    joined = jnp.concatenate([large, *split2(small)], axis=0)
    for k in range(count):
        out[k] = joined


def k_tick(value, out):
    out[...] = value[0, 0:16, :]


def k_quarter(cut, slots, parts, out):
    count = parts.shape[0]
    _, each, rest = slots
    rows = each + rest
    for k in range(count):
        value = parts[k, cut:, :].astype(F32)
        small = value[each : each + rest + 8] + value[each + rest + 8 :]
        out[k * rows : k * rows + each, :] = value[:each]
        out[k * rows + each : (k + 1) * rows, :] = small[:rest]
        out[count * rows + k : count * rows + k + 1, :] = small[rest : rest + 1]


def unstack(value, rows):
    return jnp.concatenate(
        [value[k : k + rows, :] for k in range(0, value.shape[0], rows)], axis=1
    )


def k_unpack_out(place, mine, other, w_out_o):
    count = 2 * mine.shape[0]
    ro = w_out_o.shape[0] // count
    rows = ro * w_out_o.shape[1] // LANES
    side = place[3] % 2
    for k in range(count // 2):
        for part, at in ((mine, 2 * k + side), (other, 2 * k + 1 - side)):
            piece = part[k].astype(F32)
            w_out_o[pl.ds(pl.multiple_of(at * ro, 8), ro), :] = unstack(piece[piece.shape[0] - rows :], ro)


def k_unpack(place, mine, other, b, w_zx_o):
    count = b.shape[0]
    dim, _, real = w_zx_o.shape
    rz = dim // count
    cut = rz * -(-real // LANES)
    side = place[3] % 2
    for k in range(count // 2):
        for part, at in ((mine, 2 * k + side), (other, 2 * k + 1 - side)):
            piece = part[k].astype(F32)
            w_zx_o[pl.ds(at * rz, rz), 0, :] = unstack(piece[0:cut], rz)[:, :real]
    for k in range(count):
        own = unstack(b[k, 0:cut, :].astype(F32), rz)[:, :real]
        w_zx_o[k * rz : (k + 1) * rz, 1, :] = own


def k_small(slots, place, *refs):
    count = len(refs) - 10
    w_bc_o, w_dt_o, bc_taps_o, bias_o, alog_o, skip_o, norm_o, taps_o, gain_o, buf = refs[count:]
    total, each, rest = slots
    steps = total // count
    norms = []
    for k in range(count):
        from_head, at = place[2] ^ k, 0
        for mask in powers(count):
            at = 2 * at + (from_head // mask) % 2
        for t in range(steps):
            slot = at * steps + t
            value = refs[k][t * (each + rest) : (t + 1) * (each + rest), :]
            buf[pl.ds(pl.multiple_of(slot * each, 8), each), :] = value[:each]
            buf[pl.ds(pl.multiple_of(total * each + slot * rest, 8), rest), :] = value[each:]
        norms.append(refs[k][steps * (each + rest) : steps * (each + rest) + 8, :])
    norm = tree(norms)
    dim = w_bc_o.shape[0]
    for k in range(dim // LANES):
        norm_o[:, k * LANES : (k + 1) * LANES] = norm[k : k + 1, :]
    w_bc_o[:, :LANES] = buf[0:dim, :]
    w_bc_o[:, LANES:] = buf[dim : 2 * dim, :]
    at = total * each
    heads = w_dt_o.shape[0]
    w_dt_o[...] = unstack(buf[at : at + heads * dim // LANES, :], heads)
    at += heads * dim // LANES
    bc_taps_o[...] = unstack(buf[at : at + 16, :], 8)[0 : KCONV + 1]
    for k, out in enumerate((bias_o, alog_o, skip_o)):
        out[...] = buf[at + KCONV + 1 + k : at + KCONV + 2 + k, 0 : out.shape[1]]
    real = taps_o.shape[1]
    tiles = -(-real // LANES)
    own = buf[pl.ds(pl.multiple_of(at + 16 + place[2] * (8 * tiles), 8), 8 * tiles), :]
    own = unstack(own, 8)[:, 0:real]
    taps_o[...] = own[0 : KCONV + 1]
    gain_o[...] = own[KCONV + 1 : KCONV + 2]


def k_out(hid, *refs):
    count = (len(refs) - 1) // 2
    out = refs[-1]
    total = tree([mm(refs[k][...], refs[count + k][...]) for k in range(count)])
    out[...] = (hid[...].astype(F32) + total).astype(BF16)


def k_in_back(steps, place, hid, og, gain, *refs):
    i = pl.program_id(0)
    cuts = pl.num_programs(0) // steps
    out = refs[-1]
    count = (len(refs) - 1) // cuts

    def finish(parts):
        gh = tree([part[...].astype(F32) for part in parts])
        u = hid[...].astype(F32)
        inv = rms_inv(u)
        scaled = gh * gain[...]
        dot = jnp.sum(scaled * u, axis=1, keepdims=True) / u.shape[1]
        out[...] = inv * scaled - u * (inv * inv * inv * dot) + og[...].astype(F32)

    for k in range(cuts):
        pl.when(i // steps == k)(functools.partial(finish, refs[k * count : (k + 1) * count]))


def row_block(shape, rows, at=None):
    at = at or (lambda i, *s: i)
    rest = tuple(shape[1:])
    return pl.BlockSpec((rows,) + rest, lambda i, *s: (at(i, *s),) + (0,) * len(rest))


def whole(shape):
    return pl.BlockSpec(tuple(shape), lambda i, *s: (0,) * len(shape))


SMEM = pl.BlockSpec(memory_space=pltpu.SMEM)
VMEM = pl.BlockSpec(memory_space=pltpu.VMEM)


class Kept:
    def __init__(self, rows, at=None):
        self.rows = rows
        self.at = at or (lambda i, *s: i)

    def view(self, ref, i, scalars):
        start = pl.multiple_of(self.at(i, *scalars) * self.rows, self.rows)
        return ref.at[pl.ds(start, self.rows)]


def call(kernel, steps, ins, outs, scratch, flops, name, place=None, weight=1, alias=()):
    moved = sum(a.size * a.dtype.itemsize for a, _ in ins)
    for shape, dtype, _ in outs:
        moved += functools.reduce(lambda x, y: x * y, shape) * jnp.dtype(dtype).itemsize
    scalars = [] if place is None else [place]
    specs = [spec for _, spec in ins] + [spec for _, _, spec in outs]
    first = len(scalars)

    def body(*refs):
        i = pl.program_id(0)
        seen = list(refs)
        for k, spec in enumerate(specs):
            if isinstance(spec, Kept):
                seen[first + k] = spec.view(refs[first + k], i, refs[:first])
        kernel(*seen)

    places = [
        pl.BlockSpec(memory_space=pltpu.VMEM) if isinstance(spec, Kept) else spec for spec in specs
    ]
    held = 4 * 1024 * 1024
    for (shape, dtype), spec in zip(
        [(a.shape, a.dtype) for a, _ in ins] + [(shape, dtype) for shape, dtype, _ in outs], places
    ):
        if spec.block_shape is not None:
            padded = list(spec.block_shape)
            padded[-1] = -(-padded[-1] // LANES) * LANES
            held += 2 * math.prod(padded) * jnp.dtype(dtype).itemsize
    for buffer in scratch:
        held += math.prod(buffer.shape) * jnp.dtype(buffer.dtype).itemsize
    return pl.pallas_call(
        body,
        grid_spec=pltpu.PrefetchScalarGridSpec(
            num_scalar_prefetch=len(scalars),
            grid=(steps,),
            in_specs=places[: len(ins)],
            out_specs=places[len(ins) :],
            scratch_shapes=scratch,
        ),
        out_shape=[jax.ShapeDtypeStruct(s, d) for s, d, _ in outs],
        compiler_params=pltpu.CompilerParams(
            dimension_semantics=("arbitrary",), vmem_limit_bytes=max(VMEM_LIMIT, held)
        ),
        cost_estimate=pl.CostEstimate(
            flops=flops * weight, bytes_accessed=moved * weight, transcendentals=0
        ),
        input_output_aliases={first + k: j for k, j in alias},
        name=name,
    )(*scalars, *[a for a, _ in ins])


def swap(value, axis, mask):
    return lax.ppermute(value, axis, [(i, i ^ mask) for i in range(lax.axis_size(axis))])


def after(value, *others):
    return lax.optimization_barrier((value,) + others)[0]


def powers(count):
    return [1 << k for k in range(count.bit_length() - 1)]


def k_merge(mask, backward, first, place, *refs):
    total, other = refs[:2]
    before = None if first else refs[2]
    outs = refs[2 if first else 3 :]
    upper = (place[3] // mask) % 2 == 1
    later = jnp.logical_not(upper) if backward else upper

    def merge(early, late, out):
        scale = late[N : N + 1, :]
        out[0:N, :] = scale * early[0:N, :] + late[0:N, :]
        out[N:, :] = scale * early[N:, :]

    @pl.when(later)
    def _():
        if first:
            outs[0][...] = other[...]
        else:
            merge(other, before, outs[0])
        if len(outs) > 1:
            merge(other, total, outs[1])

    @pl.when(jnp.logical_not(later))
    def _():
        if first:
            outs[0][0:N, :] = jnp.zeros((N, total.shape[1]), F32)
            outs[0][N:, :] = jnp.ones((8, total.shape[1]), F32)
        else:
            outs[0][...] = before[...]
        if len(outs) > 1:
            merge(total, other, outs[1])


def carried_in(total, backward, place, beside=()):
    before, firsts = [], []
    shape = total.shape
    masks = powers(lax.axis_size("tok"))
    for mask in masks:
        other = swap(total, "tok", mask)
        ins = [total, other if before else after(other, *beside), *before]
        last = mask == masks[-1]
        found = call(
            functools.partial(k_merge, mask, backward, not before),
            1,
            [(a, whole(shape)) for a in ins],
            [(shape, F32, whole(shape))] * (1 if last else 2),
            [],
            10**6,
            "merge",
            place,
        )
        before, total = [found[0]], found[-1]
        firsts.append(found[0])
    return before[0], firsts[0]


def exchange(pieces, axis):
    return lax.all_to_all(pieces, axis, 0, 0, tiled=True)


def distances(value, axis, step):
    return [value] + [swap(value, axis, step * k) for k in range(1, lax.axis_size(axis) // step)]


def head_gathered(value):
    found = [value]
    masks = powers(lax.axis_size("head"))
    for mask in masks[1:] + masks[:1]:
        found = found + [swap(a, "head", mask) for a in found]
    return found


def on_device(
    hidden_in, norm_gain, w_zx, w_bc, w_dt, dt_bias, a_log, conv_x, conv_bc, d_skip, gate_gain,
    w_out, out_grad, group_first, group_valid,
):
    tokens, dim = hidden_in.shape
    real = w_zx.shape[2]
    own_heads = real // P_SIZE
    heads = w_dt.shape[1]
    groups = tokens // GROUP
    chunks = groups * PARTS
    width = -(-real // LANES) * LANES
    extra = width - real
    conv_width = width + 2 * N
    tok_count = lax.axis_size("tok")
    head_count = lax.axis_size("head")
    head_start = lax.axis_index("head") * own_heads

    def wide(a, dim_at, by=extra):
        return jnp.pad(a, [(0, by if k == dim_at else 0) for k in range(a.ndim)]) if by else a

    route = [(i - 1, i) for i in range(1, tok_count)]
    rim = lax.ppermute(hidden_in[tokens - 16 :], "tok", route)
    flat_zx = wide(w_zx, 2).reshape(dim, 2 * width)
    w_o = wide(w_out, 0)
    w_dt_here = wide(lax.dynamic_slice_in_dim(w_dt, head_start, own_heads, 1), 1, LANES - own_heads)
    per_head = jnp.stack([dt_bias, a_log, d_skip])
    per_head = lax.dynamic_slice_in_dim(per_head, head_start, own_heads, 1)
    per_head = jnp.pad(per_head, ((0, 5), (0, LANES - own_heads)))
    cx = wide(conv_x, 1)
    gain_in = norm_gain[None, :]
    gain_gate = wide(gate_gain, 0)[None, :]
    at_head = lax.axis_index("head")
    place = jnp.stack([at_head & 1, head_start, at_head, lax.axis_index("tok")]).astype(jnp.int32)
    hidden_in, place, flat_zx, w_o, w_dt_here, per_head, cx, gain_in, gain_gate = lax.optimization_barrier(
        (hidden_in, place, flat_zx, w_o, w_dt_here, per_head, cx, gain_in, gain_gate)
    )
    part_z, part_x = [
        (flat_zx, pl.BlockSpec((dim, width), lambda i, *s, side=side: (0, side))) for side in range(2)
    ]
    w_outs = head_gathered(w_o)

    def rows(a, at=None):
        return (a, row_block(a.shape, GROUP, at))

    def full(a):
        return (a, whole(a.shape))

    def kept(a, at=None):
        return (a, Kept(GROUP, at))

    def per_chunk(a, at=None):
        return (a, Kept(PARTS, at))

    def out_rows(cols, dtype, at=None):
        return ((tokens, cols), dtype, row_block((tokens, cols), GROUP, at))

    def out_kept(cols, dtype, at=None):
        return ((tokens, cols), dtype, Kept(GROUP, at))

    def out_full(shape, dtype):
        return (shape, dtype, whole(shape))

    def out_chunk(shape, dtype, at=None):
        return ((chunks,) + shape, dtype, Kept(PARTS, at))

    carry = (N + 8, width)
    h, v, pre, vprev, cvlead, xs, bc, dt, cum, ent, pd, fin = call(
        k_front,
        groups,
        [
            (group_first, SMEM), (group_valid, SMEM), rows(hidden_in), full(rim), full(gain_in),
            part_x, full(w_bc), full(w_dt_here), full(per_head), full(cx), full(conv_bc),
        ],
        [
            out_kept(dim, BF16), out_kept(conv_width, F32), out_kept(LANES, F32),
            ((groups, 8, conv_width), F32, Kept(1)), ((groups, 16, conv_width), F32, Kept(1)), out_kept(width, BF16), out_kept(2 * N, BF16),
            out_kept(LANES, F32), out_kept(LANES, F32), out_chunk((N, width), F32),
            out_chunk((1, width), F32), out_full(carry, F32),
        ],
        [
            pltpu.VMEM((GROUP + 8, conv_width), F32), pltpu.VMEM((N, width), F32),
            pltpu.VMEM((8, width), F32),
        ],
        4 * 10**9,
        "front",
    )
    prev, _ = carried_in(fin, False, place)
    silu, slope, gyn = call(
        k_proj,
        groups,
        [kept(h), rows(after(out_grad, fin)), part_z, full(w_o)],
        [out_kept(width, F32)] * 3,
        [],
        5 * 10**9,
        "proj",
    )
    yw, ecum = call(
        k_within,
        groups,
        [kept(xs), kept(bc), kept(dt), kept(cum)],
        [out_kept(width, F32)] * 2,
        [],
        5 * 10**9,
        "within",
    )
    mix, entry, sums = call(
        k_gate,
        groups,
        [
            per_chunk(ent), per_chunk(pd), full(after(prev, *w_outs)), kept(bc), kept(ecum), kept(yw), kept(xs),
            kept(silu), kept(gyn), full(gain_gate), full(per_head),
        ],
        [
            out_kept(width, F32), out_chunk((N, width), F32),
            ((2, tokens), F32, pl.BlockSpec((2, GROUP), lambda i: (0, i))),
        ],
        [],
        3 * 10**9,
        "gate",
    )
    sums = [sums] + [swap(sums, "head", mask) for mask in range(1, head_count)]

    def back(i):
        return groups - 1 - i

    yn, gm, gz, ds, qd, acc_gain, acc_skip, fin_back = call(
        functools.partial(k_gate_back, float(heads * P_SIZE), head_count),
        groups,
        [
            (group_first, SMEM), kept(mix, back), kept(silu, back), kept(slope, back), kept(gyn, back), full(gain_gate),
            kept(xs, back), kept(bc, back), kept(ecum, back),
        ]
        + [(a, pl.BlockSpec((2, GROUP), lambda i: (0, groups - 1 - i))) for a in sums],
        [
            out_kept(width, BF16, back), out_kept(width, BF16, back), out_kept(width, BF16, back),
            out_chunk((N, width), F32, back), out_chunk((1, width), F32, back),
            out_full((8, width), F32), out_full((8, width), F32), out_full(carry, F32),
        ],
        [pltpu.VMEM((N, width), F32), pltpu.VMEM((8, width), F32)],
        3 * 10**9,
        "gate_back",
    )
    yns = [yn]
    for mask in powers(head_count)[1:]:
        yns = yns + [swap(a, "head", mask) for a in yns]
    rows_z, rows_o = dim // tok_count, width // tok_count
    piece_a = (rows_z * width + rows_o * dim) // LANES
    sides = tok_count // 2
    keep_a, send_a = call(
        k_weights,
        groups,
        [kept(yn), rows(out_grad), kept(h), kept(gz)],
        [out_full((sides, piece_a, LANES), F32)] * 2,
        [pltpu.VMEM((dim, width), F32), pltpu.VMEM((width, dim), F32)],
        3 * 10**9,
        "weights",
        place,
        4,
    )
    end_grad, first_grad = carried_in(fin_back, True, place, (keep_a,))
    arrived_a = swap(after(send_a, first_grad), "tok", 1)
    per_token = [
        out_kept(width, F32), out_kept(2 * N, F32), out_kept(LANES, F32), out_kept(LANES, F32)
    ]
    inner = [kept(xs), kept(bc), kept(after(gm, keep_a)), kept(dt), kept(cum), kept(mix), per_chunk(entry), full(per_head)]
    dxw, dbc, rq, qw = call(
        k_within_back, groups, inner, per_token, [], 10 * 10**9, "within_back", None, 4
    )

    def leading(a):
        per = GROUP // 16
        return (a, Kept(16, lambda i: i * per))

    rims, lead = call(
        k_rim,
        groups,
        [
            (group_first, SMEM), leading(xs), leading(bc), leading(gm), leading(dt), leading(cum),
            (cum, Kept(8, lambda i: i * (GROUP // 8) + CHUNK // 8 - 1)),
            leading(dxw), leading(dbc), (cvlead, Kept(1)),
            (ds, Kept(1, lambda i: i * PARTS)),
            (qd, Kept(1, lambda i: i * PARTS)),
            full(end_grad), full(per_head),
        ],
        [((groups, 16, conv_width), F32, Kept(1)), out_full((8, conv_width), F32)],
        [],
        10**9,
        "rim",
    )
    rim_in = lax.ppermute(lead, "tok", [(i, i - 1) for i in range(1, tok_count)])
    at_head = lax.axis_index("head")
    place = jnp.stack([at_head & 1, head_start, at_head, lax.axis_index("tok")]).astype(jnp.int32)
    pairs_a = call(
        k_pair,
        1,
        [full(after(keep_a, lead)), full(arrived_a)],
        [out_full((piece_a, LANES), BF16)] * sides,
        [],
        10**6,
        "pair",
        place,
    )
    arrived_a = [pairs_a[0]] + [swap(pairs_a[k], "tok", 2 * k) for k in range(1, sides)]
    half = groups // 2
    piece_b = rows_z * width // LANES
    tiles = width // LANES
    count = head_count * tok_count
    each = -(-2 * dim // (16 * count)) * 16
    rest = -(-(heads * dim // LANES + 16 + head_count * 8 * tiles) // (8 * count)) * 8
    slots = (count, each, rest)
    small_rows = count * (each + rest)
    acc_shapes = [(dim, width), (dim, 2 * N), (heads, dim), (8 * KCONV + 8, conv_width), (16, LANES)]

    def back_call(final, more_in, more_out, more_scratch, alias, ready):
        def at(i, *s):
            return i + half if final else i

        return call(
            functools.partial(k_back, final, slots),
            half,
            [(group_valid, SMEM)]
            + [
                kept(a, at)
                for a in (after(h, *ready), xs, bc, gm, pre, dt, cum, v)
            ]
            + [(vprev, Kept(1, at))]
            + [
                kept(a, at)
                for a in (dxw, dbc, rq, qw)
            ]
            + [per_chunk(entry, at), per_chunk(ds, at), per_chunk(qd, at), full(end_grad)]
            + [(rims, Kept(1, lambda i, s: jnp.minimum(at(i) + 1, groups - 1)))]
            + [full(cx), full(conv_bc), full(per_head)]
            + more_in,
            [out_kept(width, BF16, at), out_kept(4 * N, BF16, at), out_kept(LANES, BF16, at)]
            + [(a, F32, VMEM) for a in acc_shapes]
            + more_out,
            [pltpu.VMEM((GROUP + 8, conv_width), F32)] * 2 + more_scratch,
            5 * 10**9,
            "back_end" if final else "back_start",
            place,
            4,
            alias,
        )

    partial = back_call(False, [], [], [], (), (pairs_a[0],))
    (total_a,) = call(
        k_reduce, 1, [full(after(a, partial[0])) for a in arrived_a], [out_full((piece_a, LANES), BF16)],
        [], 10**6, "reduce",
    )
    found = back_call(
        True,
        [full(rim_in), full(acc_gain), full(acc_skip)] + [(a, VMEM) for a in partial],
        [
            out_full((tok_count, piece_b, LANES), BF16), out_full((small_rows // 2, LANES), F32),
            out_full((small_rows // 2, LANES), F32),
        ],
        [pltpu.VMEM((small_rows, LANES), F32)],
        [(25 + k, k) for k in range(8)],
        (total_a, yns[1]),
    )
    gx, gbc, gpre = found[:3]
    grads_b, small_keep, small_send = found[8:]
    parts_a = distances(total_a, "tok", 2)
    (mine_a,) = call(
        k_join, 1, [full(after(a, gx)) for a in parts_a], [out_full((sides, piece_a, LANES), BF16)], [],
        10**6, "join", place,
    )

    cuts = 2
    steps = half // cuts
    shape = (tokens // 2 // cuts, dim)

    def input_call(own, k, norm, more, ready):
        def turned(i, s):
            return i + k * steps + half * (s[0] if own else 1 - s[0])

        ends = own and k == cuts - 1
        return call(
            functools.partial(k_input, norm is None, own, ends),
            steps,
            [rows(hidden_in, turned)]
            + [kept(a, turned) for a in (gz, gx, gbc, after(gpre, *ready))]
            + [part_z, part_x, full(w_bc), full(w_dt_here)]
            + [rows(a) for a in more]
            + ([] if norm is None else [full(norm)]),
            [
                (shape, BF16 if own else F32, row_block(shape, GROUP)),
                out_full((8, LANES if ends else dim), F32),
            ],
            [pltpu.VMEM((8, dim), F32)],
            10**9,
            "input_own" if own else "input_sent",
            place,
        )

    sent, norm = input_call(False, 0, None, [], (mine_a,))
    arrived = [swap(sent, "head", 1)]
    small_arrived = after(swap(after(small_send, mine_a), "head", 1), sent)
    for mask in powers(head_count)[1:]:
        small_shape = (small_keep.shape[0] // 2, LANES)
        small_keep, small_send = call(
            functools.partial(k_halve, mask), 1, [full(small_keep), full(small_arrived)],
            [out_full(small_shape, F32)] * 2, [], 10**6, "halve", place,
        )
        small_arrived = swap(small_send, "head", mask)
    for k in range(1, cuts):
        sent, norm = input_call(False, k, norm, [], (mine_a, small_keep))
        arrived.append(swap(sent, "head", 1))
    parts = []
    for k in range(cuts):
        part, norm = input_call(True, k, norm, [arrived[k]], (mine_a,))
        found = [part]
        for mask in powers(head_count)[1:]:
            found = found + [swap(a, "head", mask) for a in found]
        parts.append(found)

    shape = (tok_count, piece_b + each + 2 * (rest + 8), LANES)
    (pieces,) = call(
        functools.partial(k_pieces, slots), 1, [full(small_keep), full(small_arrived), full(norm), full(grads_b)],
        [out_full(shape, BF16)], [], 10**6, "pieces",
    )
    yns = yns + [swap(after(a, pieces), "head", 1) for a in yns]
    (block_out,) = call(
        k_out,
        groups,
        [rows(after(hidden_in, pieces))] + [rows(a) for a in yns] + [full(a) for a in w_outs],
        [out_rows(dim, BF16)],
        [],
        5 * 10**9,
        "out",
    )

    (copies,) = call(
        functools.partial(k_reduce_both, piece_b + each), 1,
        [full(after(exchange(pieces, "tok"), block_out))],
        [out_full(shape, BF16)], [], 10**6, "reduce_both",
    )
    sum_b = exchange(copies, "tok")
    other_a = swap(after(mine_a, copies), "tok", 1)
    (tick,) = call(
        k_tick, 1, [(copies, row_block(copies.shape, 1))], [out_full((16, LANES), BF16)], [], 1, "tick"
    )
    (grad_w_out,) = call(
        k_unpack_out, 1, [full(mine_a), full(other_a)], [out_full((width, dim), F32)],
        [], 10**6, "unpack_out", place,
    )
    others = [
        [swap(found[0], "head", 1)] + [swap(after(a, tick), "head", 1) for a in found[1:]]
        for found in parts
    ]

    def turned_back(i, s):
        return lax.rem(i + half * s[0], groups)

    def in_cut(a, k):
        return (a, row_block(a.shape, GROUP, lambda i, s: jnp.clip(i - k * steps, 0, steps - 1)))

    (grad_in,) = call(
        functools.partial(k_in_back, steps),
        groups,
        [rows(hidden_in, turned_back), rows(out_grad, turned_back), full(gain_in)]
        + [in_cut(a, k) for k, found in enumerate(parts + others) for a in found],
        [out_rows(dim, F32, turned_back)],
        [],
        10**9,
        "in_back",
        place,
    )
    shape = (small_rows // head_count + tok_count, LANES)
    (quarter,) = call(
        functools.partial(k_quarter, piece_b, slots), 1, [full(after(sum_b, grad_in))], [out_full(shape, F32)],
        [], 10**6, "quarter",
    )
    quarters = [(quarter, 0)]
    for mask in powers(head_count):
        quarters = quarters + [(swap(a, "head", mask), k | mask) for a, k in quarters]
    quarters = [a for a, _ in sorted(quarters, key=lambda item: item[1])]

    (grad_w_zx,) = call(
        k_unpack,
        1,
        [full(mine_a), full(other_a), full(sum_b)],
        [out_full((dim, 2, real), F32)],
        [],
        10**6,
        "unpack",
        place,
    )
    grad_w_bc, grad_w_dt, grad_taps, grad_bias, grad_alog, grad_skip, grad_norm, own_taps, own_gain = call(
        functools.partial(k_small, slots),
        1,
        [full(a) for a in quarters],
        [
            out_full((dim, 2 * N), F32), out_full((heads, dim), F32), out_full((KCONV + 1, 2 * N), F32),
            out_full((1, heads), F32), out_full((1, heads), F32), out_full((1, heads), F32),
            out_full((1, dim), F32), out_full((KCONV + 1, real), F32), out_full((1, real), F32),
        ],
        [pltpu.VMEM((small_rows, LANES), F32)],
        10**6,
        "small",
        place,
    )

    return (
        block_out,
        grad_in,
        grad_norm[0],
        grad_w_zx,
        grad_w_bc,
        grad_w_dt.T,
        grad_bias[0],
        grad_alog[0],
        own_taps,
        grad_taps,
        grad_skip[0],
        own_gain[0],
        grad_w_out[:real],
    )


def solution(mesh):
    return jax.shard_map(
        on_device,
        mesh=mesh,
        in_specs=(
            P("tok", None), P(), P(None, None, "head"), P(), P(), P(), P(), P(None, "head"), P(), P(),
            P("head"), P("head", None), P("tok", None), P("tok"), P("tok"),
        ),
        out_specs=(
            P("tok", None), P("tok", None), P(), P(None, None, "head"), P(), P(), P(), P(),
            P(None, "head"), P(), P(), P("head"), P("head", None),
        ),
        check_vma=False,
    )
```

```python
import functools
import math

import jax
import jax.numpy as jnp
from jax import lax
from jax.experimental import pallas as pl
from jax.experimental.pallas import tpu as pltpu
from jax.sharding import PartitionSpec as P

P_SIZE = 64
N = 128
KCONV = 4
GROUP = 256
CHUNK = 128
LANES = 128
PARTS = GROUP // CHUNK
EPS = 1e-05
VMEM_LIMIT = 10 * 1024 * 1024
F32 = jnp.float32
BF16 = jnp.bfloat16


def mm(a, b, ca=1, cb=0):
    return lax.dot_general(a, b, (((ca,), (cb,)), ((), ())), preferred_element_type=F32)


def iota(shape, dim):
    return lax.broadcasted_iota(jnp.int32, shape, dim)


def spread(cols, width):
    rows = cols.shape[0]
    low = iota((rows, LANES), 1) < P_SIZE
    tiles = [
        jnp.where(low, cols[:, 2 * p : 2 * p + 1], cols[:, 2 * p + 1 : 2 * p + 2])
        for p in range(width // LANES)
    ]
    return jnp.concatenate(tiles, axis=1)


def gather_heads(width):
    return (iota((width, LANES), 0) // P_SIZE == iota((width, LANES), 1)).astype(BF16)


def fold_rows(value):
    rows, width = value.shape
    return value.reshape(rows // 8, 8, width).sum(axis=0)


def tri(kind):
    row, col = iota((CHUNK, CHUNK), 0), iota((CHUNK, CHUNK), 1)
    return {"le": col <= row, "ge": col >= row, "lt": col < row}[kind]


def pair_rows(tile):
    low = iota(tile.shape, 1) < P_SIZE
    zero = jnp.zeros_like(tile)
    return jnp.concatenate([jnp.where(low, tile, zero), jnp.where(low, zero, tile)], axis=0)


def split2(value):
    high = value.astype(BF16)
    return high, (value - high.astype(F32)).astype(BF16)


def split3(value):
    high, rest = split2(value)
    return high, rest, (value - high.astype(F32) - rest.astype(F32)).astype(BF16)


def mm_left(a, b, ca=1, cb=0):
    high, low = split2(a)
    return mm(high, b, ca, cb) + mm(low, b, ca, cb)


def mm_right(a, b, ca=1, cb=0):
    high, low = split2(b)
    return mm(a, high, ca, cb) + mm(a, low, ca, cb)


def mm_both(a, b, ca=1, cb=0):
    ah, al = split2(a)
    bh, bl = split2(b)
    return mm(ah, bh, ca, cb) + mm(al, bh, ca, cb) + mm(ah, bl, ca, cb)


def stacked(value):
    return jnp.concatenate(
        [value[:, c : c + LANES] for c in range(0, value.shape[1], LANES)], axis=0
    )


def tree(terms):
    while len(terms) > 1:
        terms = [terms[k] + terms[k + 1] for k in range(0, len(terms), 2)]
    return terms[0]


def rms_inv(u):
    return lax.rsqrt(jnp.mean(u * u, axis=1, keepdims=True) + EPS)


def k_front(
    first, valid, hid, rim, gain, w_x, w_bc, w_dt, hp, cx, cb,
    h_o, v_o, pre_o, prev_o, lead_o, xs_o, bc_o, dt_o, cum_o, ent_o, pd_o, fin_o,
    vbuf, state, decay,
):
    g = pl.program_id(0)
    width = w_x.shape[1]

    def normed(block):
        u = block.astype(F32)
        return (u * rms_inv(u) * gain[...]).astype(BF16)

    @pl.when(g == 0)
    def _():
        hr = normed(rim[...])
        vbuf[0:8, :width] = mm(hr, w_x[...])[8:16]
        vbuf[0:8, width:] = mm(hr, w_bc[...])[8:16]
        state[...] = jnp.zeros_like(state)
        decay[...] = jnp.ones_like(decay)

    keep = 1.0 - first[g].astype(F32)
    vbuf[0:8, :] = vbuf[0:8, :] * keep
    state[...] = state[...] * keep
    decay[...] = decay[...] * keep
    h = normed(hid[...])
    h_o[...] = h
    raw = mm(h, w_dt[...]) + hp[0:1, :]
    pre_o[...] = raw
    vbuf[8:, :width] = mm(h, w_x[...])
    vbuf[8:, width:] = mm(h, w_bc[...])
    v_o[...] = vbuf[8:, :]
    taps = jnp.concatenate([cx[...], cb[...]], axis=1)
    conv = taps[KCONV : KCONV + 1, :] + taps[0:1, :] * vbuf[5 : 5 + GROUP, :]
    for k in range(1, KCONV):
        conv = conv + taps[k : k + 1, :] * vbuf[5 + k : 5 + k + GROUP, :]
    prev_o[0] = vbuf[0:8, :]
    lead_o[0] = conv[0:16, :]
    act = (conv * jax.nn.sigmoid(conv)).astype(BF16)
    xs_o[...] = act[:, :width]
    bc_o[...] = act[:, width:]
    vbuf[0:8, :] = vbuf[GROUP : GROUP + 8, :]
    live = iota((GROUP, LANES), 0) < valid[g]
    soft = jnp.maximum(raw, 0.0) + jnp.log1p(jnp.exp(-jnp.abs(raw)))
    dt = jnp.where(live, soft, 0.0)
    dt_o[...] = dt
    ld = dt * -jnp.exp(hp[1:2, :])
    lower = tri("le").astype(BF16)
    lower = jnp.concatenate([lower] * 3, axis=1)
    for c in range(PARTS):
        rows = slice(c * CHUNK, (c + 1) * CHUNK)
        cum = mm(lower, jnp.concatenate(split3(ld[rows]), axis=0))
        cum_o[rows, :] = cum
        end = cum[CHUNK - 1 : CHUNK, :]
        factor = dt[rows] * jnp.exp(end - cum)
        ent_o[c] = state[...]
        pd_o[c] = decay[0:1]
        xd = act[rows, :width].astype(F32) * spread(factor, width)
        new = mm_right(act[rows, width : width + N], xd, 0, 0)
        ec = spread(jnp.exp(end), width)
        state[...] = state[...] * ec + new
        decay[...] = decay[...] * ec

    @pl.when(g == pl.num_programs(0) - 1)
    def _():
        fin_o[0:N, :] = state[...]
        fin_o[N:, :] = decay[...]


def k_proj(h, og, w_z, w_out, silu_o, slope_o, gyn_o):
    z = mm(h[...], w_z[...])
    sig = jax.nn.sigmoid(z)
    silu_o[...] = z * sig
    slope_o[...] = sig * (1.0 + z * (1.0 - sig))
    gyn_o[...] = mm(og[...], w_out[...], 1, 1)


def k_within(xs, bc, dt, cum, y_o, ecum_o):
    width = xs.shape[1]
    mask = tri("le")
    for c in range(PARTS):
        rows = slice(c * CHUNK, (c + 1) * CHUNK)
        scores = mm(bc[rows, N:], bc[rows, :N], 1, 1)
        a = cum[rows, :]
        ecum_o[rows, :] = spread(jnp.exp(a), width)
        b = jnp.transpose(a - jnp.log(dt[rows, :]))
        for p in range(width // LANES):
            lanes = slice(p * LANES, (p + 1) * LANES)
            weights = []
            for h in (2 * p, 2 * p + 1):
                gap = a[:, h : h + 1] - b[h : h + 1, :]
                weights.append(jnp.where(mask, jnp.exp(gap), 0.0) * scores)
            y_o[rows, lanes] = mm_left(jnp.concatenate(weights, axis=1), pair_rows(xs[rows, lanes]))


def k_gate(ent, pd, prev, bc, ecum, yw, xs, silu, gyn, gain, hp, mix_o, ent_o, sums_o):
    width = xs.shape[1]
    skip = spread(hp[2:3, :], width)
    for c in range(PARTS):
        rows = slice(c * CHUNK, (c + 1) * CHUNK)
        entry = ent[c] + pd[c] * prev[0:N, :]
        ent_o[c] = entry
        across = mm_right(bc[rows, N:], entry) * ecum[rows, :]
        mix_o[rows, :] = yw[rows, :] + across + skip * xs[rows, :].astype(F32)
    gated = mix_o[...] * silu[...]
    square = jnp.sum(gated * gated, axis=1, keepdims=True)
    inner = jnp.sum(gyn[...] * gain[...] * gated, axis=1, keepdims=True)
    lane = iota((GROUP, LANES), 1)
    both = jnp.where(lane == 0, square, inner)
    sums_o[...] = jnp.transpose(both)[0:2, :]


def k_gate_back(
    total, count, first, mix, silu, slope, gyn, gain, xs, bc, ecum, *rest,
):
    sums = rest[:count]
    yn_o, g_o, gz_o, ds_o, qd_o, again_o, askip_o, fin_o, state, decay = rest[count:]
    i = pl.program_id(0)
    g = pl.num_programs(0) - 1 - i
    width = xs.shape[1]

    @pl.when(i == 0)
    def _():
        state[...] = jnp.zeros_like(state)
        decay[...] = jnp.ones_like(decay)
        again_o[...] = jnp.zeros_like(again_o)
        askip_o[...] = jnp.zeros_like(askip_o)

    rows2 = tree([part[...] for part in sums])
    both = jnp.transpose(jnp.concatenate([rows2, jnp.zeros((LANES - 2, GROUP), F32)], axis=0))
    inv = lax.rsqrt(both[:, 0:1] / total + EPS)
    inner = both[:, 1:2] / total
    silu = silu[...]
    mixer = mix[...]
    gated = mixer * silu
    scaled = gated * inv
    gy = gyn[...]
    gn = gain[...]
    yn_o[...] = (scaled * gn).astype(BF16)
    again_o[...] += fold_rows(gy * scaled)
    gg = inv * gn * gy - gated * (inv * inv * inv * inner)
    gm = (gg * silu).astype(BF16)
    g_o[...] = gm
    gz_o[...] = (gg * mixer * slope[...]).astype(BF16)
    gmf = gm.astype(F32)
    askip_o[...] += fold_rows(gmf * xs[...].astype(F32))
    for c in reversed(range(PARTS)):
        rows = slice(c * CHUNK, (c + 1) * CHUNK)
        ds_o[c] = state[...]
        qd_o[c] = decay[0:1]
        new = mm_right(bc[rows, N:], gmf[rows] * ecum[rows, :], 0, 0)
        ec = ecum[(c + 1) * CHUNK - 1 : (c + 1) * CHUNK, :]
        state[...] = state[...] * ec + new
        decay[...] = decay[...] * ec
    keep = 1.0 - first[g].astype(F32)
    state[...] = state[...] * keep
    decay[...] = decay[...] * keep

    @pl.when(i == pl.num_programs(0) - 1)
    def _():
        fin_o[0:N, :] = state[...]
        fin_o[N:, :] = decay[...]


def k_weights(place, yn, og, h, gz, keep_o, send_o, acc_z, acc_out):
    i = pl.program_id(0)

    @pl.when(i == 0)
    def _():
        acc_z[...] = jnp.zeros_like(acc_z)
        acc_out[...] = jnp.zeros_like(acc_out)

    acc_z[...] += mm(h[...], gz[...], 0, 0)
    acc_out[...] += mm(yn[...], og[...], 0, 0)

    @pl.when(i == pl.num_programs(0) - 1)
    def _():
        count = keep_o.shape[0]
        rz, ro = acc_z.shape[0] // (2 * count), acc_out.shape[0] // (2 * count)
        side = place[3] % 2
        for k in range(count):
            for out, at in ((keep_o, 2 * k + side), (send_o, 2 * k + 1 - side)):
                out[k] = jnp.concatenate(
                    [
                        stacked(acc_z[pl.ds(pl.multiple_of(at * rz, 8), rz), :]),
                        stacked(acc_out[pl.ds(pl.multiple_of(at * ro, 8), ro), :]),
                    ],
                    axis=0,
                )


def k_pair(place, keep, arrived, *outs):
    for k, out in enumerate(outs):
        at = (place[3] // 2) ^ k
        out[...] = (keep[at] + arrived[at]).astype(BF16)


def k_join(place, *refs):
    out = refs[-1]
    for k, part in enumerate(refs[:-1]):
        out[(place[3] // 2) ^ k] = part[...]


def k_within_back(
    xs, bc, g, dt, cum, mix, ent, hp,
    dxw_o, dbc_o, rq_o, qw_o,
):
    width = xs.shape[1]
    mask = tri("ge")
    heads = gather_heads(width)
    skip = spread(hp[2:3, :], width)
    for c in range(PARTS):
        rows = slice(c * CHUNK, (c + 1) * CHUNK)
        bw, cr = bc[rows, :N], bc[rows, N:]
        scores = mm(bw, cr, 1, 1)
        a = cum[rows, :]
        b = a - jnp.log(dt[rows, :])
        at = jnp.transpose(a)
        dscore = jnp.zeros((CHUNK, CHUNK), F32)
        for p in range(width // LANES):
            lanes = slice(p * LANES, (p + 1) * LANES)
            decays = [
                jnp.where(mask, jnp.exp(at[h : h + 1, :] - b[:, h : h + 1]), 0.0)
                for h in (2 * p, 2 * p + 1)
            ]
            gt = g[rows, lanes]
            pairs = mm(pair_rows(xs[rows, lanes]), gt, 1, 1)
            dscore = dscore + pairs[:CHUNK] * decays[0] + pairs[CHUNK:] * decays[1]
            weights = jnp.concatenate([d * scores for d in decays], axis=1)
            dxw_o[rows, lanes] = mm_left(weights, pair_rows(gt))
        high, low = split2(dscore)
        gf = g[rows, :].astype(F32)
        xf = xs[rows, :].astype(F32)
        ge = gf * spread(jnp.exp(a), width)
        dbc_o[rows, :N] = mm(high, cr) + mm(low, cr)
        dbc_o[rows, N:] = mm(high, bw, 0, 0) + mm(low, bw, 0, 0) + mm_both(ge, ent[c], 1, 1)
        row_part = mm_left(gf * (mix[rows, :] - skip * xf), heads)
        col_part = mm_left(xf * dxw_o[rows, :], heads)
        rq_o[rows, :] = row_part - col_part
        qw_o[rows, :] = col_part


def silu_slope(value):
    sig = jax.nn.sigmoid(value)
    return sig * (1.0 + value * (1.0 - sig))


def k_rim(first, xs, bc, g, dt, cum, cend, dxw, dbc, cv, ds, qd, endg, hp, out, lead_o):
    i = pl.program_id(0)
    width = xs.shape[1]
    d_state = ds[0] + qd[0] * endg[0:N, :]
    factor = spread(dt[...] * jnp.exp(cend[7:8, :] - cum[...]), width)
    skip = spread(hp[2:3, :], width)
    xd = xs[...].astype(F32) * factor
    gx = dxw[...] + factor * mm_right(bc[:, :N], d_state) + g[...].astype(F32) * skip
    gb = dbc[:, :N] + mm_both(xd, d_state, 1, 1)
    slope = silu_slope(cv[0]) * (1.0 - first[i].astype(F32))
    out[0, :, :width] = gx * slope[:, :width]
    out[0, :, width : width + N] = gb * slope[:, width : width + N]
    out[0, :, width + N :] = dbc[:, N:] * slope[:, width + N :]

    @pl.when(i == 0)
    def _():
        lead_o[...] = out[0, 0:8, :]


def k_back(final, slots, place, *refs):
    (
        valid, h, xs, bc, g, pre, dt, cum, v, vprev, dxw, dbc, rq, qw, ent, ds, qd, endg, rims, cx, cb, hp,
    ) = refs[:22]
    if final:
        rim_in, acc_gain, acc_skip = refs[22:25]
        gx_o, gbc_o, gpre_o = refs[33:36]
        acc_x, acc_bc, acc_dt, acc_taps, acc_heads = refs[36:41]
        grads_o, keep_o, send_o, gbuf, vbuf, small_o = refs[41:]
    else:
        gx_o, gbc_o, gpre_o, acc_x, acc_bc, acc_dt, acc_taps, acc_heads, gbuf, vbuf = refs[22:]
    i = pl.program_id(0)
    last = pl.num_programs(0) - 1
    group = i + pl.num_programs(0) if final else i
    width = xs.shape[1]
    heads = gather_heads(width)
    skip = spread(hp[2:3, :], width)
    rate = -jnp.exp(hp[1:2, :])

    if not final:

        @pl.when(i == 0)
        def _():
            for ref in (acc_x, acc_bc, acc_dt, acc_taps, acc_heads):
                ref[...] = jnp.zeros_like(ref)

    upper, below = tri("ge").astype(BF16), tri("lt").astype(BF16)
    both = jnp.concatenate([upper, upper, below, below], axis=1)
    taps = jnp.concatenate([cx[...], cb[...]], axis=1)
    vbuf[0:8, :] = vprev[0]
    vbuf[8:, :] = v[...]
    for c in range(PARTS):
        rows = slice(c * CHUNK, (c + 1) * CHUNK)
        d_state = ds[c] + qd[c] * endg[0:N, :]
        d_high, d_low = split2(d_state)
        a = cum[rows, :]
        end = a[CHUNK - 1 : CHUNK, :]
        factor = spread(dt[rows, :] * jnp.exp(end - a), width)
        xf = xs[rows, :].astype(F32)
        bw = bc[rows, :N]
        dxs = factor * (mm(bw, d_high) + mm(bw, d_low))
        x_high, x_low = split2(xf * factor)
        gb = dbc[rows, :N] + (mm(x_high, d_high, 1, 1) + mm(x_low, d_high, 1, 1) + mm(x_high, d_low, 1, 1))
        gx = dxw[rows, :] + dxs + g[rows, :].astype(F32) * skip
        conv = taps[KCONV : KCONV + 1, :]
        for k in range(KCONV):
            start = 5 + k + c * CHUNK
            conv = conv + taps[k : k + 1, :] * vbuf[start : start + CHUNK, :]
        slope = silu_slope(conv)
        gbuf[rows, :width] = gx * slope[:, :width]
        gbuf[rows, width : width + N] = gb * slope[:, width : width + N]
        gbuf[rows, width + N :] = dbc[rows, N:] * slope[:, width + N :]
        qs = mm_left(xf * dxs, heads)
        carried = mm_left(fold_rows(d_state * ent[c]), heads)
        ends = jnp.sum(carried, axis=0, keepdims=True) * jnp.exp(end)
        g_ld = mm(both, jnp.concatenate(split2(rq[rows, :]) + split2(qs), axis=0)) + ends
        step = dt[rows, :]
        direct = jnp.where(step > 0.0, (qw[rows, :] + qs) / jnp.where(step > 0.0, step, 1.0), 0.0)
        live = iota((CHUNK, LANES), 0) + c * CHUNK < valid[group]
        own = iota((CHUNK, LANES), 1) < width // P_SIZE
        g_pre = jnp.where(
            live & own, (direct + g_ld * rate) * jax.nn.sigmoid(pre[rows, :]), 0.0
        )
        acc_heads[0:8, :] += fold_rows(g_pre)
        acc_heads[8:16, :] += fold_rows(g_ld * step * rate)
        low = g_pre.astype(BF16)
        gpre_o[rows, :] = low
        acc_dt[...] += mm(pltpu.roll(low.astype(F32), place[1], 1).astype(BF16), h[rows, :], 0, 0)[0 : acc_dt.shape[0]]

    gbuf[GROUP:, :] = rims[0, 0:8, :]
    if final:

        @pl.when(i == last)
        def _():
            gbuf[GROUP:, :] = rim_in[0:8, :]

    vv = v[...]
    gv = jnp.zeros_like(vv)
    for k in range(KCONV):
        shifted = gbuf[KCONV - 1 - k : KCONV - 1 - k + GROUP, :]
        gv = gv + taps[k : k + 1, :] * shifted
        acc_taps[8 * k : 8 * k + 8, :] += fold_rows(vv * shifted)
    acc_taps[8 * KCONV :, :] += fold_rows(gbuf[0:GROUP, :])
    gx_low = gv[:, :width].astype(BF16)
    bc_high, bc_low = split2(gv[:, width:])
    gx_o[...] = gx_low
    gbc_o[:, : 2 * N] = bc_high
    gbc_o[:, 2 * N :] = bc_low
    hh = h[...]
    acc_x[...] += mm(hh, gx_low, 0, 0)
    acc_bc[...] += mm(hh, bc_high, 0, 0) + mm(hh, bc_low, 0, 0)
    if not final:
        return

    @pl.when(i == last)
    def _():
        count = grads_o.shape[0]
        rx = acc_x.shape[0] // count
        for k in range(count):
            grads_o[k] = stacked(acc_x[k * rx : (k + 1) * rx, :]).astype(BF16)
        dim = acc_bc.shape[0]
        at = 0

        def put(value):
            nonlocal at
            small_o[at : at + value.shape[0], :] = value
            at += value.shape[0]

        put(acc_bc[:, :LANES])
        put(acc_bc[:, LANES:])
        count, each, rest = slots
        if at < count * each:
            put(jnp.zeros((count * each - at, LANES), F32))
        put(stacked(acc_dt[...]))

        def line(value):
            return jnp.sum(value, axis=0, keepdims=True)

        def lane_home(value):
            return pltpu.roll(jnp.broadcast_to(value, (8, LANES)), place[1], 1)[0:1]

        own = iota((1, LANES), 1) < width // P_SIZE
        taps_sum = [line(acc_taps[8 * k : 8 * k + 8, :]) for k in range(KCONV + 1)]
        skips = mm_left(acc_skip[...], heads)
        head_rows = [
            lane_home(jnp.where(own, line(x), 0.0))
            for x in (acc_heads[0:8, :], acc_heads[8:16, :], skips)
        ]
        put(jnp.concatenate([t[:, width : width + N] for t in taps_sum] + head_rows, axis=0))
        spare = jnp.zeros((8 - KCONV - 1, LANES), F32)
        put(jnp.concatenate([t[:, width + N :] for t in taps_sum] + [spare], axis=0))
        small_o[at:, :] = jnp.zeros_like(small_o[at:, :])
        gains = line(acc_gain[...])
        tiles = width // LANES
        own_rows = jnp.concatenate(
            [
                jnp.concatenate(
                    [t[:, k * LANES : (k + 1) * LANES] for t in taps_sum]
                    + [gains[:, k * LANES : (k + 1) * LANES], spare[0:2]],
                    axis=0,
                )
                for k in range(tiles)
            ],
            axis=0,
        )
        small_o[pl.ds(pl.multiple_of(at + place[2] * (8 * tiles), 8), 8 * tiles), :] = own_rows
        for k in range(count // 2):
            for out, side in ((keep_o, place[0]), (send_o, 1 - place[0])):
                slot = side * (count // 2) + k
                to = k * (each + rest)
                out[to : to + each, :] = small_o[pl.ds(pl.multiple_of(slot * each, 8), each), :]
                start = pl.multiple_of(count * each + slot * rest, 8)
                out[to + each : to + each + rest, :] = small_o[pl.ds(start, rest), :]


def input_grad(hid, gz, gx, gbc, gpre, w_z, w_x, w_bc, w_dt):
    gh = (
        mm(gpre[...], w_dt[...], 1, 1)
        + mm(gz[...], w_z[...], 1, 1)
        + mm(gx[...], w_x[...], 1, 1)
        + mm(gbc[:, : 2 * N], w_bc[...], 1, 1)
        + mm(gbc[:, 2 * N :], w_bc[...], 1, 1)
    )
    u = hid[...].astype(F32)
    return gh, fold_rows(gh * (u * rms_inv(u)))


def k_input(begins, own, ends, place, *refs):
    refs, (out, norm_o, acc) = refs[:-3], refs[-3:]
    i = pl.program_id(0)

    @pl.when(i == 0)
    def _():
        acc[...] = jnp.zeros_like(acc) if begins else refs[-1][...]

    gh, norm = input_grad(*refs[:9])
    out[...] = (gh + refs[9][...]).astype(BF16) if own else gh
    acc[...] += norm

    @pl.when(i == pl.num_programs(0) - 1)
    def _():
        if ends:
            rows = acc.shape[1] // LANES
            norm_o[0:rows, :] = stacked(jnp.sum(acc[...], axis=0, keepdims=True))
            norm_o[rows:, :] = jnp.zeros((8 - rows, LANES), F32)
        else:
            norm_o[...] = acc[...]


def k_reduce(*refs):
    out = refs[-1]
    out[...] = tree([part[...].astype(F32) for part in refs[:-1]]).astype(BF16)


def k_halve(mask, place, kept, arrived, keep_o, send_o):
    rows = keep_o.shape[0]
    upper = (place[2] // mask) % 2
    for out, at in ((keep_o, upper * rows), (send_o, (1 - upper) * rows)):
        at = pl.multiple_of(at, 8)
        out[...] = kept[pl.ds(at, rows), :] + arrived[pl.ds(at, rows), :]


def k_pieces(slots, kept, arrived, norm, large, out):
    count = out.shape[0]
    _, each, rest = slots
    rows = each + rest
    cut = large.shape[1]
    spare = jnp.zeros((7, LANES), F32)
    for k in range(count):
        own = slice(k * rows, (k + 1) * rows)
        value = kept[own, :] + arrived[own, :]
        line = norm[k : k + 1, :] if k < 8 else spare[0:1]
        small = jnp.concatenate([value[each:], line, spare], axis=0)
        out[k, 0:cut, :] = large[k]
        out[k, cut : cut + each, :] = value[:each].astype(BF16)
        out[k, cut + each :, :] = jnp.concatenate(split2(small), axis=0)


def k_reduce_both(cut, parts, out):
    count = out.shape[0]
    rows = (out.shape[1] - cut) // 2
    terms = [parts[k].astype(F32) for k in range(count)]
    small = tree([term[cut : cut + rows] + term[cut + rows :] for term in terms])
    large = tree([term[:cut] for term in terms]).astype(BF16)
    joined = jnp.concatenate([large, *split2(small)], axis=0)
    for k in range(count):
        out[k] = joined


def k_tick(value, out):
    out[...] = value[0, 0:16, :]


def k_quarter(cut, parts, out):
    rows = parts.shape[1] - cut
    for k in range(parts.shape[0]):
        out[k * rows : (k + 1) * rows, :] = parts[k, cut:, :]


def unstack(value, rows):
    return jnp.concatenate(
        [value[k : k + rows, :] for k in range(0, value.shape[0], rows)], axis=1
    )


def k_unpack_out(place, mine, other, w_out_o):
    count = 2 * mine.shape[0]
    ro = w_out_o.shape[0] // count
    rows = ro * w_out_o.shape[1] // LANES
    side = place[3] % 2
    for k in range(count // 2):
        for part, at in ((mine, 2 * k + side), (other, 2 * k + 1 - side)):
            piece = part[k].astype(F32)
            w_out_o[pl.ds(pl.multiple_of(at * ro, 8), ro), :] = unstack(piece[piece.shape[0] - rows :], ro)


def k_unpack(place, mine, other, b, w_zx_o):
    count = b.shape[0]
    dim, _, real = w_zx_o.shape
    rz = dim // count
    cut = rz * -(-real // LANES)
    side = place[3] % 2
    for k in range(count // 2):
        for part, at in ((mine, 2 * k + side), (other, 2 * k + 1 - side)):
            piece = part[k].astype(F32)
            w_zx_o[pl.ds(at * rz, rz), 0, :] = unstack(piece[0:cut], rz)[:, :real]
    for k in range(count):
        own = unstack(b[k, 0:cut, :].astype(F32), rz)[:, :real]
        w_zx_o[k * rz : (k + 1) * rz, 1, :] = own


def k_small(slots, place, *refs):
    count = len(refs) - 10
    w_bc_o, w_dt_o, bc_taps_o, bias_o, alog_o, skip_o, norm_o, taps_o, gain_o, buf = refs[count:]
    total, each, rest = slots
    steps = total // count
    tall = each + 2 * (rest + 8)
    dim = w_bc_o.shape[0]
    norms = [[] for _ in range(dim // LANES)]
    for k in range(count):
        from_head, at = place[2] ^ k, 0
        for mask in powers(count):
            at = 2 * at + (from_head // mask) % 2
        for t in range(steps):
            slot = at * steps + t
            value = refs[k][t * tall : (t + 1) * tall, :].astype(F32)
            small = value[each : each + rest + 8] + value[each + rest + 8 :]
            buf[pl.ds(pl.multiple_of(slot * each, 8), each), :] = value[:each]
            buf[pl.ds(pl.multiple_of(total * each + slot * rest, 8), rest), :] = small[:rest]
            if t < len(norms):
                norms[t].append(small[rest : rest + 1])
    for k, rows in enumerate(norms):
        norm_o[:, k * LANES : (k + 1) * LANES] = tree(rows)
    w_bc_o[:, :LANES] = buf[0:dim, :]
    w_bc_o[:, LANES:] = buf[dim : 2 * dim, :]
    at = total * each
    heads = w_dt_o.shape[0]
    w_dt_o[...] = unstack(buf[at : at + heads * dim // LANES, :], heads)
    at += heads * dim // LANES
    bc_taps_o[...] = unstack(buf[at : at + 16, :], 8)[0 : KCONV + 1]
    for k, out in enumerate((bias_o, alog_o, skip_o)):
        out[...] = buf[at + KCONV + 1 + k : at + KCONV + 2 + k, 0 : out.shape[1]]
    real = taps_o.shape[1]
    tiles = -(-real // LANES)
    own = buf[pl.ds(pl.multiple_of(at + 16 + place[2] * (8 * tiles), 8), 8 * tiles), :]
    own = unstack(own, 8)[:, 0:real]
    taps_o[...] = own[0 : KCONV + 1]
    gain_o[...] = own[KCONV + 1 : KCONV + 2]


def k_out(hid, *refs):
    count = (len(refs) - 1) // 2
    out = refs[-1]
    total = tree([mm(refs[k][...], refs[count + k][...]) for k in range(count)])
    out[...] = (hid[...].astype(F32) + total).astype(BF16)


def k_in_back(steps, place, hid, og, gain, *refs):
    i = pl.program_id(0)
    cuts = pl.num_programs(0) // steps
    out = refs[-1]
    count = (len(refs) - 1) // cuts

    def finish(parts):
        gh = tree([part[...].astype(F32) for part in parts])
        u = hid[...].astype(F32)
        inv = rms_inv(u)
        scaled = gh * gain[...]
        dot = jnp.sum(scaled * u, axis=1, keepdims=True) / u.shape[1]
        out[...] = inv * scaled - u * (inv * inv * inv * dot) + og[...].astype(F32)

    for k in range(cuts):
        pl.when(i // steps == k)(functools.partial(finish, refs[k * count : (k + 1) * count]))


def row_block(shape, rows, at=None):
    at = at or (lambda i, *s: i)
    rest = tuple(shape[1:])
    return pl.BlockSpec((rows,) + rest, lambda i, *s: (at(i, *s),) + (0,) * len(rest))


def whole(shape):
    return pl.BlockSpec(tuple(shape), lambda i, *s: (0,) * len(shape))


SMEM = pl.BlockSpec(memory_space=pltpu.SMEM)
VMEM = pl.BlockSpec(memory_space=pltpu.VMEM)


class Kept:
    def __init__(self, rows, at=None):
        self.rows = rows
        self.at = at or (lambda i, *s: i)

    def view(self, ref, i, scalars):
        start = pl.multiple_of(self.at(i, *scalars) * self.rows, self.rows)
        return ref.at[pl.ds(start, self.rows)]


def call(kernel, steps, ins, outs, scratch, flops, name, place=None, weight=1, alias=()):
    moved = sum(a.size * a.dtype.itemsize for a, _ in ins)
    for shape, dtype, _ in outs:
        moved += functools.reduce(lambda x, y: x * y, shape) * jnp.dtype(dtype).itemsize
    scalars = [] if place is None else [place]
    specs = [spec for _, spec in ins] + [spec for _, _, spec in outs]
    first = len(scalars)

    def body(*refs):
        i = pl.program_id(0)
        seen = list(refs)
        for k, spec in enumerate(specs):
            if isinstance(spec, Kept):
                seen[first + k] = spec.view(refs[first + k], i, refs[:first])
        kernel(*seen)

    places = [
        pl.BlockSpec(memory_space=pltpu.VMEM) if isinstance(spec, Kept) else spec for spec in specs
    ]
    held = 4 * 1024 * 1024
    for (shape, dtype), spec in zip(
        [(a.shape, a.dtype) for a, _ in ins] + [(shape, dtype) for shape, dtype, _ in outs], places
    ):
        if spec.block_shape is not None:
            padded = list(spec.block_shape)
            padded[-1] = -(-padded[-1] // LANES) * LANES
            held += 2 * math.prod(padded) * jnp.dtype(dtype).itemsize
    for buffer in scratch:
        held += math.prod(buffer.shape) * jnp.dtype(buffer.dtype).itemsize
    return pl.pallas_call(
        body,
        grid_spec=pltpu.PrefetchScalarGridSpec(
            num_scalar_prefetch=len(scalars),
            grid=(steps,),
            in_specs=places[: len(ins)],
            out_specs=places[len(ins) :],
            scratch_shapes=scratch,
        ),
        out_shape=[jax.ShapeDtypeStruct(s, d) for s, d, _ in outs],
        compiler_params=pltpu.CompilerParams(
            dimension_semantics=("arbitrary",), vmem_limit_bytes=max(VMEM_LIMIT, held)
        ),
        cost_estimate=pl.CostEstimate(
            flops=flops * weight, bytes_accessed=moved * weight, transcendentals=0
        ),
        input_output_aliases={first + k: j for k, j in alias},
        name=name,
    )(*scalars, *[a for a, _ in ins])


def far(pair):
    return (pltpu.with_memory_space_constraint(pair[0], pltpu.HBM), pair[1])


def swap(value, axis, mask):
    return lax.ppermute(value, axis, [(i, i ^ mask) for i in range(lax.axis_size(axis))])


def after(value, *others):
    return lax.optimization_barrier((value,) + others)[0]


def powers(count):
    return [1 << k for k in range(count.bit_length() - 1)]


def k_merge(mask, backward, first, place, *refs):
    total, other = refs[:2]
    before = None if first else refs[2]
    outs = refs[2 if first else 3 :]
    upper = (place[3] // mask) % 2 == 1
    later = jnp.logical_not(upper) if backward else upper

    def merge(early, late, out):
        scale = late[N : N + 1, :]
        out[0:N, :] = scale * early[0:N, :] + late[0:N, :]
        out[N:, :] = scale * early[N:, :]

    @pl.when(later)
    def _():
        if first:
            outs[0][...] = other[...]
        else:
            merge(other, before, outs[0])
        if len(outs) > 1:
            merge(other, total, outs[1])

    @pl.when(jnp.logical_not(later))
    def _():
        if first:
            outs[0][0:N, :] = jnp.zeros((N, total.shape[1]), F32)
            outs[0][N:, :] = jnp.ones((8, total.shape[1]), F32)
        else:
            outs[0][...] = before[...]
        if len(outs) > 1:
            merge(total, other, outs[1])


def carried_in(total, backward, place, beside=()):
    before, firsts = [], []
    shape = total.shape
    masks = powers(lax.axis_size("tok"))
    for mask in masks:
        other = swap(total, "tok", mask)
        ins = [total, other if before else after(other, *beside), *before]
        last = mask == masks[-1]
        found = call(
            functools.partial(k_merge, mask, backward, not before),
            1,
            [(a, whole(shape)) for a in ins],
            [(shape, F32, whole(shape))] * (1 if last else 2),
            [],
            10**6,
            "merge",
            place,
        )
        before, total = [found[0]], found[-1]
        firsts.append(found[0])
    return before[0], firsts[0]


def exchange(pieces, axis):
    return lax.all_to_all(pieces, axis, 0, 0, tiled=True)


def distances(value, axis, step):
    return [value] + [swap(value, axis, step * k) for k in range(1, lax.axis_size(axis) // step)]


def head_gathered(value):
    found = [value]
    masks = powers(lax.axis_size("head"))
    for mask in masks[1:] + masks[:1]:
        found = found + [swap(a, "head", mask) for a in found]
    return found


def on_device(
    hidden_in, norm_gain, w_zx, w_bc, w_dt, dt_bias, a_log, conv_x, conv_bc, d_skip, gate_gain,
    w_out, out_grad, group_first, group_valid,
):
    tokens, dim = hidden_in.shape
    real = w_zx.shape[2]
    own_heads = real // P_SIZE
    heads = w_dt.shape[1]
    groups = tokens // GROUP
    chunks = groups * PARTS
    width = -(-real // LANES) * LANES
    extra = width - real
    conv_width = width + 2 * N
    tok_count = lax.axis_size("tok")
    head_count = lax.axis_size("head")
    head_start = lax.axis_index("head") * own_heads

    def wide(a, dim_at, by=extra):
        return jnp.pad(a, [(0, by if k == dim_at else 0) for k in range(a.ndim)]) if by else a

    route = [(i - 1, i) for i in range(1, tok_count)]
    rim = lax.ppermute(hidden_in[tokens - 16 :], "tok", route)
    flat_zx = wide(w_zx, 2).reshape(dim, 2 * width)
    w_o = wide(w_out, 0)
    w_dt_here = wide(lax.dynamic_slice_in_dim(w_dt, head_start, own_heads, 1), 1, LANES - own_heads)
    per_head = jnp.stack([dt_bias, a_log, d_skip])
    per_head = lax.dynamic_slice_in_dim(per_head, head_start, own_heads, 1)
    per_head = jnp.pad(per_head, ((0, 5), (0, LANES - own_heads)))
    cx = wide(conv_x, 1)
    gain_in = norm_gain[None, :]
    gain_gate = wide(gate_gain, 0)[None, :]
    at_head = lax.axis_index("head")
    place = jnp.stack([at_head & 1, head_start, at_head, lax.axis_index("tok")]).astype(jnp.int32)
    hidden_in, place, flat_zx, w_o, w_dt_here, per_head, cx, gain_in, gain_gate = lax.optimization_barrier(
        (hidden_in, place, flat_zx, w_o, w_dt_here, per_head, cx, gain_in, gain_gate)
    )
    part_z, part_x = [
        (flat_zx, pl.BlockSpec((dim, width), lambda i, *s, side=side: (0, side))) for side in range(2)
    ]
    w_outs = head_gathered(w_o)

    def rows(a, at=None):
        return (a, row_block(a.shape, GROUP, at))

    def full(a):
        return (a, whole(a.shape))

    def kept(a, at=None):
        return (a, Kept(GROUP, at))

    def per_chunk(a, at=None):
        return (a, Kept(PARTS, at))

    def out_rows(cols, dtype, at=None):
        return ((tokens, cols), dtype, row_block((tokens, cols), GROUP, at))

    def out_kept(cols, dtype, at=None):
        return ((tokens, cols), dtype, Kept(GROUP, at))

    def out_full(shape, dtype):
        return (shape, dtype, whole(shape))

    def out_chunk(shape, dtype, at=None):
        return ((chunks,) + shape, dtype, Kept(PARTS, at))

    carry = (N + 8, width)
    h, v, pre, vprev, cvlead, xs, bc, dt, cum, ent, pd, fin = call(
        k_front,
        groups,
        [
            (group_first, SMEM), (group_valid, SMEM), far(rows(hidden_in)), full(rim), full(gain_in),
            part_x, full(w_bc), full(w_dt_here), full(per_head), full(cx), full(conv_bc),
        ],
        [
            out_kept(dim, BF16), out_kept(conv_width, F32), out_kept(LANES, F32),
            ((groups, 8, conv_width), F32, Kept(1)), ((groups, 16, conv_width), F32, Kept(1)), out_kept(width, BF16), out_kept(2 * N, BF16),
            out_kept(LANES, F32), out_kept(LANES, F32), out_chunk((N, width), F32),
            out_chunk((1, width), F32), out_full(carry, F32),
        ],
        [
            pltpu.VMEM((GROUP + 8, conv_width), F32), pltpu.VMEM((N, width), F32),
            pltpu.VMEM((8, width), F32),
        ],
        4 * 10**9,
        "front",
    )
    prev, _ = carried_in(fin, False, place)
    silu, slope, gyn = call(
        k_proj,
        groups,
        [kept(h), rows(after(out_grad, fin)), part_z, full(w_o)],
        [out_kept(width, F32)] * 3,
        [],
        5 * 10**9,
        "proj",
    )
    yw, ecum = call(
        k_within,
        groups,
        [kept(xs), kept(bc), kept(dt), kept(cum)],
        [out_kept(width, F32)] * 2,
        [],
        5 * 10**9,
        "within",
    )
    mix, entry, sums = call(
        k_gate,
        groups,
        [
            per_chunk(ent), per_chunk(pd), full(after(prev, *w_outs)), kept(bc), kept(ecum), kept(yw), kept(xs),
            kept(silu), kept(gyn), full(gain_gate), full(per_head),
        ],
        [
            out_kept(width, F32), out_chunk((N, width), F32),
            ((2, tokens), F32, pl.BlockSpec((2, GROUP), lambda i: (0, i))),
        ],
        [],
        3 * 10**9,
        "gate",
    )
    sums = [sums] + [swap(sums, "head", mask) for mask in range(1, head_count)]

    def back(i):
        return groups - 1 - i

    yn, gm, gz, ds, qd, acc_gain, acc_skip, fin_back = call(
        functools.partial(k_gate_back, float(heads * P_SIZE), head_count),
        groups,
        [
            (group_first, SMEM), kept(mix, back), kept(silu, back), kept(slope, back), kept(gyn, back), full(gain_gate),
            kept(xs, back), kept(bc, back), kept(ecum, back),
        ]
        + [(a, pl.BlockSpec((2, GROUP), lambda i: (0, groups - 1 - i))) for a in sums],
        [
            out_kept(width, BF16, back), out_kept(width, BF16, back), out_kept(width, BF16, back),
            out_chunk((N, width), F32, back), out_chunk((1, width), F32, back),
            out_full((8, width), F32), out_full((8, width), F32), out_full(carry, F32),
        ],
        [pltpu.VMEM((N, width), F32), pltpu.VMEM((8, width), F32)],
        3 * 10**9,
        "gate_back",
    )
    yns = [yn]
    for mask in powers(head_count)[1:]:
        yns = yns + [swap(a, "head", mask) for a in yns]
    rows_z, rows_o = dim // tok_count, width // tok_count
    piece_a = (rows_z * width + rows_o * dim) // LANES
    sides = tok_count // 2
    keep_a, send_a = call(
        k_weights,
        groups,
        [kept(yn), rows(out_grad), kept(h), kept(gz)],
        [out_full((sides, piece_a, LANES), F32)] * 2,
        [pltpu.VMEM((dim, width), F32), pltpu.VMEM((width, dim), F32)],
        3 * 10**9,
        "weights",
        place,
        4,
    )
    end_grad, first_grad = carried_in(fin_back, True, place, (keep_a,))
    arrived_a = swap(after(send_a, first_grad), "tok", 1)
    per_token = [
        out_kept(width, F32), out_kept(2 * N, F32), out_kept(LANES, F32), out_kept(LANES, F32)
    ]
    inner = [kept(xs), kept(bc), kept(after(gm, keep_a)), kept(dt), kept(cum), kept(mix), per_chunk(entry), full(per_head)]
    dxw, dbc, rq, qw = call(
        k_within_back, groups, inner, per_token, [], 10 * 10**9, "within_back", None, 4
    )

    def leading(a):
        per = GROUP // 16
        return (a, Kept(16, lambda i: i * per))

    rims, lead = call(
        k_rim,
        groups,
        [
            (group_first, SMEM), leading(xs), leading(bc), leading(gm), leading(dt), leading(cum),
            (cum, Kept(8, lambda i: i * (GROUP // 8) + CHUNK // 8 - 1)),
            leading(dxw), leading(dbc), (cvlead, Kept(1)),
            (ds, Kept(1, lambda i: i * PARTS)),
            (qd, Kept(1, lambda i: i * PARTS)),
            full(end_grad), full(per_head),
        ],
        [((groups, 16, conv_width), F32, Kept(1)), out_full((8, conv_width), F32)],
        [],
        10**9,
        "rim",
    )
    rim_in = lax.ppermute(lead, "tok", [(i, i - 1) for i in range(1, tok_count)])
    at_head = lax.axis_index("head")
    place = jnp.stack([at_head & 1, head_start, at_head, lax.axis_index("tok")]).astype(jnp.int32)
    pairs_a = call(
        k_pair,
        1,
        [full(after(keep_a, lead)), full(arrived_a)],
        [out_full((piece_a, LANES), BF16)] * sides,
        [],
        10**6,
        "pair",
        place,
    )
    arrived_a = [pairs_a[0]] + [swap(pairs_a[k], "tok", 2 * k) for k in range(1, sides)]
    half = groups // 2
    piece_b = rows_z * width // LANES
    tiles = width // LANES
    count = head_count * tok_count
    each = -(-2 * dim // (16 * count)) * 16
    rest = -(-(heads * dim // LANES + 16 + head_count * 8 * tiles) // (8 * count)) * 8
    slots = (count, each, rest)
    small_rows = count * (each + rest)
    acc_shapes = [(dim, width), (dim, 2 * N), (heads, dim), (8 * KCONV + 8, conv_width), (16, LANES)]

    def back_call(final, more_in, more_out, more_scratch, alias, ready):
        def at(i, *s):
            return i + half if final else i

        return call(
            functools.partial(k_back, final, slots),
            half,
            [(group_valid, SMEM)]
            + [
                kept(a, at)
                for a in (after(h, *ready), xs, bc, gm, pre, dt, cum, v)
            ]
            + [(vprev, Kept(1, at))]
            + [
                kept(a, at)
                for a in (dxw, dbc, rq, qw)
            ]
            + [per_chunk(entry, at), per_chunk(ds, at), per_chunk(qd, at), full(end_grad)]
            + [(rims, Kept(1, lambda i, s: jnp.minimum(at(i) + 1, groups - 1)))]
            + [full(cx), full(conv_bc), full(per_head)]
            + more_in,
            [out_kept(width, BF16, at), out_kept(4 * N, BF16, at), out_kept(LANES, BF16, at)]
            + [(a, F32, VMEM) for a in acc_shapes]
            + more_out,
            [pltpu.VMEM((GROUP + 8, conv_width), F32)] * 2 + more_scratch,
            5 * 10**9,
            "back_end" if final else "back_start",
            place,
            4,
            alias,
        )

    partial = back_call(False, [], [], [], (), (pairs_a[0],))
    (total_a,) = call(
        k_reduce, 1, [full(after(a, partial[0])) for a in arrived_a], [out_full((piece_a, LANES), BF16)],
        [], 10**6, "reduce",
    )
    found = back_call(
        True,
        [full(rim_in), full(acc_gain), full(acc_skip)] + [(a, VMEM) for a in partial],
        [
            out_full((tok_count, piece_b, LANES), BF16), out_full((small_rows // 2, LANES), F32),
            out_full((small_rows // 2, LANES), F32),
        ],
        [pltpu.VMEM((small_rows, LANES), F32)],
        [(25 + k, k) for k in range(8)],
        (total_a, yns[1]),
    )
    gx, gbc, gpre = found[:3]
    grads_b, small_keep, small_send = found[8:]
    parts_a = distances(total_a, "tok", 2)
    (mine_a,) = call(
        k_join, 1, [full(after(a, gx)) for a in parts_a], [out_full((sides, piece_a, LANES), BF16)], [],
        10**6, "join", place,
    )

    cuts = 2
    steps = half // cuts
    shape = (tokens // 2 // cuts, dim)

    def input_call(own, k, norm, more, ready):
        def turned(i, s):
            return i + k * steps + half * (s[0] if own else 1 - s[0])

        ends = own and k == cuts - 1
        return call(
            functools.partial(k_input, norm is None, own, ends),
            steps,
            [rows(hidden_in, turned)]
            + [kept(a, turned) for a in (gz, gx, gbc, after(gpre, *ready))]
            + [part_z, part_x, full(w_bc), full(w_dt_here)]
            + [rows(a) for a in more]
            + ([] if norm is None else [full(norm)]),
            [
                (shape, BF16 if own else F32, row_block(shape, GROUP)),
                out_full((8, LANES if ends else dim), F32),
            ],
            [pltpu.VMEM((8, dim), F32)],
            10**9,
            "input_own" if own else "input_sent",
            place,
        )

    sent, norm = input_call(False, 0, None, [], (mine_a,))
    arrived = [swap(sent, "head", 1)]
    small_arrived = after(swap(after(small_send, mine_a), "head", 1), sent)
    for mask in powers(head_count)[1:]:
        small_shape = (small_keep.shape[0] // 2, LANES)
        small_keep, small_send = call(
            functools.partial(k_halve, mask), 1, [full(small_keep), full(small_arrived)],
            [out_full(small_shape, F32)] * 2, [], 10**6, "halve", place,
        )
        small_arrived = swap(small_send, "head", mask)
    for k in range(1, cuts):
        sent, norm = input_call(False, k, norm, [], (mine_a, small_keep))
        arrived.append(swap(sent, "head", 1))
    parts = []
    for k in range(cuts):
        part, norm = input_call(True, k, norm, [arrived[k]], (mine_a,))
        found = [part]
        for mask in powers(head_count)[1:]:
            found = found + [swap(a, "head", mask) for a in found]
        parts.append(found)

    shape = (tok_count, piece_b + each + 2 * (rest + 8), LANES)
    (pieces,) = call(
        functools.partial(k_pieces, slots), 1, [full(small_keep), full(small_arrived), full(norm), full(grads_b)],
        [out_full(shape, BF16)], [], 10**6, "pieces",
    )
    yns = yns + [swap(after(a, pieces), "head", 1) for a in yns]
    (block_out,) = call(
        k_out,
        groups,
        [rows(after(hidden_in, pieces))] + [rows(a) for a in yns] + [full(a) for a in w_outs],
        [out_rows(dim, BF16)],
        [],
        5 * 10**9,
        "out",
    )

    (copies,) = call(
        functools.partial(k_reduce_both, piece_b + each), 1,
        [full(after(exchange(pieces, "tok"), block_out))],
        [out_full(shape, BF16)], [], 10**6, "reduce_both",
    )
    sum_b = exchange(copies, "tok")
    other_a = swap(after(mine_a, copies), "tok", 1)
    (tick,) = call(
        k_tick, 1, [(copies, row_block(copies.shape, 1))], [out_full((16, LANES), BF16)], [], 1, "tick"
    )
    (grad_w_out,) = call(
        k_unpack_out, 1, [full(mine_a), full(other_a)], [out_full((width, dim), F32)],
        [], 10**6, "unpack_out", place,
    )
    others = [
        [swap(found[0], "head", 1)] + [swap(after(a, tick), "head", 1) for a in found[1:]]
        for found in parts
    ]

    def turned_back(i, s):
        return lax.rem(i + half * s[0], groups)

    def in_cut(a, k):
        return (a, row_block(a.shape, GROUP, lambda i, s: jnp.clip(i - k * steps, 0, steps - 1)))

    (grad_in,) = call(
        functools.partial(k_in_back, steps),
        groups,
        [far(rows(hidden_in, turned_back)), far(rows(out_grad, turned_back)), full(gain_in)]
        + [in_cut(a, k) for k, found in enumerate(parts + others) for a in found],
        [out_rows(dim, F32, turned_back)],
        [],
        10**9,
        "in_back",
        place,
    )
    shape = (tok_count * (each + 2 * (rest + 8)), LANES)
    (quarter,) = call(
        functools.partial(k_quarter, piece_b), 1, [full(after(sum_b, grad_in))], [out_full(shape, BF16)],
        [], 10**6, "quarter",
    )
    quarters = [(quarter, 0)]
    for mask in powers(head_count):
        quarters = quarters + [(swap(a, "head", mask), k | mask) for a, k in quarters]
    quarters = [a for a, _ in sorted(quarters, key=lambda item: item[1])]

    (grad_w_zx,) = call(
        k_unpack,
        1,
        [full(mine_a), full(other_a), full(sum_b)],
        [out_full((dim, 2, real), F32)],
        [],
        10**6,
        "unpack",
        place,
    )
    grad_w_bc, grad_w_dt, grad_taps, grad_bias, grad_alog, grad_skip, grad_norm, own_taps, own_gain = call(
        functools.partial(k_small, slots),
        1,
        [full(a) for a in quarters],
        [
            out_full((dim, 2 * N), F32), out_full((heads, dim), F32), out_full((KCONV + 1, 2 * N), F32),
            out_full((1, heads), F32), out_full((1, heads), F32), out_full((1, heads), F32),
            out_full((1, dim), F32), out_full((KCONV + 1, real), F32), out_full((1, real), F32),
        ],
        [pltpu.VMEM((small_rows, LANES), F32)],
        10**6,
        "small",
        place,
    )

    return (
        block_out,
        grad_in,
        grad_norm[0],
        grad_w_zx,
        grad_w_bc,
        grad_w_dt.T,
        grad_bias[0],
        grad_alog[0],
        own_taps,
        grad_taps,
        grad_skip[0],
        own_gain[0],
        grad_w_out[:real],
    )


def solution(mesh):
    return jax.shard_map(
        on_device,
        mesh=mesh,
        in_specs=(
            P("tok", None), P(), P(None, None, "head"), P(), P(), P(), P(), P(None, "head"), P(), P(),
            P("head"), P("head", None), P("tok", None), P("tok"), P("tok"),
        ),
        out_specs=(
            P("tok", None), P("tok", None), P(), P(None, None, "head"), P(), P(), P(), P(),
            P(None, "head"), P(), P(), P("head"), P("head", None),
        ),
        check_vma=False,
    )
```

```python
import functools
import math

import jax
import jax.numpy as jnp
from jax import lax
from jax.experimental import pallas as pl
from jax.experimental.pallas import tpu as pltpu
from jax.sharding import PartitionSpec as P

P_SIZE = 64
N = 128
KCONV = 4
GROUP = 256
CHUNK = 128
LANES = 128
PARTS = GROUP // CHUNK
EPS = 1e-05
VMEM_LIMIT = 10 * 1024 * 1024
F32 = jnp.float32
BF16 = jnp.bfloat16


def mm(a, b, ca=1, cb=0):
    return lax.dot_general(a, b, (((ca,), (cb,)), ((), ())), preferred_element_type=F32)


def iota(shape, dim):
    return lax.broadcasted_iota(jnp.int32, shape, dim)


def spread(cols, width):
    rows = cols.shape[0]
    low = iota((rows, LANES), 1) < P_SIZE
    tiles = [
        jnp.where(low, cols[:, 2 * p : 2 * p + 1], cols[:, 2 * p + 1 : 2 * p + 2])
        for p in range(width // LANES)
    ]
    return jnp.concatenate(tiles, axis=1)


def gather_heads(width):
    return (iota((width, LANES), 0) // P_SIZE == iota((width, LANES), 1)).astype(BF16)


def fold_rows(value):
    rows, width = value.shape
    return value.reshape(rows // 8, 8, width).sum(axis=0)


def tri(kind):
    row, col = iota((CHUNK, CHUNK), 0), iota((CHUNK, CHUNK), 1)
    return {"le": col <= row, "ge": col >= row, "lt": col < row}[kind]


def pair_rows(tile):
    low = iota(tile.shape, 1) < P_SIZE
    zero = jnp.zeros_like(tile)
    return jnp.concatenate([jnp.where(low, tile, zero), jnp.where(low, zero, tile)], axis=0)


def split2(value):
    high = value.astype(BF16)
    return high, (value - high.astype(F32)).astype(BF16)


def split3(value):
    high, rest = split2(value)
    return high, rest, (value - high.astype(F32) - rest.astype(F32)).astype(BF16)


def mm_left(a, b, ca=1, cb=0):
    high, low = split2(a)
    return mm(high, b, ca, cb) + mm(low, b, ca, cb)


def mm_right(a, b, ca=1, cb=0):
    high, low = split2(b)
    if ca == 0:
        both = mm(a, jnp.concatenate([high, low], axis=1), ca, cb)
        return both[:, : b.shape[1]] + both[:, b.shape[1] :]
    return mm(a, high, ca, cb) + mm(a, low, ca, cb)


def mm_both(a, b, ca=1, cb=0):
    ah, al = split2(a)
    bh, bl = split2(b)
    return mm(ah, bh, ca, cb) + mm(al, bh, ca, cb) + mm(ah, bl, ca, cb)


def stacked(value):
    return jnp.concatenate(
        [value[:, c : c + LANES] for c in range(0, value.shape[1], LANES)], axis=0
    )


def tree(terms):
    while len(terms) > 1:
        terms = [terms[k] + terms[k + 1] for k in range(0, len(terms), 2)]
    return terms[0]


def rms_inv(u):
    return lax.rsqrt(jnp.mean(u * u, axis=1, keepdims=True) + EPS)


def k_front(
    first, valid, hid, rim, gain, w_x, w_bc, w_dt, hp, cx, cb,
    h_o, v_o, pre_o, prev_o, lead_o, xs_o, bc_o, dt_o, cum_o, ent_o, pd_o, fin_o,
    vbuf, state, decay,
):
    g = pl.program_id(0)
    width = w_x.shape[1]

    def normed(block):
        u = block.astype(F32)
        return (u * rms_inv(u) * gain[...]).astype(BF16)

    @pl.when(g == 0)
    def _():
        hr = normed(rim[...])
        vbuf[0:8, :width] = mm(hr, w_x[...])[8:16]
        vbuf[0:8, width:] = mm(hr, w_bc[...])[8:16]
        state[...] = jnp.zeros_like(state)
        decay[...] = jnp.ones_like(decay)

    keep = 1.0 - first[g].astype(F32)
    vbuf[0:8, :] = vbuf[0:8, :] * keep
    state[...] = state[...] * keep
    decay[...] = decay[...] * keep
    h = normed(hid[...])
    h_o[...] = h
    raw = mm(h, w_dt[...]) + hp[0:1, :]
    pre_o[...] = raw
    vbuf[8:, :width] = mm(h, w_x[...])
    vbuf[8:, width:] = mm(h, w_bc[...])
    v_o[...] = vbuf[8:, :]
    taps = jnp.concatenate([cx[...], cb[...]], axis=1)
    conv = taps[KCONV : KCONV + 1, :] + taps[0:1, :] * vbuf[5 : 5 + GROUP, :]
    for k in range(1, KCONV):
        conv = conv + taps[k : k + 1, :] * vbuf[5 + k : 5 + k + GROUP, :]
    prev_o[0] = vbuf[0:8, :]
    lead_o[0] = conv[0:16, :]
    act = (conv * jax.nn.sigmoid(conv)).astype(BF16)
    xs_o[...] = act[:, :width]
    bc_o[...] = act[:, width:]
    vbuf[0:8, :] = vbuf[GROUP : GROUP + 8, :]
    live = iota((GROUP, LANES), 0) < valid[g]
    soft = jnp.maximum(raw, 0.0) + jnp.log1p(jnp.exp(-jnp.abs(raw)))
    dt = jnp.where(live, soft, 0.0)
    dt_o[...] = dt
    ld = dt * -jnp.exp(hp[1:2, :])
    lower = tri("le").astype(BF16)
    lower = jnp.concatenate([lower] * 3, axis=1)
    for c in range(PARTS):
        rows = slice(c * CHUNK, (c + 1) * CHUNK)
        cum = mm(lower, jnp.concatenate(split3(ld[rows]), axis=0))
        cum_o[rows, :] = cum
        end = cum[CHUNK - 1 : CHUNK, :]
        factor = dt[rows] * jnp.exp(end - cum)
        ent_o[c] = state[...]
        pd_o[c] = decay[0:1]
        xd = act[rows, :width].astype(F32) * spread(factor, width)
        new = mm_right(act[rows, width : width + N], xd, 0, 0)
        ec = spread(jnp.exp(end), width)
        state[...] = state[...] * ec + new
        decay[...] = decay[...] * ec

    @pl.when(g == pl.num_programs(0) - 1)
    def _():
        fin_o[0:N, :] = state[...]
        fin_o[N:, :] = decay[...]


def k_proj(h, og, w_z, w_out, silu_o, slope_o, gyn_o):
    z = mm(h[...], w_z[...])
    sig = jax.nn.sigmoid(z)
    silu_o[...] = z * sig
    slope_o[...] = sig * (1.0 + z * (1.0 - sig))
    gyn_o[...] = mm(og[...], w_out[...], 1, 1)


def k_within(xs, bc, dt, cum, y_o, ecum_o):
    width = xs.shape[1]
    mask = tri("le")
    for c in range(PARTS):
        rows = slice(c * CHUNK, (c + 1) * CHUNK)
        scores = mm(bc[rows, N:], bc[rows, :N], 1, 1)
        a = cum[rows, :]
        ecum_o[rows, :] = spread(jnp.exp(a), width)
        b = jnp.transpose(a - jnp.log(dt[rows, :]))
        for p in range(width // LANES):
            lanes = slice(p * LANES, (p + 1) * LANES)
            weights = []
            for h in (2 * p, 2 * p + 1):
                gap = a[:, h : h + 1] - b[h : h + 1, :]
                weights.append(jnp.where(mask, jnp.exp(gap), 0.0) * scores)
            y_o[rows, lanes] = mm_left(jnp.concatenate(weights, axis=1), pair_rows(xs[rows, lanes]))


def k_gate(ent, pd, prev, bc, ecum, yw, xs, silu, gyn, gain, hp, mix_o, ent_o, sums_o):
    width = xs.shape[1]
    skip = spread(hp[2:3, :], width)
    for c in range(PARTS):
        rows = slice(c * CHUNK, (c + 1) * CHUNK)
        entry = ent[c] + pd[c] * prev[0:N, :]
        ent_o[c] = entry
        across = mm_right(bc[rows, N:], entry) * ecum[rows, :]
        mix_o[rows, :] = yw[rows, :] + across + skip * xs[rows, :].astype(F32)
    gated = mix_o[...] * silu[...]
    square = jnp.sum(gated * gated, axis=1, keepdims=True)
    inner = jnp.sum(gyn[...] * gain[...] * gated, axis=1, keepdims=True)
    lane = iota((GROUP, LANES), 1)
    both = jnp.where(lane == 0, square, inner)
    sums_o[...] = jnp.transpose(both)[0:2, :]


def k_gate_back(
    total, count, first, mix, silu, slope, gyn, gain, xs, bc, ecum, *rest,
):
    sums = rest[:count]
    yn_o, g_o, gz_o, ds_o, qd_o, again_o, askip_o, fin_o, state, decay = rest[count:]
    i = pl.program_id(0)
    g = pl.num_programs(0) - 1 - i
    width = xs.shape[1]

    @pl.when(i == 0)
    def _():
        state[...] = jnp.zeros_like(state)
        decay[...] = jnp.ones_like(decay)
        again_o[...] = jnp.zeros_like(again_o)
        askip_o[...] = jnp.zeros_like(askip_o)

    rows2 = tree([part[...] for part in sums])
    both = jnp.transpose(jnp.concatenate([rows2, jnp.zeros((LANES - 2, GROUP), F32)], axis=0))
    inv = lax.rsqrt(both[:, 0:1] / total + EPS)
    inner = both[:, 1:2] / total
    silu = silu[...]
    mixer = mix[...]
    gated = mixer * silu
    scaled = gated * inv
    gy = gyn[...]
    gn = gain[...]
    yn_o[...] = (scaled * gn).astype(BF16)
    again_o[...] += fold_rows(gy * scaled)
    gg = inv * gn * gy - gated * (inv * inv * inv * inner)
    gm = (gg * silu).astype(BF16)
    g_o[...] = gm
    gz_o[...] = (gg * mixer * slope[...]).astype(BF16)
    gmf = gm.astype(F32)
    askip_o[...] += fold_rows(gmf * xs[...].astype(F32))
    for c in reversed(range(PARTS)):
        rows = slice(c * CHUNK, (c + 1) * CHUNK)
        ds_o[c] = state[...]
        qd_o[c] = decay[0:1]
        new = mm_right(bc[rows, N:], gmf[rows] * ecum[rows, :], 0, 0)
        ec = ecum[(c + 1) * CHUNK - 1 : (c + 1) * CHUNK, :]
        state[...] = state[...] * ec + new
        decay[...] = decay[...] * ec
    keep = 1.0 - first[g].astype(F32)
    state[...] = state[...] * keep
    decay[...] = decay[...] * keep

    @pl.when(i == pl.num_programs(0) - 1)
    def _():
        fin_o[0:N, :] = state[...]
        fin_o[N:, :] = decay[...]


def k_weights(place, yn, og, h, gz, keep_o, send_o, acc_z, acc_out):
    i = pl.program_id(0)

    @pl.when(i == 0)
    def _():
        acc_z[...] = jnp.zeros_like(acc_z)
        acc_out[...] = jnp.zeros_like(acc_out)

    acc_z[...] += mm(h[...], gz[...], 0, 0)
    acc_out[...] += mm(yn[...], og[...], 0, 0)

    @pl.when(i == pl.num_programs(0) - 1)
    def _():
        count = keep_o.shape[0]
        rz, ro = acc_z.shape[0] // (2 * count), acc_out.shape[0] // (2 * count)
        side = place[3] % 2
        for k in range(count):
            for out, at in ((keep_o, 2 * k + side), (send_o, 2 * k + 1 - side)):
                out[k] = jnp.concatenate(
                    [
                        stacked(acc_z[pl.ds(pl.multiple_of(at * rz, 8), rz), :]),
                        stacked(acc_out[pl.ds(pl.multiple_of(at * ro, 8), ro), :]),
                    ],
                    axis=0,
                )


def k_pair(place, keep, arrived, *outs):
    for k, out in enumerate(outs):
        at = (place[3] // 2) ^ k
        out[...] = (keep[at] + arrived[at]).astype(BF16)


def k_join(place, *refs):
    out = refs[-1]
    for k, part in enumerate(refs[:-1]):
        out[(place[3] // 2) ^ k] = part[...]


def k_within_back(
    xs, bc, g, dt, cum, mix, ent, hp,
    dxw_o, dbc_o, rq_o, qw_o,
):
    width = xs.shape[1]
    mask = tri("ge")
    heads = gather_heads(width)
    skip = spread(hp[2:3, :], width)
    for c in range(PARTS):
        rows = slice(c * CHUNK, (c + 1) * CHUNK)
        bw, cr = bc[rows, :N], bc[rows, N:]
        scores = mm(bw, cr, 1, 1)
        a = cum[rows, :]
        b = a - jnp.log(dt[rows, :])
        at = jnp.transpose(a)
        dscore = jnp.zeros((CHUNK, CHUNK), F32)
        for p in range(width // LANES):
            lanes = slice(p * LANES, (p + 1) * LANES)
            decays = [
                jnp.where(mask, jnp.exp(at[h : h + 1, :] - b[:, h : h + 1]), 0.0)
                for h in (2 * p, 2 * p + 1)
            ]
            gt = g[rows, lanes]
            pairs = mm(pair_rows(xs[rows, lanes]), gt, 1, 1)
            dscore = dscore + pairs[:CHUNK] * decays[0] + pairs[CHUNK:] * decays[1]
            weights = jnp.concatenate([d * scores for d in decays], axis=1)
            dxw_o[rows, lanes] = mm_left(weights, pair_rows(gt))
        high, low = split2(dscore)
        gf = g[rows, :].astype(F32)
        xf = xs[rows, :].astype(F32)
        ge = gf * spread(jnp.exp(a), width)
        dbc_o[rows, :N] = mm(high, cr) + mm(low, cr)
        dbc_o[rows, N:] = mm(high, bw, 0, 0) + mm(low, bw, 0, 0) + mm_both(ge, ent[c], 1, 1)
        row_part = mm_left(gf * (mix[rows, :] - skip * xf), heads)
        col_part = mm_left(xf * dxw_o[rows, :], heads)
        rq_o[rows, :] = row_part - col_part
        qw_o[rows, :] = col_part


def silu_slope(value):
    sig = jax.nn.sigmoid(value)
    return sig * (1.0 + value * (1.0 - sig))


def k_rim(first, xs, bc, g, dt, cum, cend, dxw, dbc, cv, ds, qd, endg, hp, out, lead_o):
    i = pl.program_id(0)
    width = xs.shape[1]
    d_state = ds[0] + qd[0] * endg[0:N, :]
    factor = spread(dt[...] * jnp.exp(cend[7:8, :] - cum[...]), width)
    skip = spread(hp[2:3, :], width)
    xd = xs[...].astype(F32) * factor
    gx = dxw[...] + factor * mm_right(bc[:, :N], d_state) + g[...].astype(F32) * skip
    gb = dbc[:, :N] + mm_both(xd, d_state, 1, 1)
    slope = silu_slope(cv[0]) * (1.0 - first[i].astype(F32))
    out[0, :, :width] = gx * slope[:, :width]
    out[0, :, width : width + N] = gb * slope[:, width : width + N]
    out[0, :, width + N :] = dbc[:, N:] * slope[:, width + N :]

    @pl.when(i == 0)
    def _():
        lead_o[...] = out[0, 0:8, :]


def k_back(final, slots, n_heads, place, *refs):
    (
        valid, h, xs, bc, g, pre, dt, cum, v, vprev, dxw, dbc, rq, qw, ent, ds, qd, endg, rims, cx, cb, hp,
    ) = refs[:22]
    if final:
        rim_in, acc_gain, acc_skip = refs[22:25]
        gx_o, gbc_o, gpre_o = refs[33:36]
        acc_x, acc_bc, acc_dt, acc_taps, acc_heads = refs[36:41]
        grads_o, keep_o, send_o, gbuf, vbuf, small_o = refs[41:]
    else:
        gx_o, gbc_o, gpre_o, acc_x, acc_bc, acc_dt, acc_taps, acc_heads, gbuf, vbuf = refs[22:]
    i = pl.program_id(0)
    last = pl.num_programs(0) - 1
    group = i + pl.num_programs(0) if final else i
    width = xs.shape[1]
    heads = gather_heads(width)
    skip = spread(hp[2:3, :], width)
    rate = -jnp.exp(hp[1:2, :])

    if not final:

        @pl.when(i == 0)
        def _():
            for ref in (acc_x, acc_bc, acc_dt, acc_taps, acc_heads):
                ref[...] = jnp.zeros_like(ref)

    upper, below = tri("ge").astype(BF16), tri("lt").astype(BF16)
    both = jnp.concatenate([upper, upper, below, below], axis=1)
    taps = jnp.concatenate([cx[...], cb[...]], axis=1)
    vbuf[0:8, :] = vprev[0]
    vbuf[8:, :] = v[...]
    for c in range(PARTS):
        rows = slice(c * CHUNK, (c + 1) * CHUNK)
        d_state = ds[c] + qd[c] * endg[0:N, :]
        d_high, d_low = split2(d_state)
        a = cum[rows, :]
        end = a[CHUNK - 1 : CHUNK, :]
        factor = spread(dt[rows, :] * jnp.exp(end - a), width)
        xf = xs[rows, :].astype(F32)
        bw = bc[rows, :N]
        dxs = factor * (mm(bw, d_high) + mm(bw, d_low))
        x_high, x_low = split2(xf * factor)
        gb = dbc[rows, :N] + (mm(x_high, d_high, 1, 1) + mm(x_low, d_high, 1, 1) + mm(x_high, d_low, 1, 1))
        gx = dxw[rows, :] + dxs + g[rows, :].astype(F32) * skip
        conv = taps[KCONV : KCONV + 1, :]
        for k in range(KCONV):
            start = 5 + k + c * CHUNK
            conv = conv + taps[k : k + 1, :] * vbuf[start : start + CHUNK, :]
        slope = silu_slope(conv)
        gbuf[rows, :width] = gx * slope[:, :width]
        gbuf[rows, width : width + N] = gb * slope[:, width : width + N]
        gbuf[rows, width + N :] = dbc[rows, N:] * slope[:, width + N :]
        qs = mm_left(xf * dxs, heads)
        carried = mm_left(fold_rows(d_state * ent[c]), heads)
        ends = jnp.sum(carried, axis=0, keepdims=True) * jnp.exp(end)
        g_ld = mm(both, jnp.concatenate(split2(rq[rows, :]) + split2(qs), axis=0)) + ends
        step = dt[rows, :]
        direct = jnp.where(step > 0.0, (qw[rows, :] + qs) / jnp.where(step > 0.0, step, 1.0), 0.0)
        live = iota((CHUNK, LANES), 0) + c * CHUNK < valid[group]
        own = iota((CHUNK, LANES), 1) < width // P_SIZE
        g_pre = jnp.where(
            live & own, (direct + g_ld * rate) * jax.nn.sigmoid(pre[rows, :]), 0.0
        )
        acc_heads[0:8, :] += fold_rows(g_pre)
        acc_heads[8:16, :] += fold_rows(g_ld * step * rate)
        low = g_pre.astype(BF16)
        gpre_o[rows, :] = low

    gbuf[GROUP:, :] = rims[0, 0:8, :]
    if final:

        @pl.when(i == last)
        def _():
            gbuf[GROUP:, :] = rim_in[0:8, :]

    vv = v[...]
    gv = jnp.zeros_like(vv)
    for k in range(KCONV):
        shifted = gbuf[KCONV - 1 - k : KCONV - 1 - k + GROUP, :]
        gv = gv + taps[k : k + 1, :] * shifted
        acc_taps[8 * k : 8 * k + 8, :] += fold_rows(vv * shifted)
    acc_taps[8 * KCONV :, :] += fold_rows(gbuf[0:GROUP, :])
    gx_low = gv[:, :width].astype(BF16)
    bc_high, bc_low = split2(gv[:, width:])
    gx_o[...] = gx_low
    gbc_o[:, : 2 * N] = bc_high
    gbc_o[:, 2 * N :] = bc_low
    hh = h[...]
    moved = pltpu.roll(gpre_o[...].astype(F32), place[1], 1).astype(BF16)
    both = mm(hh, jnp.concatenate([gx_low, moved], axis=1), 0, 0)
    acc_x[...] += both[:, :width]
    acc_dt[...] += both[:, width:]
    both = mm(hh, jnp.concatenate([bc_high, bc_low], axis=1), 0, 0)
    acc_bc[...] += both[:, : 2 * N] + both[:, 2 * N :]
    if not final:
        return

    @pl.when(i == last)
    def _():
        count = grads_o.shape[0]
        rx = acc_x.shape[0] // count
        for k in range(count):
            grads_o[k] = stacked(acc_x[k * rx : (k + 1) * rx, :]).astype(BF16)
        dim = acc_bc.shape[0]
        at = 0

        def put(value):
            nonlocal at
            small_o[at : at + value.shape[0], :] = value
            at += value.shape[0]

        put(acc_bc[:, :LANES])
        put(acc_bc[:, LANES:])
        count, each, rest = slots
        if at < count * each:
            put(jnp.zeros((count * each - at, LANES), F32))
        for k in range(0, dim, LANES):
            put(jnp.transpose(acc_dt[k : k + LANES, :])[0:n_heads])

        def line(value):
            return jnp.sum(value, axis=0, keepdims=True)

        def lane_home(value):
            return pltpu.roll(jnp.broadcast_to(value, (8, LANES)), place[1], 1)[0:1]

        own = iota((1, LANES), 1) < width // P_SIZE
        taps_sum = [line(acc_taps[8 * k : 8 * k + 8, :]) for k in range(KCONV + 1)]
        skips = mm_left(acc_skip[...], heads)
        head_rows = [
            lane_home(jnp.where(own, line(x), 0.0))
            for x in (acc_heads[0:8, :], acc_heads[8:16, :], skips)
        ]
        put(jnp.concatenate([t[:, width : width + N] for t in taps_sum] + head_rows, axis=0))
        spare = jnp.zeros((8 - KCONV - 1, LANES), F32)
        put(jnp.concatenate([t[:, width + N :] for t in taps_sum] + [spare], axis=0))
        small_o[at:, :] = jnp.zeros_like(small_o[at:, :])
        gains = line(acc_gain[...])
        tiles = width // LANES
        own_rows = jnp.concatenate(
            [
                jnp.concatenate(
                    [t[:, k * LANES : (k + 1) * LANES] for t in taps_sum]
                    + [gains[:, k * LANES : (k + 1) * LANES], spare[0:2]],
                    axis=0,
                )
                for k in range(tiles)
            ],
            axis=0,
        )
        small_o[pl.ds(pl.multiple_of(at + place[2] * (8 * tiles), 8), 8 * tiles), :] = own_rows
        for k in range(count // 2):
            for out, side in ((keep_o, place[0]), (send_o, 1 - place[0])):
                slot = side * (count // 2) + k
                to = k * (each + rest)
                out[to : to + each, :] = small_o[pl.ds(pl.multiple_of(slot * each, 8), each), :]
                start = pl.multiple_of(count * each + slot * rest, 8)
                out[to + each : to + each + rest, :] = small_o[pl.ds(start, rest), :]


def input_grad(hid, gz, gx, gbc, gpre, w_z, w_x, w_bc, w_dt):
    gh = (
        mm(gpre[...], w_dt[...], 1, 1)
        + mm(gz[...], w_z[...], 1, 1)
        + mm(gx[...], w_x[...], 1, 1)
        + mm(gbc[:, : 2 * N], w_bc[...], 1, 1)
        + mm(gbc[:, 2 * N :], w_bc[...], 1, 1)
    )
    u = hid[...].astype(F32)
    return gh, fold_rows(gh * (u * rms_inv(u)))


def k_input(begins, own, ends, place, *refs):
    refs, (out, norm_o, acc) = refs[:-3], refs[-3:]
    i = pl.program_id(0)

    @pl.when(i == 0)
    def _():
        acc[...] = jnp.zeros_like(acc) if begins else refs[-1][...]

    gh, norm = input_grad(*refs[:9])
    out[...] = (gh + refs[9][...]).astype(BF16) if own else gh
    acc[...] += norm

    @pl.when(i == pl.num_programs(0) - 1)
    def _():
        if ends:
            rows = acc.shape[1] // LANES
            norm_o[0:rows, :] = stacked(jnp.sum(acc[...], axis=0, keepdims=True))
            norm_o[rows:, :] = jnp.zeros((8 - rows, LANES), F32)
        else:
            norm_o[...] = acc[...]


def k_reduce(*refs):
    out = refs[-1]
    out[...] = tree([part[...].astype(F32) for part in refs[:-1]]).astype(BF16)


def k_halve(mask, place, kept, arrived, keep_o, send_o):
    rows = keep_o.shape[0]
    upper = (place[2] // mask) % 2
    for out, at in ((keep_o, upper * rows), (send_o, (1 - upper) * rows)):
        at = pl.multiple_of(at, 8)
        out[...] = kept[pl.ds(at, rows), :] + arrived[pl.ds(at, rows), :]


def k_pieces(slots, kept, arrived, norm, large, out):
    count = out.shape[0]
    _, each, rest = slots
    rows = each + rest
    cut = large.shape[1]
    spare = jnp.zeros((7, LANES), F32)
    for k in range(count):
        own = slice(k * rows, (k + 1) * rows)
        value = kept[own, :] + arrived[own, :]
        line = norm[k : k + 1, :] if k < 8 else spare[0:1]
        small = jnp.concatenate([value[each:], line, spare], axis=0)
        out[k, 0:cut, :] = large[k]
        out[k, cut : cut + each, :] = value[:each].astype(BF16)
        out[k, cut + each :, :] = jnp.concatenate(split2(small), axis=0)


def k_reduce_both(cut, parts, out):
    count = out.shape[0]
    rows = (out.shape[1] - cut) // 2
    terms = [parts[k].astype(F32) for k in range(count)]
    small = tree([term[cut : cut + rows] + term[cut + rows :] for term in terms])
    large = tree([term[:cut] for term in terms]).astype(BF16)
    joined = jnp.concatenate([large, *split2(small)], axis=0)
    for k in range(count):
        out[k] = joined


def k_tick(value, out):
    out[...] = value[0, 0:16, :]


def k_quarter(cut, parts, out):
    rows = parts.shape[1] - cut
    for k in range(parts.shape[0]):
        out[k * rows : (k + 1) * rows, :] = parts[k, cut:, :]


def unstack(value, rows):
    return jnp.concatenate(
        [value[k : k + rows, :] for k in range(0, value.shape[0], rows)], axis=1
    )


def k_unpack_out(place, mine, other, w_out_o):
    count = 2 * mine.shape[0]
    ro = w_out_o.shape[0] // count
    rows = ro * w_out_o.shape[1] // LANES
    side = place[3] % 2
    for k in range(count // 2):
        for part, at in ((mine, 2 * k + side), (other, 2 * k + 1 - side)):
            piece = part[k].astype(F32)
            w_out_o[pl.ds(pl.multiple_of(at * ro, 8), ro), :] = unstack(piece[piece.shape[0] - rows :], ro)


def k_unpack(place, mine, other, b, w_zx_o):
    count = b.shape[0]
    dim, _, real = w_zx_o.shape
    rz = dim // count
    cut = rz * -(-real // LANES)
    side = place[3] % 2
    for k in range(count // 2):
        for part, at in ((mine, 2 * k + side), (other, 2 * k + 1 - side)):
            piece = part[k].astype(F32)
            w_zx_o[pl.ds(at * rz, rz), 0, :] = unstack(piece[0:cut], rz)[:, :real]
    for k in range(count):
        own = unstack(b[k, 0:cut, :].astype(F32), rz)[:, :real]
        w_zx_o[k * rz : (k + 1) * rz, 1, :] = own


def k_small(slots, place, *refs):
    count = len(refs) - 10
    w_bc_o, w_dt_o, bc_taps_o, bias_o, alog_o, skip_o, norm_o, taps_o, gain_o, buf = refs[count:]
    total, each, rest = slots
    steps = total // count
    tall = each + 2 * (rest + 8)
    dim = w_bc_o.shape[0]
    norms = [[] for _ in range(dim // LANES)]
    for k in range(count):
        from_head, at = place[2] ^ k, 0
        for mask in powers(count):
            at = 2 * at + (from_head // mask) % 2
        for t in range(steps):
            slot = at * steps + t
            value = refs[k][t * tall : (t + 1) * tall, :].astype(F32)
            small = value[each : each + rest + 8] + value[each + rest + 8 :]
            buf[pl.ds(pl.multiple_of(slot * each, 8), each), :] = value[:each]
            buf[pl.ds(pl.multiple_of(total * each + slot * rest, 8), rest), :] = small[:rest]
            if t < len(norms):
                norms[t].append(small[rest : rest + 1])
    for k, rows in enumerate(norms):
        norm_o[:, k * LANES : (k + 1) * LANES] = tree(rows)
    w_bc_o[:, :LANES] = buf[0:dim, :]
    w_bc_o[:, LANES:] = buf[dim : 2 * dim, :]
    at = total * each
    heads = w_dt_o.shape[0]
    w_dt_o[...] = unstack(buf[at : at + heads * dim // LANES, :], heads)
    at += heads * dim // LANES
    bc_taps_o[...] = unstack(buf[at : at + 16, :], 8)[0 : KCONV + 1]
    for k, out in enumerate((bias_o, alog_o, skip_o)):
        out[...] = buf[at + KCONV + 1 + k : at + KCONV + 2 + k, 0 : out.shape[1]]
    real = taps_o.shape[1]
    tiles = -(-real // LANES)
    own = buf[pl.ds(pl.multiple_of(at + 16 + place[2] * (8 * tiles), 8), 8 * tiles), :]
    own = unstack(own, 8)[:, 0:real]
    taps_o[...] = own[0 : KCONV + 1]
    gain_o[...] = own[KCONV + 1 : KCONV + 2]


def k_out(hid, *refs):
    count = (len(refs) - 1) // 2
    out = refs[-1]
    total = tree([mm(refs[k][...], refs[count + k][...]) for k in range(count)])
    out[...] = (hid[...].astype(F32) + total).astype(BF16)


def k_in_back(steps, place, hid, og, gain, *refs):
    i = pl.program_id(0)
    cuts = pl.num_programs(0) // steps
    out = refs[-1]
    count = (len(refs) - 1) // cuts

    def finish(parts):
        gh = tree([part[...].astype(F32) for part in parts])
        u = hid[...].astype(F32)
        inv = rms_inv(u)
        scaled = gh * gain[...]
        dot = jnp.sum(scaled * u, axis=1, keepdims=True) / u.shape[1]
        out[...] = inv * scaled - u * (inv * inv * inv * dot) + og[...].astype(F32)

    for k in range(cuts):
        pl.when(i // steps == k)(functools.partial(finish, refs[k * count : (k + 1) * count]))


def row_block(shape, rows, at=None):
    at = at or (lambda i, *s: i)
    rest = tuple(shape[1:])
    return pl.BlockSpec((rows,) + rest, lambda i, *s: (at(i, *s),) + (0,) * len(rest))


def whole(shape):
    return pl.BlockSpec(tuple(shape), lambda i, *s: (0,) * len(shape))


SMEM = pl.BlockSpec(memory_space=pltpu.SMEM)
VMEM = pl.BlockSpec(memory_space=pltpu.VMEM)


class Kept:
    def __init__(self, rows, at=None):
        self.rows = rows
        self.at = at or (lambda i, *s: i)

    def view(self, ref, i, scalars):
        start = pl.multiple_of(self.at(i, *scalars) * self.rows, self.rows)
        return ref.at[pl.ds(start, self.rows)]


def call(kernel, steps, ins, outs, scratch, flops, name, place=None, weight=1, alias=()):
    moved = sum(a.size * a.dtype.itemsize for a, _ in ins)
    for shape, dtype, _ in outs:
        moved += functools.reduce(lambda x, y: x * y, shape) * jnp.dtype(dtype).itemsize
    scalars = [] if place is None else [place]
    specs = [spec for _, spec in ins] + [spec for _, _, spec in outs]
    first = len(scalars)

    def body(*refs):
        i = pl.program_id(0)
        seen = list(refs)
        for k, spec in enumerate(specs):
            if isinstance(spec, Kept):
                seen[first + k] = spec.view(refs[first + k], i, refs[:first])
        kernel(*seen)

    places = [
        pl.BlockSpec(memory_space=pltpu.VMEM) if isinstance(spec, Kept) else spec for spec in specs
    ]
    held = 4 * 1024 * 1024
    for (shape, dtype), spec in zip(
        [(a.shape, a.dtype) for a, _ in ins] + [(shape, dtype) for shape, dtype, _ in outs], places
    ):
        if spec.block_shape is not None:
            padded = list(spec.block_shape)
            padded[-1] = -(-padded[-1] // LANES) * LANES
            held += 2 * math.prod(padded) * jnp.dtype(dtype).itemsize
    for buffer in scratch:
        held += math.prod(buffer.shape) * jnp.dtype(buffer.dtype).itemsize
    return pl.pallas_call(
        body,
        grid_spec=pltpu.PrefetchScalarGridSpec(
            num_scalar_prefetch=len(scalars),
            grid=(steps,),
            in_specs=places[: len(ins)],
            out_specs=places[len(ins) :],
            scratch_shapes=scratch,
        ),
        out_shape=[jax.ShapeDtypeStruct(s, d) for s, d, _ in outs],
        compiler_params=pltpu.CompilerParams(
            dimension_semantics=("arbitrary",), vmem_limit_bytes=max(VMEM_LIMIT, held)
        ),
        cost_estimate=pl.CostEstimate(
            flops=flops * weight, bytes_accessed=moved * weight, transcendentals=0
        ),
        input_output_aliases={first + k: j for k, j in alias},
        name=name,
    )(*scalars, *[a for a, _ in ins])


def far(pair):
    return (pltpu.with_memory_space_constraint(pair[0], pltpu.HBM), pair[1])


def swap(value, axis, mask):
    return lax.ppermute(value, axis, [(i, i ^ mask) for i in range(lax.axis_size(axis))])


def after(value, *others):
    return lax.optimization_barrier((value,) + others)[0]


def powers(count):
    return [1 << k for k in range(count.bit_length() - 1)]


def k_merge(mask, backward, first, place, *refs):
    total, other = refs[:2]
    before = None if first else refs[2]
    outs = refs[2 if first else 3 :]
    upper = (place[3] // mask) % 2 == 1
    later = jnp.logical_not(upper) if backward else upper

    def merge(early, late, out):
        scale = late[N : N + 1, :]
        out[0:N, :] = scale * early[0:N, :] + late[0:N, :]
        out[N:, :] = scale * early[N:, :]

    @pl.when(later)
    def _():
        if first:
            outs[0][...] = other[...]
        else:
            merge(other, before, outs[0])
        if len(outs) > 1:
            merge(other, total, outs[1])

    @pl.when(jnp.logical_not(later))
    def _():
        if first:
            outs[0][0:N, :] = jnp.zeros((N, total.shape[1]), F32)
            outs[0][N:, :] = jnp.ones((8, total.shape[1]), F32)
        else:
            outs[0][...] = before[...]
        if len(outs) > 1:
            merge(total, other, outs[1])


def carried_in(total, backward, place, beside=()):
    before, firsts = [], []
    shape = total.shape
    masks = powers(lax.axis_size("tok"))
    for mask in masks:
        other = swap(total, "tok", mask)
        ins = [total, other if before else after(other, *beside), *before]
        last = mask == masks[-1]
        found = call(
            functools.partial(k_merge, mask, backward, not before),
            1,
            [(a, whole(shape)) for a in ins],
            [(shape, F32, whole(shape))] * (1 if last else 2),
            [],
            10**6,
            "merge",
            place,
        )
        before, total = [found[0]], found[-1]
        firsts.append(found[0])
    return before[0], firsts[0]


def exchange(pieces, axis):
    return lax.all_to_all(pieces, axis, 0, 0, tiled=True)


def distances(value, axis, step):
    return [value] + [swap(value, axis, step * k) for k in range(1, lax.axis_size(axis) // step)]


def head_gathered(value):
    found = [value]
    masks = powers(lax.axis_size("head"))
    for mask in masks[1:] + masks[:1]:
        found = found + [swap(a, "head", mask) for a in found]
    return found


def on_device(
    hidden_in, norm_gain, w_zx, w_bc, w_dt, dt_bias, a_log, conv_x, conv_bc, d_skip, gate_gain,
    w_out, out_grad, group_first, group_valid,
):
    tokens, dim = hidden_in.shape
    real = w_zx.shape[2]
    own_heads = real // P_SIZE
    heads = w_dt.shape[1]
    groups = tokens // GROUP
    chunks = groups * PARTS
    width = -(-real // LANES) * LANES
    extra = width - real
    conv_width = width + 2 * N
    tok_count = lax.axis_size("tok")
    head_count = lax.axis_size("head")
    head_start = lax.axis_index("head") * own_heads

    def wide(a, dim_at, by=extra):
        return jnp.pad(a, [(0, by if k == dim_at else 0) for k in range(a.ndim)]) if by else a

    route = [(i - 1, i) for i in range(1, tok_count)]
    rim = lax.ppermute(hidden_in[tokens - 16 :], "tok", route)
    flat_zx = wide(w_zx, 2).reshape(dim, 2 * width)
    w_o = wide(w_out, 0)
    w_dt_here = wide(lax.dynamic_slice_in_dim(w_dt, head_start, own_heads, 1), 1, LANES - own_heads)
    per_head = jnp.stack([dt_bias, a_log, d_skip])
    per_head = lax.dynamic_slice_in_dim(per_head, head_start, own_heads, 1)
    per_head = jnp.pad(per_head, ((0, 5), (0, LANES - own_heads)))
    cx = wide(conv_x, 1)
    gain_in = norm_gain[None, :]
    gain_gate = wide(gate_gain, 0)[None, :]
    at_head = lax.axis_index("head")
    place = jnp.stack([at_head & 1, head_start, at_head, lax.axis_index("tok")]).astype(jnp.int32)
    hidden_in, place, flat_zx, w_o, w_dt_here, per_head, cx, gain_in, gain_gate = lax.optimization_barrier(
        (hidden_in, place, flat_zx, w_o, w_dt_here, per_head, cx, gain_in, gain_gate)
    )
    part_z, part_x = [
        (flat_zx, pl.BlockSpec((dim, width), lambda i, *s, side=side: (0, side))) for side in range(2)
    ]
    w_outs = head_gathered(w_o)

    def rows(a, at=None):
        return (a, row_block(a.shape, GROUP, at))

    def full(a):
        return (a, whole(a.shape))

    def kept(a, at=None):
        return (a, Kept(GROUP, at))

    def per_chunk(a, at=None):
        return (a, Kept(PARTS, at))

    def out_rows(cols, dtype, at=None):
        return ((tokens, cols), dtype, row_block((tokens, cols), GROUP, at))

    def out_kept(cols, dtype, at=None):
        return ((tokens, cols), dtype, Kept(GROUP, at))

    def out_full(shape, dtype):
        return (shape, dtype, whole(shape))

    def out_chunk(shape, dtype, at=None):
        return ((chunks,) + shape, dtype, Kept(PARTS, at))

    carry = (N + 8, width)
    h, v, pre, vprev, cvlead, xs, bc, dt, cum, ent, pd, fin = call(
        k_front,
        groups,
        [
            (group_first, SMEM), (group_valid, SMEM), far(rows(hidden_in)), full(rim), full(gain_in),
            part_x, full(w_bc), full(w_dt_here), full(per_head), full(cx), full(conv_bc),
        ],
        [
            out_kept(dim, BF16), out_kept(conv_width, F32), out_kept(LANES, F32),
            ((groups, 8, conv_width), F32, Kept(1)), ((groups, 16, conv_width), F32, Kept(1)), out_kept(width, BF16), out_kept(2 * N, BF16),
            out_kept(LANES, F32), out_kept(LANES, F32), out_chunk((N, width), F32),
            out_chunk((1, width), F32), out_full(carry, F32),
        ],
        [
            pltpu.VMEM((GROUP + 8, conv_width), F32), pltpu.VMEM((N, width), F32),
            pltpu.VMEM((8, width), F32),
        ],
        4 * 10**9,
        "front",
    )
    prev, _ = carried_in(fin, False, place)
    silu, slope, gyn = call(
        k_proj,
        groups,
        [kept(h), rows(after(out_grad, fin)), part_z, full(w_o)],
        [out_kept(width, F32)] * 3,
        [],
        5 * 10**9,
        "proj",
    )
    yw, ecum = call(
        k_within,
        groups,
        [kept(xs), kept(bc), kept(dt), kept(cum)],
        [out_kept(width, F32)] * 2,
        [],
        5 * 10**9,
        "within",
    )
    mix, entry, sums = call(
        k_gate,
        groups,
        [
            per_chunk(ent), per_chunk(pd), full(after(prev, *w_outs)), kept(bc), kept(ecum), kept(yw), kept(xs),
            kept(silu), kept(gyn), full(gain_gate), full(per_head),
        ],
        [
            out_kept(width, F32), out_chunk((N, width), F32),
            ((2, tokens), F32, pl.BlockSpec((2, GROUP), lambda i: (0, i))),
        ],
        [],
        3 * 10**9,
        "gate",
    )
    sums = [sums] + [swap(sums, "head", mask) for mask in range(1, head_count)]

    def back(i):
        return groups - 1 - i

    yn, gm, gz, ds, qd, acc_gain, acc_skip, fin_back = call(
        functools.partial(k_gate_back, float(heads * P_SIZE), head_count),
        groups,
        [
            (group_first, SMEM), kept(mix, back), kept(silu, back), kept(slope, back), kept(gyn, back), full(gain_gate),
            kept(xs, back), kept(bc, back), kept(ecum, back),
        ]
        + [(a, pl.BlockSpec((2, GROUP), lambda i: (0, groups - 1 - i))) for a in sums],
        [
            out_kept(width, BF16, back), out_kept(width, BF16, back), out_kept(width, BF16, back),
            out_chunk((N, width), F32, back), out_chunk((1, width), F32, back),
            out_full((8, width), F32), out_full((8, width), F32), out_full(carry, F32),
        ],
        [pltpu.VMEM((N, width), F32), pltpu.VMEM((8, width), F32)],
        3 * 10**9,
        "gate_back",
    )
    yns = [yn]
    for mask in powers(head_count)[1:]:
        yns = yns + [swap(a, "head", mask) for a in yns]
    rows_z, rows_o = dim // tok_count, width // tok_count
    piece_a = (rows_z * width + rows_o * dim) // LANES
    sides = tok_count // 2
    keep_a, send_a = call(
        k_weights,
        groups,
        [kept(yn), rows(out_grad), kept(h), kept(gz)],
        [out_full((sides, piece_a, LANES), F32)] * 2,
        [pltpu.VMEM((dim, width), F32), pltpu.VMEM((width, dim), F32)],
        3 * 10**9,
        "weights",
        place,
        4,
    )
    end_grad, first_grad = carried_in(fin_back, True, place, (keep_a,))
    arrived_a = swap(after(send_a, first_grad), "tok", 1)
    per_token = [
        out_kept(width, F32), out_kept(2 * N, F32), out_kept(LANES, F32), out_kept(LANES, F32)
    ]
    inner = [kept(xs), kept(bc), kept(after(gm, keep_a)), kept(dt), kept(cum), kept(mix), per_chunk(entry), full(per_head)]
    dxw, dbc, rq, qw = call(
        k_within_back, groups, inner, per_token, [], 10 * 10**9, "within_back", None, 4
    )

    def leading(a):
        per = GROUP // 16
        return (a, Kept(16, lambda i: i * per))

    rims, lead = call(
        k_rim,
        groups,
        [
            (group_first, SMEM), leading(xs), leading(bc), leading(gm), leading(dt), leading(cum),
            (cum, Kept(8, lambda i: i * (GROUP // 8) + CHUNK // 8 - 1)),
            leading(dxw), leading(dbc), (cvlead, Kept(1)),
            (ds, Kept(1, lambda i: i * PARTS)),
            (qd, Kept(1, lambda i: i * PARTS)),
            full(end_grad), full(per_head),
        ],
        [((groups, 16, conv_width), F32, Kept(1)), out_full((8, conv_width), F32)],
        [],
        10**9,
        "rim",
    )
    rim_in = lax.ppermute(lead, "tok", [(i, i - 1) for i in range(1, tok_count)])
    at_head = lax.axis_index("head")
    place = jnp.stack([at_head & 1, head_start, at_head, lax.axis_index("tok")]).astype(jnp.int32)
    pairs_a = call(
        k_pair,
        1,
        [full(after(keep_a, lead)), full(arrived_a)],
        [out_full((piece_a, LANES), BF16)] * sides,
        [],
        10**6,
        "pair",
        place,
    )
    arrived_a = [pairs_a[0]] + [swap(pairs_a[k], "tok", 2 * k) for k in range(1, sides)]
    half = groups // 2
    piece_b = rows_z * width // LANES
    tiles = width // LANES
    count = head_count * tok_count
    each = -(-2 * dim // (16 * count)) * 16
    rest = -(-(heads * dim // LANES + 16 + head_count * 8 * tiles) // (8 * count)) * 8
    slots = (count, each, rest)
    small_rows = count * (each + rest)
    acc_shapes = [(dim, width), (dim, 2 * N), (dim, LANES), (8 * KCONV + 8, conv_width), (16, LANES)]

    def back_call(final, more_in, more_out, more_scratch, alias, ready):
        def at(i, *s):
            return i + half if final else i

        return call(
            functools.partial(k_back, final, slots, heads),
            half,
            [(group_valid, SMEM)]
            + [
                kept(a, at)
                for a in (after(h, *ready), xs, bc, gm, pre, dt, cum, v)
            ]
            + [(vprev, Kept(1, at))]
            + [
                kept(a, at)
                for a in (dxw, dbc, rq, qw)
            ]
            + [per_chunk(entry, at), per_chunk(ds, at), per_chunk(qd, at), full(end_grad)]
            + [(rims, Kept(1, lambda i, s: jnp.minimum(at(i) + 1, groups - 1)))]
            + [full(cx), full(conv_bc), full(per_head)]
            + more_in,
            [out_kept(width, BF16, at), out_kept(4 * N, BF16, at), out_kept(LANES, BF16, at)]
            + [(a, F32, VMEM) for a in acc_shapes]
            + more_out,
            [pltpu.VMEM((GROUP + 8, conv_width), F32)] * 2 + more_scratch,
            5 * 10**9,
            "back_end" if final else "back_start",
            place,
            4,
            alias,
        )

    partial = back_call(False, [], [], [], (), (pairs_a[0],))
    (total_a,) = call(
        k_reduce, 1, [full(after(a, partial[0])) for a in arrived_a], [out_full((piece_a, LANES), BF16)],
        [], 10**6, "reduce",
    )
    found = back_call(
        True,
        [full(rim_in), full(acc_gain), full(acc_skip)] + [(a, VMEM) for a in partial],
        [
            out_full((tok_count, piece_b, LANES), BF16), out_full((small_rows // 2, LANES), F32),
            out_full((small_rows // 2, LANES), F32),
        ],
        [pltpu.VMEM((small_rows, LANES), F32)],
        [(25 + k, k) for k in range(8)],
        (total_a, yns[1]),
    )
    gx, gbc, gpre = found[:3]
    grads_b, small_keep, small_send = found[8:]
    parts_a = distances(total_a, "tok", 2)
    (mine_a,) = call(
        k_join, 1, [full(after(a, gx)) for a in parts_a], [out_full((sides, piece_a, LANES), BF16)], [],
        10**6, "join", place,
    )

    cuts = 2
    steps = half // cuts
    shape = (tokens // 2 // cuts, dim)

    def input_call(own, k, norm, more, ready):
        def turned(i, s):
            return i + k * steps + half * (s[0] if own else 1 - s[0])

        ends = own and k == cuts - 1
        return call(
            functools.partial(k_input, norm is None, own, ends),
            steps,
            [rows(hidden_in, turned)]
            + [kept(a, turned) for a in (gz, gx, gbc, after(gpre, *ready))]
            + [part_z, part_x, full(w_bc), full(w_dt_here)]
            + [rows(a) for a in more]
            + ([] if norm is None else [full(norm)]),
            [
                (shape, BF16 if own else F32, row_block(shape, GROUP)),
                out_full((8, LANES if ends else dim), F32),
            ],
            [pltpu.VMEM((8, dim), F32)],
            10**9,
            "input_own" if own else "input_sent",
            place,
        )

    sent, norm = input_call(False, 0, None, [], (mine_a,))
    arrived = [swap(sent, "head", 1)]
    small_arrived = after(swap(after(small_send, mine_a), "head", 1), sent)
    for mask in powers(head_count)[1:]:
        small_shape = (small_keep.shape[0] // 2, LANES)
        small_keep, small_send = call(
            functools.partial(k_halve, mask), 1, [full(small_keep), full(small_arrived)],
            [out_full(small_shape, F32)] * 2, [], 10**6, "halve", place,
        )
        small_arrived = swap(small_send, "head", mask)
    for k in range(1, cuts):
        sent, norm = input_call(False, k, norm, [], (mine_a, small_keep))
        arrived.append(swap(sent, "head", 1))
    parts = []
    for k in range(cuts):
        part, norm = input_call(True, k, norm, [arrived[k]], (mine_a,))
        found = [part]
        for mask in powers(head_count)[1:]:
            found = found + [swap(a, "head", mask) for a in found]
        parts.append(found)

    shape = (tok_count, piece_b + each + 2 * (rest + 8), LANES)
    (pieces,) = call(
        functools.partial(k_pieces, slots), 1, [full(small_keep), full(small_arrived), full(norm), full(grads_b)],
        [out_full(shape, BF16)], [], 10**6, "pieces",
    )
    yns = yns + [swap(after(a, pieces), "head", 1) for a in yns]
    (block_out,) = call(
        k_out,
        groups,
        [rows(after(hidden_in, pieces))] + [rows(a) for a in yns] + [full(a) for a in w_outs],
        [out_rows(dim, BF16)],
        [],
        5 * 10**9,
        "out",
        None,
        16,
    )

    (copies,) = call(
        functools.partial(k_reduce_both, piece_b + each), 1,
        [full(after(exchange(pieces, "tok"), block_out))],
        [out_full(shape, BF16)], [], 10**6, "reduce_both",
    )
    sum_b = exchange(copies, "tok")
    other_a = swap(after(mine_a, copies), "tok", 1)
    (tick,) = call(
        k_tick, 1, [(copies, row_block(copies.shape, 1))], [out_full((16, LANES), BF16)], [], 1, "tick"
    )
    (grad_w_out,) = call(
        k_unpack_out, 1, [full(mine_a), full(other_a)], [out_full((width, dim), F32)],
        [], 10**6, "unpack_out", place,
    )
    others = [
        [swap(found[0], "head", 1)] + [swap(after(a, tick), "head", 1) for a in found[1:]]
        for found in parts
    ]

    def turned_back(i, s):
        return lax.rem(i + half * s[0], groups)

    def in_cut(a, k):
        return (a, row_block(a.shape, GROUP, lambda i, s: jnp.clip(i - k * steps, 0, steps - 1)))

    (grad_in,) = call(
        functools.partial(k_in_back, steps),
        groups,
        [far(rows(hidden_in, turned_back)), far(rows(out_grad, turned_back)), full(gain_in)]
        + [in_cut(a, k) for k, found in enumerate(parts + others) for a in found],
        [out_rows(dim, F32, turned_back)],
        [],
        10**9,
        "in_back",
        place,
    )
    shape = (tok_count * (each + 2 * (rest + 8)), LANES)
    (quarter,) = call(
        functools.partial(k_quarter, piece_b), 1, [full(after(sum_b, grad_in))], [out_full(shape, BF16)],
        [], 10**6, "quarter",
    )
    quarters = [(quarter, 0)]
    for mask in powers(head_count):
        quarters = quarters + [(swap(a, "head", mask), k | mask) for a, k in quarters]
    quarters = [a for a, _ in sorted(quarters, key=lambda item: item[1])]

    (grad_w_zx,) = call(
        k_unpack,
        1,
        [full(mine_a), full(other_a), full(sum_b)],
        [out_full((dim, 2, real), F32)],
        [],
        10**6,
        "unpack",
        place,
    )
    grad_w_bc, grad_w_dt, grad_taps, grad_bias, grad_alog, grad_skip, grad_norm, own_taps, own_gain = call(
        functools.partial(k_small, slots),
        1,
        [full(a) for a in quarters],
        [
            out_full((dim, 2 * N), F32), out_full((heads, dim), F32), out_full((KCONV + 1, 2 * N), F32),
            out_full((1, heads), F32), out_full((1, heads), F32), out_full((1, heads), F32),
            out_full((1, dim), F32), out_full((KCONV + 1, real), F32), out_full((1, real), F32),
        ],
        [pltpu.VMEM((small_rows, LANES), F32)],
        10**6,
        "small",
        place,
    )

    return (
        block_out,
        grad_in,
        grad_norm[0],
        grad_w_zx,
        grad_w_bc,
        grad_w_dt.T,
        grad_bias[0],
        grad_alog[0],
        own_taps,
        grad_taps,
        grad_skip[0],
        own_gain[0],
        grad_w_out[:real],
    )


def solution(mesh):
    return jax.shard_map(
        on_device,
        mesh=mesh,
        in_specs=(
            P("tok", None), P(), P(None, None, "head"), P(), P(), P(), P(), P(None, "head"), P(), P(),
            P("head"), P("head", None), P("tok", None), P("tok"), P("tok"),
        ),
        out_specs=(
            P("tok", None), P("tok", None), P(), P(None, None, "head"), P(), P(), P(), P(),
            P(None, "head"), P(), P(), P("head"), P("head", None),
        ),
        check_vma=False,
    )
```
